32 devices in a mesh: fsdp: 16 (over z, y, x), rep: 2 (over core).
Axes of the slice: x: 2, y: 2, z: 4, core: 2. Of those that a mesh axis runs over, the one named last changes fastest.
Arguments:
- hidden_in: bfloat16 [16384, 768], P(('fsdp', 'rep')), may hold values from -6 to 6
- caption_lengths: int32 [32, 16], P(('fsdp', 'rep')), may hold values from 1 to 40, 512 in all within a row
- norm_gain: bfloat16 [2, 2, 768], P(None, None, ('fsdp', 'rep')), may hold values from 0.5 to 1.5
- norm_bias: bfloat16 [2, 2, 768], P(None, None, ('fsdp', 'rep')), may hold values from -3 to 3
- qkv_weight: bfloat16 [2, 768, 2304], P(None, ('fsdp', 'rep')), may hold values from -0.21875 to 0.21875
- out_weight: bfloat16 [2, 768, 768], P(None, ('fsdp', 'rep')), may hold values from -1.25 to 1.25
- up_weight: bfloat16 [2, 768, 3072], P(None, ('fsdp', 'rep')), may hold values from -0.21875 to 0.21875
- up_bias: bfloat16 [2, 3072], P(None, ('fsdp', 'rep')), may hold values from -3 to 3
- down_weight: bfloat16 [2, 3072, 768], P(None, ('fsdp', 'rep')), may hold values from -0.109375 to 0.109375
- down_bias: bfloat16 [2, 768], P(None, ('fsdp', 'rep')), may hold values from -3 to 3
- grad_out: bfloat16 [16384, 768], P(('fsdp', 'rep')), may hold values from -6 to 6
Outputs:
- hidden_out: float32 [16384, 768], P(('fsdp', 'rep'))
- d_hidden_in: float32 [16384, 768], P(('fsdp', 'rep'))
- d_norm_gain: float32 [2, 2, 768], P(None, None, ('fsdp', 'rep'))
- d_norm_bias: float32 [2, 2, 768], P(None, None, ('fsdp', 'rep'))
- d_up_weight: float32 [2, 768, 3072], P(None, ('fsdp', 'rep'))
- d_up_bias: float32 [2, 3072], P(None, ('fsdp', 'rep'))
- d_down_weight: float32 [2, 3072, 768], P(None, ('fsdp', 'rep'))
- d_down_bias: float32 [2, 768], P(None, ('fsdp', 'rep'))
The draws below stay inside these ranges and needn't reach their ends.
Inputs may be any that keep to these rules, and one draw needn't show every extreme that they name: `caption_lengths`: each row's 16 caption lengths add up to 512.
All inputs are finite; a program needn't handle non-finite values.
Results may differ from the reference program's by a relative error of at most 0.015.
Values may be sent and summed in bfloat16 or wider, within the bound.
A program may use at most 256 MiB of HBM per device.

```python
import math
import jax
import jax.numpy as jnp
import numpy as np
from jax import lax

D = 768
FF = 3072
HEADS = 12
SEQ = 512
CAPS = 16
MOST = 40
LAYERS = 2
ROWS = 32
TOKENS = 16384


def block_levels(key, dims, split, least, high):
    level = 1.0
    for axis_at, blocks in split:
        heights = jax.random.uniform(jax.random.fold_in(jax.random.fold_in(key, 6), axis_at), (blocks,), jnp.float32, least / len(split), high / len(split))
        level = level * jnp.repeat(jnp.exp(heights), dims[axis_at] // blocks).reshape((-1,) + (1,) * (len(dims) - 1 - axis_at))
    return level


def length_profile(count, total, most, skew):
    weights = [(1 << 20) // math.isqrt(rank ** skew) + 1 for rank in range(2, count + 1)]
    rest, holding = total - most - (count - 1), [1] * (count - 1)
    while rest > 0:
        candidates = [i for i in range(count - 1) if holding[i] < most]
        whole, budget = sum([weights[i] for i in candidates]), rest
        for i in candidates:
            addition = min(most - holding[i], max(1, budget * weights[i] // whole), rest)
            holding[i] = holding[i] + addition
            rest = rest - addition
    return np.array([most] + holding)


def uneven(rng, count, total, limit, slope):
    if count == 2:
        one = jax.random.randint(rng, (), max(1, total - limit), min(limit, total - 1) + 1)
        return jnp.stack([one, total - one])
    sizes = jnp.asarray(length_profile(count, total, limit, slope), jnp.int32)
    twos = (count - 1) // 2
    source_of, receiver = sizes[1:1 + 2 * twos:2], sizes[2:2 + 2 * twos:2]
    slack = jnp.minimum(source_of - 1, limit - receiver)
    shifted = jax.random.randint(jax.random.fold_in(rng, 1), (twos,), 0, 1 << 20) % (slack + 1)
    sizes = sizes.at[1:1 + 2 * twos:2].set(source_of - shifted).at[2:2 + 2 * twos:2].set(receiver + shifted)
    return sizes[jax.random.permutation(jax.random.fold_in(rng, 2), count)]


def bell_draw(own_key, extent, scale, reach, shards=(), kind=jnp.bfloat16):
    level = block_levels(own_key, extent, shards, -0.22, 0.18) if shards else 1.0
    values = jax.random.normal(own_key, extent, jnp.float32) * scale * level
    return jnp.minimum(jnp.maximum(values, -reach), reach).astype(kind)


def setup_inputs(seed: int = 0) -> dict:
    key_of = jax.random.split(jax.random.key(seed), 12)
    return {
        "hidden_in": bell_draw(key_of[0], (TOKENS, D), 1.0, 6.0, ((0, 32),)),
        "caption_lengths": jax.vmap(lambda own: uneven(own, CAPS, SEQ, MOST, 1))(jax.random.split(key_of[1], ROWS)).reshape((ROWS, CAPS)).astype(jnp.int32),
        "norm_gain": jnp.clip(1.0 + 0.1 * jax.random.normal(key_of[2], (LAYERS, 2, D), jnp.float32), 0.5, 1.5).astype(jnp.bfloat16),
        "norm_bias": bell_draw(key_of[3], (LAYERS, 2, D), 0.5, 3.0, ((2, 32),)),
        "qkv_weight": bell_draw(key_of[4], (LAYERS, D, 3 * D), D ** -0.5, 0.21875, ((1, 32),)),
        "out_weight": bell_draw(key_of[5], (LAYERS, D, D), (D // 32) ** -0.5, 1.25, ((1, 32),)),
        "up_weight": bell_draw(key_of[6], (LAYERS, D, FF), D ** -0.5, 0.21875, ((1, 32),)),
        "up_bias": bell_draw(key_of[7], (LAYERS, FF), 0.5, 3.0, ((1, 32),)),
        "down_weight": bell_draw(key_of[8], (LAYERS, FF, D), FF ** -0.5, 0.109375, ((1, 32),)),
        "down_bias": bell_draw(key_of[9], (LAYERS, D), 0.5, 3.0, ((1, 32),)),
        "grad_out": bell_draw(key_of[10], (TOKENS, D), 1.0, 6.0, ((0, 32),)),
    }


@jax.custom_vjp
def low(v):
    return lax.optimization_barrier(v.astype(jnp.bfloat16)).astype(jnp.float32)

@jax.custom_vjp
def low_back(v):
    return v

def low_keep(v):
    return (low(v), None)

def low_pass(kept, grad):
    return (grad,)

def back_keep(v):
    return (v, None)

def back_low(kept, grad):
    return (low(grad),)
low.defvjp(low_keep, low_pass)
low_back.defvjp(back_keep, back_low)
EPSILON = 1e-05
SCALE = 0.125
HIGH = lax.Precision.HIGHEST

def layer_norm(values, gain, shift):
    centre = lax.optimization_barrier(jnp.mean(values, axis=-1, keepdims=True))
    centred = values - centre
    spread = lax.optimization_barrier(jnp.mean(centred * centred, axis=-1, keepdims=True))
    return centred * lax.rsqrt(spread + EPSILON) * gain + shift

def caption_ids(lengths):
    starts = (jnp.cumsum(lengths, axis=-1) - lengths).astype(jnp.int32)
    places = jnp.arange(SEQ, dtype=jnp.int32)
    passed = (places[None, :, None] >= starts[:, None, :]).astype(jnp.int32)
    return (lax.optimization_barrier(jnp.sum(passed, axis=-1)) - 1).astype(jnp.int32)

def attention(packed, captions):
    row_count = packed.shape[0]
    width = D // HEADS
    queries = packed[..., :D].reshape(row_count, SEQ, HEADS, width)
    keys_part = packed[..., D:2 * D].reshape(row_count, SEQ, HEADS, width)
    values_part = packed[..., 2 * D:].reshape(row_count, SEQ, HEADS, width)
    scores = jnp.einsum('rqhd,rkhd->rhqk', queries, keys_part, precision=HIGH) * SCALE
    scores = low_back(scores)
    same = captions[:, :, None] == captions[:, None, :]
    scores = jnp.where(same[:, None], scores, -1e+30)
    probs = low(jax.nn.softmax(scores, axis=-1))
    mixed = jnp.einsum('rhqk,rkhd->rqhd', probs, values_part, precision=HIGH)
    return mixed.reshape(row_count, SEQ, D)

def stack_forward(hidden, captions, frozen, trained):
    qkv_weight, out_weight = frozen
    gains, shifts, up_weight, up_bias, down_weight, down_bias = trained
    for layer_number in range(LAYERS):
        normed = low(layer_norm(hidden, gains[layer_number, 0], shifts[layer_number, 0]))
        packed = low(low_back(jnp.dot(normed, qkv_weight[layer_number], precision=HIGH)))
        mixed = low(low_back(attention(packed, captions)))
        hidden = hidden + low_back(jnp.dot(mixed, out_weight[layer_number], precision=HIGH))
        normed = low(layer_norm(hidden, gains[layer_number, 1], shifts[layer_number, 1]))
        preact = low_back(jnp.dot(normed, up_weight[layer_number], precision=HIGH) + up_bias[layer_number])
        active = low(jax.nn.gelu(preact, approximate=False))
        hidden = hidden + low_back(jnp.dot(active, down_weight[layer_number], precision=HIGH) + down_bias[layer_number])
    return hidden

def reference(hidden_in, caption_lengths, norm_gain, norm_bias, qkv_weight, out_weight, up_weight, up_bias, down_weight, down_bias, grad_out):
    frozen = (qkv_weight.astype(jnp.float32), out_weight.astype(jnp.float32))
    trained = (norm_gain.astype(jnp.float32), norm_bias.astype(jnp.float32), up_weight.astype(jnp.float32), up_bias.astype(jnp.float32), down_weight.astype(jnp.float32), down_bias.astype(jnp.float32))
    row_count = caption_lengths.shape[0]
    group = 8 if row_count % 8 == 0 else 1
    blocks = row_count // group
    inputs = hidden_in.astype(jnp.float32).reshape(blocks, group, SEQ, D)
    cotangent = grad_out.astype(jnp.float32).reshape(blocks, group, SEQ, D)
    captions = caption_ids(caption_lengths).reshape(blocks, group, SEQ)
    zeros = jax.tree.map(jnp.zeros_like, trained)

    def one_block(totals, item):
        block_in, block_caps, block_cot = item

        def forward(hidden, params):
            return stack_forward(hidden, block_caps, frozen, params)
        result, backward = jax.vjp(forward, block_in, trained)
        d_input, d_params = backward(block_cot)
        return (jax.tree.map(jnp.add, totals, d_params), (result, d_input))
    totals, (results, d_inputs) = lax.scan(one_block, zeros, (inputs, captions, cotangent))
    return (results.reshape(-1, D), d_inputs.reshape(-1, D), totals[0], totals[1], totals[2], totals[3], totals[4], totals[5])
```

```python
import jax
import jax.numpy as jnp
from jax import lax
from jax.sharding import PartitionSpec as P
from jax.experimental import pallas as pl
from jax.experimental.pallas import tpu as pltpu

MESH = pl.DeviceIdType.MESH

D = 768
FF = 3072
HEADS = 12
SEQ = 512
LAYERS = 2


EPSILON = 1e-05
SCALE = 0.125


def layer_norm(values, gain, shift):
    centre = jnp.mean(values, axis=-1, keepdims=True)
    centred = values - centre
    spread = jnp.mean(centred * centred, axis=-1, keepdims=True)
    return centred * lax.rsqrt(spread + EPSILON) * gain + shift


def exact_gelu(values):
    return jax.nn.gelu(values, approximate=False)


def caption_ids(lengths):
    starts = jnp.cumsum(lengths, axis=-1) - lengths
    places = jnp.arange(SEQ, dtype=jnp.int32)
    passed = (places[None, :, None] >= starts[:, None, :]).astype(jnp.int32)
    return jnp.sum(passed, axis=-1) - 1


def transposed_left(left, right):
    return lax.dot_general(
        left, right, (((0,), (0,)), ((), ())), preferred_element_type=jnp.float32
    )


def transposed_right(left, right):
    return lax.dot_general(
        left, right, (((1,), (1,)), ((), ())), preferred_element_type=jnp.float32
    )


def split_heads(packed):
    width = D // HEADS
    queries = packed[:, :D].reshape(SEQ, HEADS, width)
    keys_part = packed[:, D : 2 * D].reshape(SEQ, HEADS, width)
    values_part = packed[:, 2 * D :].reshape(SEQ, HEADS, width)
    return (queries, keys_part, values_part)


def masked_scores(queries, keys_part, caption):
    scores = (
        jnp.einsum("qhd,khd->hqk", queries, keys_part, preferred_element_type=jnp.float32) * SCALE
    )
    same = caption[:, None] == caption[None, :]
    return jnp.where(same[None], scores, -1e30)


def attend_row(inputs):
    packed, caption = inputs
    queries, keys_part, values_part = split_heads(packed)
    scores = masked_scores(queries, keys_part, caption)
    highest = jnp.max(scores, axis=-1, keepdims=True)
    weights = jnp.exp(scores - highest)
    totals = jnp.sum(weights, axis=-1, keepdims=True)
    probs = (weights / totals).astype(jnp.bfloat16)
    mixed = jnp.einsum("hqk,khd->qhd", probs, values_part, preferred_element_type=jnp.float32)
    return (mixed.reshape(SEQ, D), highest + jnp.log(totals))


def attend_back(inputs):
    packed, caption, logsum, d_mixed = inputs
    queries, keys_part, values_part = split_heads(packed)
    probs = jnp.exp(masked_scores(queries, keys_part, caption) - logsum)
    d_heads = d_mixed.reshape(SEQ, HEADS, D // HEADS)
    d_values = jnp.einsum(
        "hqk,qhd->khd", probs.astype(jnp.bfloat16), d_heads, preferred_element_type=jnp.float32
    )
    d_probs = jnp.einsum("qhd,khd->hqk", d_heads, values_part, preferred_element_type=jnp.float32)
    centre = jnp.sum(d_probs * probs, axis=-1, keepdims=True)
    d_scores = (probs * (d_probs - centre)).astype(jnp.bfloat16)
    d_queries = (
        jnp.einsum("hqk,khd->qhd", d_scores, keys_part, preferred_element_type=jnp.float32) * SCALE
    )
    d_keys = (
        jnp.einsum("hqk,qhd->khd", d_scores, queries, preferred_element_type=jnp.float32) * SCALE
    )
    joined = jnp.concatenate(
        [d_queries.reshape(SEQ, D), d_keys.reshape(SEQ, D), d_values.reshape(SEQ, D)], axis=1
    )
    return joined.astype(jnp.bfloat16)


ZS, YS, XS = 4, 2, 2


class Place:
    def __init__(self):
        f = lax.axis_index("fsdp")
        c = lax.axis_index("rep")
        self.f, self.c = f, c
        self.x = f % 2
        self.y = (f // 2) % 2
        self.z = f // 4
        fx = f + 1 - 2 * self.x
        fy = f + 2 - 4 * self.y
        self.fa = fx + c * (fy - fx)
        self.fb = fy + c * (fx - fy)
        self.ya = (self.fa // 2) % 2
        self.xa = self.fa % 2
        self.yb = (self.fb // 2) % 2
        self.xb = self.fb % 2
        self.A = (self.fa, c)
        self.B = (self.fb, c)
        self.C = (f, 1 - c)
        self.UP = (f + 4, c)
        self.DN = (f - 4, c)
        self.has_up = self.z < 3
        self.has_dn = self.z > 0
        z = self.z
        self.order = [z]
        tables = [(0, 1, 2, 3), (1, 0, 2, 3), (2, 1, 3, 0), (3, 2, 1, 0)]
        for i in range(1, 4):
            v = jnp.int32(tables[3][i])
            for zz in (2, 1, 0):
                v = jnp.where(z == zz, tables[zz][i], v)
            self.order.append(v)

    def barrier(self):
        bar = pltpu.get_barrier_semaphore()
        for d in (self.A, self.B, self.C):
            pl.semaphore_signal(bar, inc=1, device_id=d, device_id_type=MESH)

        @pl.when(self.has_up)
        def _():
            pl.semaphore_signal(bar, inc=1, device_id=self.UP, device_id_type=MESH)

        @pl.when(self.has_dn)
        def _():
            pl.semaphore_signal(bar, inc=1, device_id=self.DN, device_id_type=MESH)

        count = 3 + self.has_up.astype(jnp.int32) + self.has_dn.astype(jnp.int32)
        pl.semaphore_wait(bar, count)


class Gather:
    def __init__(self, place, ref, by_column, k, sems):
        self.p, self.ref, self.by_column, self.k = place, ref, by_column, k
        (self.zs, self.as_, self.bs, self.cs, self.zr, self.ar, self.br, self.cr) = sems

    def cut(self, zi, yi, xi, c=None):
        c = self.p.c if c is None else c
        if self.by_column:
            half = self.ref.shape[-1] // 2
            return self.ref.at[zi, yi, xi, :, pl.ds(pl.multiple_of(c * half, 128), half)]
        return self.ref.at[zi, yi, xi, c]

    def send(self, piece, to, ssem, rsem):
        return pltpu.make_async_remote_copy(
            src_ref=piece, dst_ref=piece, send_sem=ssem, recv_sem=rsem,
            device_id=to, device_id_type=MESH)

    def wait(self, piece, sem):
        pltpu.make_async_copy(piece, piece, sem).wait()

    def own(self):
        p, k = self.p, self.k
        mine = self.cut(p.z, p.y, p.x)

        @pl.when(p.has_up)
        def _():
            self.send(mine, p.UP, self.zs.at[k, 0], self.zr.at[k, p.z]).start()

        @pl.when(p.has_dn)
        def _():
            self.send(mine, p.DN, self.zs.at[k, 1], self.zr.at[k, p.z]).start()

        self.send(mine, p.A, self.as_.at[k], self.ar.at[k, p.z]).start()
        self.send(mine, p.B, self.bs.at[k], self.br.at[k, p.z]).start()

    def forward(self, i):
        p = self.p
        zi = p.order[i]
        up = (zi < p.z) & p.has_up
        dn = (zi > p.z) & p.has_dn
        return zi, up, dn

    def zvisit(self, i):
        p, k = self.p, self.k
        zi, up, dn = self.forward(i)
        piece = self.cut(zi, p.y, p.x)
        self.wait(piece, self.zr.at[k, zi])

        @pl.when(up)
        def _():
            self.send(piece, p.UP, self.zs.at[k, 1 + i], self.zr.at[k, zi]).start()

        @pl.when(dn)
        def _():
            self.send(piece, p.DN, self.zs.at[k, 1 + i], self.zr.at[k, zi]).start()

        self.send(piece, p.A, self.as_.at[k], self.ar.at[k, zi]).start()
        self.send(piece, p.B, self.bs.at[k], self.br.at[k, zi]).start()

    def avisit(self, i):
        p, k = self.p, self.k
        zi = p.order[i]
        piece = self.cut(zi, p.ya, p.xa)
        self.wait(piece, self.ar.at[k, zi])
        self.send(piece, p.B, self.bs.at[k], self.br.at[k, zi]).start()

    def plane(self, zi, c=None):
        c = self.p.c if c is None else c
        if self.by_column:
            half = self.ref.shape[-1] // 2
            return self.ref.at[zi, :, :, :, pl.ds(pl.multiple_of(c * half, 128), half)]
        return self.ref.at[zi, :, :, c]

    def row(self, zi):
        c = self.p.c
        if self.by_column:
            half = self.ref.shape[-1] // 2
            return self.ref.at[zi, 0, :, :, pl.ds(pl.multiple_of(c * half, 128), half)]
        return self.ref.at[zi, 0, :, c]

    def bvisit(self, i):
        p, k = self.p, self.k
        zi = p.order[i]
        self.wait(self.row(zi), self.br.at[k, zi])
        block = self.plane(zi)
        self.send(block, p.C, self.cs.at[k], self.cr.at[k, zi]).start()

    def cvisit(self, i):
        p, k = self.p, self.k
        zi = p.order[i]
        self.wait(self.plane(zi, 1 - p.c), self.cr.at[k, zi])

    def finish(self):
        p, k = self.p, self.k
        one = self.cut(0, 0, 0)

        @pl.when(p.has_up)
        def _():
            self.wait(one, self.zs.at[k, 0])

        @pl.when(p.has_dn)
        def _():
            self.wait(one, self.zs.at[k, 1])

        for i in range(1, 4):
            zi, up, dn = self.forward(i)

            @pl.when(up | dn)
            def _():
                self.wait(one, self.zs.at[k, 1 + i])

        c = p.c
        if self.by_column:
            half = self.ref.shape[-1] // 2
            cols = pl.ds(pl.multiple_of(c * half, 128), half)
            self.wait(self.ref.at[:, 0, 0, :, cols], self.as_.at[k])
            self.wait(self.ref.at[:, 0, :, :, cols], self.bs.at[k])
            self.wait(self.ref.at[:, :, :, :, cols], self.cs.at[k])
        else:
            self.wait(self.ref.at[:, 0, 0, c], self.as_.at[k])
            self.wait(self.ref.at[:, 0, :, c], self.bs.at[k])
            self.wait(self.ref.at[:, :, :, c], self.cs.at[k])


def gather_sems(n):
    dma = pltpu.SemaphoreType.DMA
    return [dma((n, 5)), dma((n,)), dma((n,)), dma((n,)), dma((n, 4)), dma((n, 4)), dma((n, 4)), dma((n, 4))]


def pack_rows(qkv, out, up):
    parts = []
    for h in range(2):
        for w in (qkv, out, up):
            half = w.shape[-1] // 2
            parts.append(w[:, :, h * half:(h + 1) * half])
    return jnp.pad(jnp.concatenate(parts, axis=-1), ((0, 0), (0, 8), (0, 0)))


WIDTHS = (2304, 768, 3072)


def gather_kernel(pin_ref, down_ref, *refs):
    outs = refs[:8]
    bufs = refs[8:16]
    land, psem, osem = refs[16:19]
    sems = refs[19:]
    p = Place()
    p.barrier()
    c = p.c
    width = sum(WIDTHS) // 2
    swaps = []
    for l in range(LAYERS):
        cp = pltpu.make_async_remote_copy(
            src_ref=pin_ref.at[l, :, pl.ds(pl.multiple_of((1 - c) * width, 128), width)],
            dst_ref=land.at[l], send_sem=psem.at[0, l], recv_sem=psem.at[1, l],
            device_id=p.C, device_id_type=MESH)
        cp.start()
        swaps.append(cp)
    chunks = []
    for l in range(LAYERS):
        for j in range(4):
            k = l * 4 + j
            chunks.append(Gather(p, bufs[k], j < 3, k, sems))
    for l in range(LAYERS):
        bufs[l * 4 + 3][p.z, p.y, p.x, c] = down_ref[l]
    for l in range(LAYERS):
        swaps[l].wait()
        off = 0
        for j, n in enumerate(WIDTHS):
            half = n // 2
            for cc in range(2):
                @pl.when(c == cc)
                def _():
                    mine = pin_ref[l, 0:24, cc * width + off:cc * width + off + half]
                    other = land[l, 0:24, off:off + half]
                    pair = [mine, other] if cc == 0 else [other, mine]
                    bufs[l * 4 + j][p.z, p.y, p.x, :, cc * half:(cc + 1) * half] = jnp.concatenate(pair, axis=0)
            off += half
    n = len(chunks)
    look = 2
    for t in range(look):
        chunks[t].own()
    for t in range(n + 3):
        if t + look < n:
            chunks[t + look].own()
        if t < n:
            for i in range(1, 4):
                chunks[t].zvisit(i)
        if 0 <= t - 1 < n:
            for i in range(4):
                chunks[t - 1].avisit(i)
        if 0 <= t - 2 < n:
            for i in range(4):
                chunks[t - 2].bvisit(i)
        if 0 <= t - 3 < n:
            for i in range(4):
                chunks[t - 3].cvisit(i)
            pltpu.make_async_copy(bufs[t - 3], outs[t - 3], osem.at[t - 3]).start()
    for k in range(n):
        chunks[k].finish()
        pltpu.make_async_copy(bufs[k], outs[k], osem.at[k]).wait()


def gather_all(qkv, out, up, down):
    pin = pack_rows(qkv, out, up)
    shapes = []
    for l in range(LAYERS):
        for n in WIDTHS:
            shapes.append((ZS, YS, XS, 48, n))
        shapes.append((ZS, YS, XS, 2, 96, D))
    vm = pl.BlockSpec(memory_space=pltpu.VMEM)
    got = pl.pallas_call(
        gather_kernel,
        out_shape=[jax.ShapeDtypeStruct(s, jnp.bfloat16) for s in shapes],
        in_specs=[vm, vm],
        out_specs=[pl.BlockSpec(memory_space=pl.ANY)] * 8,
        scratch_shapes=[pltpu.VMEM(s, jnp.bfloat16) for s in shapes]
        + [pltpu.VMEM((LAYERS, 32, sum(WIDTHS) // 2), jnp.bfloat16), pltpu.SemaphoreType.DMA((2, 2)), pltpu.SemaphoreType.DMA((8,))]
        + gather_sems(8),
        compiler_params=pltpu.CompilerParams(collective_id=0, has_side_effects=True, vmem_limit_bytes=60 * 2**20),
    )(pin, down)
    res = []
    for l in range(LAYERS):
        res.append([got[l * 4 + j].reshape(D, WIDTHS[j]) for j in range(3)] + [got[l * 4 + 3].reshape(FF, D)])
    return res


def fetch_forward(whole, w_qkv, w_out, w_up, w_down, gains, shifts, b_up, b_down):
    if whole is None:
        whole = [
            lax.all_gather(w, ("fsdp", "rep"), axis=0, tiled=True)
            for w in (w_qkv, w_out, w_up, w_down)
        ]
    return (
        *whole,
        lax.all_gather(gains, ("fsdp", "rep"), axis=1, tiled=True),
        lax.all_gather(shifts, ("fsdp", "rep"), axis=1, tiled=True),
        lax.all_gather(b_up, ("fsdp", "rep"), axis=0, tiled=True),
        lax.all_gather(b_down, ("fsdp", "rep"), axis=0, tiled=True),
    )


def fetch_backward(whole, w_qkv, w_out, w_up, w_down, gains, shifts):
    if whole is None:
        whole = [
            lax.all_gather(w, ("fsdp", "rep"), axis=0, tiled=True)
            for w in (w_qkv, w_out, w_up, w_down)
        ]
    return (
        *whole,
        lax.all_gather(gains, ("fsdp", "rep"), axis=1, tiled=True),
        lax.all_gather(shifts, ("fsdp", "rep"), axis=1, tiled=True),
    )


def owner_major(matrix, owners):
    width = matrix.shape[1] // owners
    return matrix.reshape(matrix.shape[0], owners, width).transpose(1, 0, 2).reshape(owners, -1)


def settle(d_up, d_down, d_gains, d_shifts, d_bup, d_bdown):
    owners = lax.axis_size("fsdp") * lax.axis_size("rep")
    members = [
        d_up.reshape(owners, -1),
        d_down.reshape(owners, -1),
        owner_major(d_gains, owners),
        owner_major(d_shifts, owners),
        d_bup.reshape(owners, -1),
        d_bdown.reshape(owners, -1),
    ]
    flat = jnp.concatenate(members, axis=1)
    mine = lax.psum_scatter(flat, ("fsdp", "rep"), scatter_dimension=0, tiled=True)
    mine = mine.reshape(-1)
    up_rows = D // owners
    down_rows = FF // owners
    norm_cols = D // owners
    sizes = [up_rows * FF, down_rows * D, 2 * norm_cols, 2 * norm_cols, down_rows, norm_cols]
    pieces = []
    begin = 0
    for length in sizes:
        pieces.append(mine[begin : begin + length])
        begin = begin + length
    return (
        pieces[0].reshape(up_rows, FF),
        pieces[1].reshape(down_rows, D),
        pieces[2].reshape(2, norm_cols),
        pieces[3].reshape(2, norm_cols),
        pieces[4],
        pieces[5],
    )


def per_device(
    hidden_in,
    caption_lengths,
    norm_gain,
    norm_bias,
    qkv_weight,
    out_weight,
    up_weight,
    up_bias,
    down_weight,
    down_bias,
    grad_out,
):
    row_count = caption_lengths.shape[0]
    near = lax.axis_size("fsdp") == 16 and lax.axis_size("rep") == 2
    weights = gather_all(qkv_weight, out_weight, up_weight, down_weight) if near else None
    captions = caption_ids(caption_lengths)
    hidden = hidden_in.astype(jnp.float32)
    stored = []
    for layer_number in range(LAYERS):
        fetched = fetch_forward(
            weights[layer_number] if near else None,
            qkv_weight[layer_number],
            out_weight[layer_number],
            up_weight[layer_number],
            down_weight[layer_number],
            norm_gain[layer_number],
            norm_bias[layer_number],
            up_bias[layer_number],
            down_bias[layer_number],
        )
        w_qkv, w_out, w_up, w_down, gains, shifts, b_up, b_down = fetched
        gains_full = gains.astype(jnp.float32)
        shifts_full = shifts.astype(jnp.float32)
        normed_a = layer_norm(hidden, gains_full[0], shifts_full[0]).astype(jnp.bfloat16)
        packed = jnp.dot(normed_a, w_qkv, preferred_element_type=jnp.float32).astype(jnp.bfloat16)
        mixed, logsum = lax.map(attend_row, (packed.reshape(row_count, SEQ, 3 * D), captions))
        mixed = mixed.reshape(-1, D).astype(jnp.bfloat16)
        middle = hidden + jnp.dot(mixed, w_out, preferred_element_type=jnp.float32)
        normed_f = layer_norm(middle, gains_full[1], shifts_full[1]).astype(jnp.bfloat16)
        preact = jnp.dot(normed_f, w_up, preferred_element_type=jnp.float32) + b_up.astype(
            jnp.float32
        )
        active = exact_gelu(preact).astype(jnp.bfloat16)
        output = (
            middle
            + jnp.dot(active, w_down, preferred_element_type=jnp.float32)
            + b_down.astype(jnp.float32)
        )
        weights_kept = None
        stored.append((hidden, packed, logsum, middle, normed_f, preact, active, weights_kept))
        hidden = output
    gradient = grad_out.astype(jnp.float32)
    settled = [None] * LAYERS
    for layer_number in reversed(range(LAYERS)):
        layer_in, packed, logsum, middle, normed_f, preact, active, weights_kept = stored[
            layer_number
        ]
        fetched = fetch_backward(
            weights[layer_number] if near else None,
            qkv_weight[layer_number],
            out_weight[layer_number],
            up_weight[layer_number],
            down_weight[layer_number],
            norm_gain[layer_number],
            norm_bias[layer_number],
        )
        w_qkv, w_out, w_up, w_down, gains, shifts = fetched
        gains_full = gains.astype(jnp.float32)
        shifts_full = shifts.astype(jnp.float32)
        grad_low = gradient.astype(jnp.bfloat16)
        d_bdown = jnp.sum(grad_low.astype(jnp.float32), axis=0)
        d_down = transposed_left(active, grad_low)
        d_active = transposed_right(grad_low, w_down)
        gelu_value, gelu_back = jax.vjp(exact_gelu, preact)
        d_preact = gelu_back(d_active)[0].astype(jnp.bfloat16)
        d_bup = jnp.sum(d_preact.astype(jnp.float32), axis=0)
        d_up = transposed_left(normed_f, d_preact)
        d_normed_f = transposed_right(d_preact, w_up)
        norm_value, norm_back = jax.vjp(layer_norm, middle, gains_full[1], shifts_full[1])
        d_middle_ln, d_gain_f, d_shift_f = norm_back(d_normed_f)
        d_middle = gradient + d_middle_ln
        d_mixed = transposed_right(d_middle.astype(jnp.bfloat16), w_out).astype(jnp.bfloat16)
        d_packed = lax.map(
            attend_back,
            (
                packed.reshape(row_count, SEQ, 3 * D),
                captions,
                logsum,
                d_mixed.reshape(row_count, SEQ, D),
            ),
        )
        d_normed_a = transposed_right(d_packed.reshape(-1, 3 * D), w_qkv)
        first_value, first_back = jax.vjp(layer_norm, layer_in, gains_full[0], shifts_full[0])
        d_input_ln, d_gain_a, d_shift_a = first_back(d_normed_a)
        gradient = d_middle + d_input_ln
        settled[layer_number] = settle(
            d_up,
            d_down,
            jnp.stack([d_gain_a, d_gain_f]),
            jnp.stack([d_shift_a, d_shift_f]),
            d_bup,
            d_bdown,
        )
    d_gains = jnp.stack([settled[number][2] for number in range(LAYERS)])
    d_shifts = jnp.stack([settled[number][3] for number in range(LAYERS)])
    d_up_all = jnp.stack([settled[number][0] for number in range(LAYERS)])
    d_bup_all = jnp.stack([settled[number][4] for number in range(LAYERS)])
    d_down_all = jnp.stack([settled[number][1] for number in range(LAYERS)])
    d_bdown_all = jnp.stack([settled[number][5] for number in range(LAYERS)])
    return (hidden, gradient, d_gains, d_shifts, d_up_all, d_bup_all, d_down_all, d_bdown_all)


def solution(mesh):
    in_specs = (
        P(("fsdp", "rep"), None),
        P(("fsdp", "rep"), None),
        P(None, None, ("fsdp", "rep")),
        P(None, None, ("fsdp", "rep")),
        P(None, ("fsdp", "rep"), None),
        P(None, ("fsdp", "rep"), None),
        P(None, ("fsdp", "rep"), None),
        P(None, ("fsdp", "rep")),
        P(None, ("fsdp", "rep"), None),
        P(None, ("fsdp", "rep")),
        P(("fsdp", "rep"), None),
    )
    out_specs = (
        P(("fsdp", "rep"), None),
        P(("fsdp", "rep"), None),
        P(None, None, ("fsdp", "rep")),
        P(None, None, ("fsdp", "rep")),
        P(None, ("fsdp", "rep"), None),
        P(None, ("fsdp", "rep")),
        P(None, ("fsdp", "rep"), None),
        P(None, ("fsdp", "rep")),
    )
    return jax.shard_map(
        per_device, mesh=mesh, in_specs=in_specs, out_specs=out_specs, check_vma=False
    )
```

```python
import jax
import jax.numpy as jnp
from jax import lax
from jax.sharding import PartitionSpec as P
from jax.experimental import pallas as pl
from jax.experimental.pallas import tpu as pltpu

MESH = pl.DeviceIdType.MESH

D = 768
FF = 3072
HEADS = 12
SEQ = 512
LAYERS = 2


EPSILON = 1e-05
SCALE = 0.125


def layer_norm(values, gain, shift):
    centre = jnp.mean(values, axis=-1, keepdims=True)
    centred = values - centre
    spread = jnp.mean(centred * centred, axis=-1, keepdims=True)
    return centred * lax.rsqrt(spread + EPSILON) * gain + shift


def exact_gelu(values):
    return jax.nn.gelu(values, approximate=False)


def caption_ids(lengths):
    starts = jnp.cumsum(lengths, axis=-1) - lengths
    places = jnp.arange(SEQ, dtype=jnp.int32)
    passed = (places[None, :, None] >= starts[:, None, :]).astype(jnp.int32)
    return jnp.sum(passed, axis=-1) - 1


def transposed_left(left, right):
    return lax.dot_general(
        left, right, (((0,), (0,)), ((), ())), preferred_element_type=jnp.float32
    )


def transposed_right(left, right):
    return lax.dot_general(
        left, right, (((1,), (1,)), ((), ())), preferred_element_type=jnp.float32
    )


def split_heads(packed):
    width = D // HEADS
    queries = packed[:, :D].reshape(SEQ, HEADS, width)
    keys_part = packed[:, D : 2 * D].reshape(SEQ, HEADS, width)
    values_part = packed[:, 2 * D :].reshape(SEQ, HEADS, width)
    return (queries, keys_part, values_part)


def masked_scores(queries, keys_part, caption):
    scores = (
        jnp.einsum("qhd,khd->hqk", queries, keys_part, preferred_element_type=jnp.float32) * SCALE
    )
    same = caption[:, None] == caption[None, :]
    return jnp.where(same[None], scores, -1e30)


def attend_row(inputs):
    packed, caption = inputs
    queries, keys_part, values_part = split_heads(packed)
    scores = masked_scores(queries, keys_part, caption)
    highest = jnp.max(scores, axis=-1, keepdims=True)
    weights = jnp.exp(scores - highest)
    totals = jnp.sum(weights, axis=-1, keepdims=True)
    probs = (weights / totals).astype(jnp.bfloat16)
    mixed = jnp.einsum("hqk,khd->qhd", probs, values_part, preferred_element_type=jnp.float32)
    return (mixed.reshape(SEQ, D), highest + jnp.log(totals))


def attend_back(inputs):
    packed, caption, logsum, d_mixed = inputs
    queries, keys_part, values_part = split_heads(packed)
    probs = jnp.exp(masked_scores(queries, keys_part, caption) - logsum)
    d_heads = d_mixed.reshape(SEQ, HEADS, D // HEADS)
    d_values = jnp.einsum(
        "hqk,qhd->khd", probs.astype(jnp.bfloat16), d_heads, preferred_element_type=jnp.float32
    )
    d_probs = jnp.einsum("qhd,khd->hqk", d_heads, values_part, preferred_element_type=jnp.float32)
    centre = jnp.sum(d_probs * probs, axis=-1, keepdims=True)
    d_scores = (probs * (d_probs - centre)).astype(jnp.bfloat16)
    d_queries = (
        jnp.einsum("hqk,khd->qhd", d_scores, keys_part, preferred_element_type=jnp.float32) * SCALE
    )
    d_keys = (
        jnp.einsum("hqk,qhd->khd", d_scores, queries, preferred_element_type=jnp.float32) * SCALE
    )
    joined = jnp.concatenate(
        [d_queries.reshape(SEQ, D), d_keys.reshape(SEQ, D), d_values.reshape(SEQ, D)], axis=1
    )
    return joined.astype(jnp.bfloat16)


ZS, YS, XS = 4, 2, 2


class Place:
    def __init__(self):
        f = lax.axis_index("fsdp")
        c = lax.axis_index("rep")
        self.f, self.c = f, c
        self.x = f % 2
        self.y = (f // 2) % 2
        self.z = f // 4
        fx = f + 1 - 2 * self.x
        fy = f + 2 - 4 * self.y
        self.fa = fx + c * (fy - fx)
        self.fb = fy + c * (fx - fy)
        self.ya = (self.fa // 2) % 2
        self.xa = self.fa % 2
        self.yb = (self.fb // 2) % 2
        self.xb = self.fb % 2
        self.A = (self.fa, c)
        self.B = (self.fb, c)
        self.C = (f, 1 - c)
        self.UP = (f + 4, c)
        self.DN = (f - 4, c)
        self.has_up = self.z < 3
        self.has_dn = self.z > 0
        z = self.z
        self.order = [z]
        tables = [(0, 1, 2, 3), (1, 0, 2, 3), (2, 1, 3, 0), (3, 2, 1, 0)]
        for i in range(1, 4):
            v = jnp.int32(tables[3][i])
            for zz in (2, 1, 0):
                v = jnp.where(z == zz, tables[zz][i], v)
            self.order.append(v)

    def barrier(self):
        bar = pltpu.get_barrier_semaphore()
        for d in (self.A, self.B, self.C):
            pl.semaphore_signal(bar, inc=1, device_id=d, device_id_type=MESH)

        @pl.when(self.has_up)
        def _():
            pl.semaphore_signal(bar, inc=1, device_id=self.UP, device_id_type=MESH)

        @pl.when(self.has_dn)
        def _():
            pl.semaphore_signal(bar, inc=1, device_id=self.DN, device_id_type=MESH)

        count = 3 + self.has_up.astype(jnp.int32) + self.has_dn.astype(jnp.int32)
        pl.semaphore_wait(bar, count)


class Gather:
    def __init__(self, place, ref, by_column, k, sems):
        self.p, self.ref, self.by_column, self.k = place, ref, by_column, k
        (self.zs, self.as_, self.bs, self.cs, self.zr, self.ar, self.br, self.cr) = sems

    def cut(self, zi, yi, xi, c=None):
        c = self.p.c if c is None else c
        if self.by_column:
            half = self.ref.shape[-1] // 2
            return self.ref.at[zi, yi, xi, :, pl.ds(pl.multiple_of(c * half, 128), half)]
        return self.ref.at[zi, yi, xi, c]

    def send(self, piece, to, ssem, rsem):
        return pltpu.make_async_remote_copy(
            src_ref=piece, dst_ref=piece, send_sem=ssem, recv_sem=rsem,
            device_id=to, device_id_type=MESH)

    def wait(self, piece, sem):
        pltpu.make_async_copy(piece, piece, sem).wait()

    def own(self):
        p, k = self.p, self.k
        mine = self.cut(p.z, p.y, p.x)

        @pl.when(p.has_up)
        def _():
            self.send(mine, p.UP, self.zs.at[k, 0], self.zr.at[k, p.z]).start()

        @pl.when(p.has_dn)
        def _():
            self.send(mine, p.DN, self.zs.at[k, 1], self.zr.at[k, p.z]).start()

        self.send(mine, p.A, self.as_.at[k], self.ar.at[k, p.z]).start()
        self.send(mine, p.B, self.bs.at[k], self.br.at[k, p.z]).start()

    def forward(self, i):
        p = self.p
        zi = p.order[i]
        up = (zi < p.z) & p.has_up
        dn = (zi > p.z) & p.has_dn
        return zi, up, dn

    def zvisit(self, i):
        p, k = self.p, self.k
        zi, up, dn = self.forward(i)
        piece = self.cut(zi, p.y, p.x)
        self.wait(piece, self.zr.at[k, zi])

        @pl.when(up)
        def _():
            self.send(piece, p.UP, self.zs.at[k, 1 + i], self.zr.at[k, zi]).start()

        @pl.when(dn)
        def _():
            self.send(piece, p.DN, self.zs.at[k, 1 + i], self.zr.at[k, zi]).start()

        self.send(piece, p.A, self.as_.at[k], self.ar.at[k, zi]).start()
        self.send(piece, p.B, self.bs.at[k], self.br.at[k, zi]).start()

    def avisit(self, i):
        p, k = self.p, self.k
        zi = p.order[i]
        piece = self.cut(zi, p.ya, p.xa)
        self.wait(piece, self.ar.at[k, zi])
        self.send(piece, p.B, self.bs.at[k], self.br.at[k, zi]).start()

    def plane(self, zi, c=None):
        c = self.p.c if c is None else c
        if self.by_column:
            half = self.ref.shape[-1] // 2
            return self.ref.at[zi, :, :, :, pl.ds(pl.multiple_of(c * half, 128), half)]
        return self.ref.at[zi, :, :, c]

    def row(self, zi):
        c = self.p.c
        if self.by_column:
            half = self.ref.shape[-1] // 2
            return self.ref.at[zi, 0, :, :, pl.ds(pl.multiple_of(c * half, 128), half)]
        return self.ref.at[zi, 0, :, c]

    def bvisit(self, i):
        p, k = self.p, self.k
        zi = p.order[i]
        self.wait(self.row(zi), self.br.at[k, zi])
        block = self.plane(zi)
        self.send(block, p.C, self.cs.at[k], self.cr.at[k, zi]).start()

    def cvisit(self, i):
        p, k = self.p, self.k
        zi = p.order[i]
        self.wait(self.plane(zi, 1 - p.c), self.cr.at[k, zi])

    def finish(self):
        p, k = self.p, self.k
        one = self.cut(0, 0, 0)

        @pl.when(p.has_up)
        def _():
            self.wait(one, self.zs.at[k, 0])

        @pl.when(p.has_dn)
        def _():
            self.wait(one, self.zs.at[k, 1])

        for i in range(1, 4):
            zi, up, dn = self.forward(i)

            @pl.when(up | dn)
            def _():
                self.wait(one, self.zs.at[k, 1 + i])

        c = p.c
        if self.by_column:
            half = self.ref.shape[-1] // 2
            cols = pl.ds(pl.multiple_of(c * half, 128), half)
            self.wait(self.ref.at[:, 0, 0, :, cols], self.as_.at[k])
            self.wait(self.ref.at[:, 0, :, :, cols], self.bs.at[k])
            self.wait(self.ref.at[:, :, :, :, cols], self.cs.at[k])
        else:
            self.wait(self.ref.at[:, 0, 0, c], self.as_.at[k])
            self.wait(self.ref.at[:, 0, :, c], self.bs.at[k])
            self.wait(self.ref.at[:, :, :, c], self.cs.at[k])


def gather_sems(n):
    dma = pltpu.SemaphoreType.DMA
    return [dma((n, 5)), dma((n,)), dma((n,)), dma((n,)), dma((n, 4)), dma((n, 4)), dma((n, 4)), dma((n, 4))]


def pack_rows(qkv, out, up):
    parts = []
    for h in range(2):
        for w in (qkv, out, up):
            half = w.shape[-1] // 2
            parts.append(w[:, :, h * half:(h + 1) * half])
    return jnp.pad(jnp.concatenate(parts, axis=-1), ((0, 0), (0, 8), (0, 0)))


WIDTHS = (2304, 768, 3072)


def gather_kernel(pin_ref, down_ref, small_ref, *refs):
    outs = refs[:9]
    bufs = refs[9:18]
    land, psem, osem = refs[18:21]
    sems = refs[21:]
    p = Place()
    p.barrier()
    c = p.c
    width = sum(WIDTHS) // 2
    swaps = []
    for l in range(LAYERS):
        cp = pltpu.make_async_remote_copy(
            src_ref=pin_ref.at[l, :, pl.ds(pl.multiple_of((1 - c) * width, 128), width)],
            dst_ref=land.at[l], send_sem=psem.at[0, l], recv_sem=psem.at[1, l],
            device_id=p.C, device_id_type=MESH)
        cp.start()
        swaps.append(cp)
    chunks = []
    for l in range(LAYERS):
        for j in range(4):
            k = l * 4 + j
            chunks.append(Gather(p, bufs[k], j < 3, k, sems))
    chunks.append(Gather(p, bufs[8], False, 8, sems))
    bufs[8][p.z, p.y, p.x, c] = small_ref[...]
    for l in range(LAYERS):
        bufs[l * 4 + 3][p.z, p.y, p.x, c] = down_ref[l]
    for l in range(LAYERS):
        swaps[l].wait()
        off = 0
        for j, n in enumerate(WIDTHS):
            half = n // 2
            for cc in range(2):
                @pl.when(c == cc)
                def _():
                    mine = pin_ref[l, 0:24, cc * width + off:cc * width + off + half]
                    other = land[l, 0:24, off:off + half]
                    pair = [mine, other] if cc == 0 else [other, mine]
                    bufs[l * 4 + j][p.z, p.y, p.x, :, cc * half:(cc + 1) * half] = jnp.concatenate(pair, axis=0)
            off += half
    n = len(chunks)
    look = 2
    for t in range(look):
        chunks[t].own()
    for t in range(n + 3):
        if t + look < n:
            chunks[t + look].own()
        if t < n:
            for i in range(1, 4):
                chunks[t].zvisit(i)
        if 0 <= t - 1 < n:
            for i in range(4):
                chunks[t - 1].avisit(i)
        if 0 <= t - 2 < n:
            for i in range(4):
                chunks[t - 2].bvisit(i)
        if 0 <= t - 3 < n:
            for i in range(4):
                chunks[t - 3].cvisit(i)
            pltpu.make_async_copy(bufs[t - 3], outs[t - 3], osem.at[t - 3]).start()
    for k in range(n):
        chunks[k].finish()
        pltpu.make_async_copy(bufs[k], outs[k], osem.at[k]).wait()


def gather_all(qkv, out, up, down, small):
    pin = pack_rows(qkv, out, up)
    shapes = []
    for l in range(LAYERS):
        for n in WIDTHS:
            shapes.append((ZS, YS, XS, 48, n))
        shapes.append((ZS, YS, XS, 2, 96, D))
    shapes.append((ZS, YS, XS, 2, 16, 128))
    vm = pl.BlockSpec(memory_space=pltpu.VMEM)
    got = pl.pallas_call(
        gather_kernel,
        out_shape=[jax.ShapeDtypeStruct(s, jnp.bfloat16) for s in shapes],
        in_specs=[vm, vm, vm],
        out_specs=[pl.BlockSpec(memory_space=pl.ANY)] * 9,
        scratch_shapes=[pltpu.VMEM(s, jnp.bfloat16) for s in shapes]
        + [pltpu.VMEM((LAYERS, 32, sum(WIDTHS) // 2), jnp.bfloat16), pltpu.SemaphoreType.DMA((2, 2)), pltpu.SemaphoreType.DMA((9,))]
        + gather_sems(9),
        compiler_params=pltpu.CompilerParams(collective_id=0, has_side_effects=True, vmem_limit_bytes=60 * 2**20),
    )(pin, down, small)
    res = []
    for l in range(LAYERS):
        res.append([got[l * 4 + j].reshape(D, WIDTHS[j]) for j in range(3)] + [got[l * 4 + 3].reshape(FF, D)])
    return res, got[8].reshape(32, 16, 128)


class Scatter:
    def __init__(self, place, k, grad, total, pass_a, pass_z, from_b, from_a, from_dn, from_up, sems):
        self.p, self.k = place, k
        self.grad, self.total, self.pass_a, self.pass_z = grad, total, pass_a, pass_z
        self.from_b, self.from_a, self.from_dn, self.from_up = from_b, from_a, from_dn, from_up
        self.sb, self.sa, self.sz, self.rb, self.ra, self.rdn, self.rup = sems

    def send(self, src, dst, to, ssem, rsem):
        pltpu.make_async_remote_copy(
            src_ref=src, dst_ref=dst, send_sem=ssem, recv_sem=rsem, device_id=to, device_id_type=MESH).start()

    def wait(self, piece, sem):
        pltpu.make_async_copy(piece, piece, sem).wait()

    def bsend(self, zi):
        p, k = self.p, self.k
        self.send(self.grad.at[zi, p.yb, p.xb], self.from_b.at[zi, 0], p.B, self.sb.at[k], self.rb.at[k, zi])
        self.send(self.grad.at[zi, 1 - p.y, 1 - p.x], self.from_b.at[zi, 1], p.B, self.sb.at[k], self.rb.at[k, zi])

    def bwait(self, zi):
        p, k = self.p, self.k
        self.wait(self.from_b.at[zi], self.rb.at[k, zi])
        part = self.grad[zi, p.ya, p.xa].astype(jnp.float32) + self.from_b[zi, 1].astype(jnp.float32)
        self.pass_a[zi] = part.astype(self.pass_a.dtype)
        self.send(self.pass_a.at[zi], self.from_a.at[zi], p.A, self.sa.at[k], self.ra.at[k, zi])

    def await_(self, zi):
        p, k = self.p, self.k
        self.wait(self.from_a.at[zi], self.ra.at[k, zi])
        self.total[zi] = (self.grad[zi, p.y, p.x].astype(jnp.float32)
                          + self.from_b[zi, 0].astype(jnp.float32)
                          + self.from_a[zi].astype(jnp.float32))

    def zstep(self, tau):
        p, k = self.p, self.k
        z = p.z

        @pl.when((z <= tau) & (z < 3))
        def _():
            d = 3 - tau + z

            @pl.when(z > 0)
            def _():
                self.wait(self.from_dn.at[d], self.rdn.at[k, d])
                self.pass_z[d] = (self.total[d] + self.from_dn[d].astype(jnp.float32)).astype(self.pass_z.dtype)

            @pl.when(z == 0)
            def _():
                self.pass_z[d] = self.total[d].astype(self.pass_z.dtype)

            self.send(self.pass_z.at[d], self.from_dn.at[d], p.UP, self.sz.at[k], self.rdn.at[k, d])

        @pl.when((3 - z <= tau) & (z > 0))
        def _():
            d = tau - 3 + z

            @pl.when(z < 3)
            def _():
                self.wait(self.from_up.at[d], self.rup.at[k, d])
                self.pass_z[d] = (self.total[d] + self.from_up[d].astype(jnp.float32)).astype(self.pass_z.dtype)

            @pl.when(z == 3)
            def _():
                self.pass_z[d] = self.total[d].astype(self.pass_z.dtype)

            self.send(self.pass_z.at[d], self.from_up.at[d], p.DN, self.sz.at[k], self.rup.at[k, d])

    def last(self):
        p, k = self.p, self.k
        z = p.z

        @pl.when(z > 0)
        def _():
            self.wait(self.from_dn.at[z], self.rdn.at[k, z])
            self.total[z] = self.total[z] + self.from_dn[z].astype(jnp.float32)

        @pl.when(z < 3)
        def _():
            self.wait(self.from_up.at[z], self.rup.at[k, z])
            self.total[z] = self.total[z] + self.from_up[z].astype(jnp.float32)

    def sent_b(self):
        self.wait(self.from_b, self.sb.at[self.k])

    def sent_a(self):
        self.wait(self.from_a, self.sa.at[self.k])

    def sent_z(self):
        self.wait(self.pass_z.at[pl.ds(0, 3)], self.sz.at[self.k])

    def sent(self):
        self.sent_b()
        self.sent_a()
        self.sent_z()


def scatter_sems(n):
    dma = pltpu.SemaphoreType.DMA
    return [dma((n,)), dma((n,)), dma((n,)), dma((n, 4)), dma((n, 4)), dma((n, 4)), dma((n, 4))]


def landing(shard, dtype):
    return [pltpu.VMEM(s + shard, dtype) for s in ((4, 2), (4,), (4,), (4,))]


def passing(shard, dtype):
    return [pltpu.VMEM((4, 2, 2) + shard, dtype), pltpu.VMEM((4,) + shard, jnp.float32),
            pltpu.VMEM((4,) + shard, dtype), pltpu.VMEM((4,) + shard, dtype)]


LAGS = (2, 4)
PLANES = (3, 0, 2, 1)
UP_SHARD = (48, FF // 2)
DOWN_SHARD = (192, D // 2)
SMALL_SHARD = (16, 128)


def transposed_dot(left, right):
    return lax.dot_general(left, right, (((0,), (0,)), ((), ())), preferred_element_type=jnp.float32)


def scatter_kernel(act_ref, g_ref, nf_ref, dp_ref, small_ref, up_out, down_out, small_out, *refs):
    land = [refs[4 * k:4 * k + 4] for k in range(5)]
    up_pass, down_pass = refs[20:24], refs[24:28]
    small_pass = refs[28:32]
    act_in, g_in, nf_in, dp_in, small_in, swap = refs[32:38]
    sems = refs[38:]
    p = Place()
    p.barrier()
    c = p.c

    def remote(src, dst, s, r):
        return pltpu.make_async_remote_copy(src_ref=src, dst_ref=dst, send_sem=swap.at[0, s], recv_sem=swap.at[1, r], device_id=p.C, device_id_type=MESH)

    mine_g = pl.ds(pl.multiple_of(c * (D // 2), 128), D // 2)
    mine_dp = pl.ds(pl.multiple_of(c * (FF // 2), 128), FF // 2)
    other_g = pl.ds(pl.multiple_of((1 - c) * (D // 2), 128), D // 2)
    other_dp = pl.ds(pl.multiple_of((1 - c) * (FF // 2), 128), FF // 2)
    swaps = []
    for l in (1, 0):
        for i, (src, dst) in enumerate([(act_ref.at[l], act_in.at[l]), (g_ref.at[l, :, other_g], g_in.at[l]),
                         (nf_ref.at[l], nf_in.at[l]), (dp_ref.at[l, :, other_dp], dp_in.at[l])]):
            cp = remote(src, dst, l * 4 + i, l * 4 + i)
            cp.start()
            swaps.append(cp)
    cps = remote(small_ref.at[1 - c], small_in, 8, 8)
    cps.start()

    chunks = []
    for k in range(4):
        ps = down_pass if k % 2 == 0 else up_pass
        chunks.append(Scatter(p, k, *ps, *land[k], sems))
    small = Scatter(p, 4, *small_pass, *land[4], sems)

    def down_block(l, k, zi):
        for yi in range(2):
            cols = pl.ds(768 * zi + 384 * yi, 384)
            acc = transposed_dot(act_ref[l, :, cols], g_ref[l, :, mine_g]) + transposed_dot(act_in[l, :, cols], g_in[l])
            chunks[k].grad[zi, yi] = acc.astype(jnp.bfloat16).reshape(2, 192, 384)

    def up_block(l, k, zi):
        rows = pl.ds(192 * zi, 192)
        for t in range(3):
            cols = pl.ds(pl.multiple_of(c * (FF // 2) + 512 * t, 128), 512)
            acc = transposed_dot(nf_ref[l, :, rows], dp_ref[l, :, cols]) + transposed_dot(nf_in[l, :, rows], dp_in[l, :, pl.ds(512 * t, 512)])
            chunks[k].grad[zi, :, :, :, pl.ds(512 * t, 512)] = acc.astype(jnp.bfloat16).reshape(2, 2, 48, 512)

    def deliver(k, l):
        s = chunks[k]
        s.last()
        out, rows, half = (down_out, 96, D // 2) if k % 2 == 0 else (up_out, 24, FF // 2)
        for cc in range(2):
            @pl.when(c == cc)
            def _():
                remote(s.total.at[p.z, pl.ds(rows * (1 - cc), rows)], out.at[l, :, pl.ds(half * cc, half)], 9 + k, 9 + k).start()
                out[l, :, half * cc:half * (cc + 1)] = s.total[p.z, rows * cc:rows * (cc + 1)]

    def delivered(k, l):
        out, rows, half = (down_out, 96, D // 2) if k % 2 == 0 else (up_out, 24, FF // 2)
        cp = remote(chunks[k].total.at[0, pl.ds(0, rows)], out.at[l, :, pl.ds(0, half)], 9 + k, 9 + k)
        cp.wait_send()
        cp.wait_recv()

    cps.wait()
    small.grad[...] = (small_ref[c] + small_in[...])
    for zi in PLANES:
        small.bsend(zi)
    steps = [(k, zi) for k in range(4) for zi in PLANES]
    n = len(steps)
    LB, LA = LAGS
    LZ = LA + 2
    for t in range(n + LZ + 4):
        if t < n:
            k, zi = steps[t]
            l = 1 - k // 2
            if t % 4 == 0:
                for cp in (swaps[0:2] if k % 2 == 0 else swaps[2:4]) if l == 1 else (swaps[4:6] if k % 2 == 0 else swaps[6:8]):
                    cp.wait()
                if k >= 2:
                    chunks[k - 2].sent_b()
            (down_block if k % 2 == 0 else up_block)(l, k, zi)
            chunks[k].bsend(zi)
        if 0 <= t - LB < n:
            k, zi = steps[t - LB]
            if (t - LB) % 4 == 0 and k >= 2:
                chunks[k - 2].sent_a()
            chunks[k].bwait(zi)
        if 0 <= t - LA < n:
            k, zi = steps[t - LA]
            if (t - LA) % 4 == 0 and k >= 2:
                chunks[k - 2].sent_z()
                delivered(k - 2, 1 - (k - 2) // 2)
            chunks[k].await_(zi)
        kk = (t - LZ) // 4
        if t >= LZ and kk < 4:
            j = (t - LZ) % 4
            if j < 3:
                chunks[kk].zstep(j)
            else:
                deliver(kk, 1 - kk // 2)
        if t == 2:
            for zi in PLANES:
                small.bwait(zi)
        if t == 3:
            for zi in PLANES:
                small.await_(zi)
        if 4 <= t < 7:
            small.zstep(t - 4)
        if t == 7:
            small.last()
            small_out[...] = small.total[p.z]
    for k in (2, 3):
        chunks[k].sent()
        delivered(k, 1 - k // 2)
    small.sent()


def scatter_all(act, g, nf, dp, small):
    vm = pl.BlockSpec(memory_space=pltpu.VMEM)
    t = act.shape[1]
    bf, f32 = jnp.bfloat16, jnp.float32
    scratch = []
    for k in range(4):
        scratch += landing(DOWN_SHARD if k % 2 == 0 else UP_SHARD, bf)
    scratch += landing(SMALL_SHARD, f32)
    scratch += passing(UP_SHARD, bf) + passing(DOWN_SHARD, bf) + passing(SMALL_SHARD, f32)
    scratch += [pltpu.VMEM((2, t, FF), bf), pltpu.VMEM((2, t, D // 2), bf), pltpu.VMEM((2, t, D), bf), pltpu.VMEM((2, t, FF // 2), bf),
                pltpu.VMEM((4, 2, 2) + SMALL_SHARD, f32), pltpu.SemaphoreType.DMA((2, 16))]
    scratch += scatter_sems(5)
    return pl.pallas_call(
        scatter_kernel,
        out_shape=[jax.ShapeDtypeStruct((2, 24, FF), f32), jax.ShapeDtypeStruct((2, 96, D), f32), jax.ShapeDtypeStruct(SMALL_SHARD, f32)],
        in_specs=[vm] * 5,
        out_specs=[vm] * 3,
        scratch_shapes=scratch,
        compiler_params=pltpu.CompilerParams(collective_id=1, has_side_effects=True, vmem_limit_bytes=64000 * 1024),
    )(act, g, nf, dp, small)


def pack_small(gains, shifts, b_up, b_down):
    wide = lambda v: jnp.pad(v, ((0, 0), (0, 0), (0, 128 - v.shape[-1])))
    rows = [wide(gains), wide(shifts), wide(b_down[:, None]), wide(b_up[:, None])]
    rows.append(jnp.zeros((LAYERS, 2, 128), gains.dtype))
    return jnp.concatenate(rows, axis=1).reshape(16, 128)


def unpack_small(whole):
    whole = whole.reshape(32, LAYERS, 8, 128)
    per = []
    for l in range(LAYERS):
        gains = whole[:, l, 0:2, :24].transpose(1, 0, 2).reshape(2, D)
        shifts = whole[:, l, 2:4, :24].transpose(1, 0, 2).reshape(2, D)
        per.append((gains, shifts, whole[:, l, 5, :96].reshape(FF), whole[:, l, 4, :24].reshape(D)))
    return per


def pack_sums(per):
    layers = []
    for gains, shifts, b_up, b_down in per:
        wide = lambda v, n: jnp.pad(v.reshape(-1, 32, n).transpose(1, 0, 2), ((0, 0), (0, 0), (0, 128 - n)))
        rows = [wide(gains, 24), wide(shifts, 24), wide(b_down, 24), wide(b_up, 96), jnp.zeros((32, 2, 128), jnp.float32)]
        layers.append(jnp.concatenate(rows, axis=1))
    both = jnp.concatenate(layers, axis=1)
    return both.reshape(ZS, YS, XS, 2, 16, 128).transpose(3, 0, 1, 2, 4, 5)


def fetch_forward(w_qkv, w_out, w_up, w_down, gains, shifts, b_up, b_down):
    return (
        lax.all_gather(w_qkv, ("fsdp", "rep"), axis=0, tiled=True),
        lax.all_gather(w_out, ("fsdp", "rep"), axis=0, tiled=True),
        lax.all_gather(w_up, ("fsdp", "rep"), axis=0, tiled=True),
        lax.all_gather(w_down, ("fsdp", "rep"), axis=0, tiled=True),
        lax.all_gather(gains, ("fsdp", "rep"), axis=1, tiled=True),
        lax.all_gather(shifts, ("fsdp", "rep"), axis=1, tiled=True),
        lax.all_gather(b_up, ("fsdp", "rep"), axis=0, tiled=True),
        lax.all_gather(b_down, ("fsdp", "rep"), axis=0, tiled=True),
    )


def fetch_backward(w_qkv, w_out, w_up, w_down, gains, shifts):
    return (
        lax.all_gather(w_qkv, ("fsdp", "rep"), axis=0, tiled=True),
        lax.all_gather(w_out, ("fsdp", "rep"), axis=0, tiled=True),
        lax.all_gather(w_up, ("fsdp", "rep"), axis=0, tiled=True),
        lax.all_gather(w_down, ("fsdp", "rep"), axis=0, tiled=True),
        lax.all_gather(gains, ("fsdp", "rep"), axis=1, tiled=True),
        lax.all_gather(shifts, ("fsdp", "rep"), axis=1, tiled=True),
    )


def owner_major(matrix, owners):
    width = matrix.shape[1] // owners
    return matrix.reshape(matrix.shape[0], owners, width).transpose(1, 0, 2).reshape(owners, -1)


def settle(d_up, d_down, d_gains, d_shifts, d_bup, d_bdown):
    owners = lax.axis_size("fsdp") * lax.axis_size("rep")
    members = [
        d_up.reshape(owners, -1),
        d_down.reshape(owners, -1),
        owner_major(d_gains, owners),
        owner_major(d_shifts, owners),
        d_bup.reshape(owners, -1),
        d_bdown.reshape(owners, -1),
    ]
    flat = jnp.concatenate(members, axis=1)
    mine = lax.psum_scatter(flat, ("fsdp", "rep"), scatter_dimension=0, tiled=True)
    mine = mine.reshape(-1)
    up_rows = D // owners
    down_rows = FF // owners
    norm_cols = D // owners
    sizes = [up_rows * FF, down_rows * D, 2 * norm_cols, 2 * norm_cols, down_rows, norm_cols]
    pieces = []
    begin = 0
    for length in sizes:
        pieces.append(mine[begin : begin + length])
        begin = begin + length
    return (
        pieces[0].reshape(up_rows, FF),
        pieces[1].reshape(down_rows, D),
        pieces[2].reshape(2, norm_cols),
        pieces[3].reshape(2, norm_cols),
        pieces[4],
        pieces[5],
    )


def per_device(
    hidden_in,
    caption_lengths,
    norm_gain,
    norm_bias,
    qkv_weight,
    out_weight,
    up_weight,
    up_bias,
    down_weight,
    down_bias,
    grad_out,
):
    row_count = caption_lengths.shape[0]
    near = lax.axis_size("fsdp") == 16 and lax.axis_size("rep") == 2
    if near:
        weights, short = gather_all(
            qkv_weight, out_weight, up_weight, down_weight, pack_small(norm_gain, norm_bias, up_bias, down_bias)
        )
        short = unpack_small(short)
    captions = caption_ids(caption_lengths)
    hidden = hidden_in.astype(jnp.float32)
    stored = []
    for layer_number in range(LAYERS):
        if near:
            fetched = (*weights[layer_number], *short[layer_number])
        else:
            fetched = fetch_forward(
                qkv_weight[layer_number],
                out_weight[layer_number],
                up_weight[layer_number],
                down_weight[layer_number],
                norm_gain[layer_number],
                norm_bias[layer_number],
                up_bias[layer_number],
                down_bias[layer_number],
            )
        w_qkv, w_out, w_up, w_down, gains, shifts, b_up, b_down = fetched
        gains_full = gains.astype(jnp.float32)
        shifts_full = shifts.astype(jnp.float32)
        normed_a = layer_norm(hidden, gains_full[0], shifts_full[0]).astype(jnp.bfloat16)
        packed = jnp.dot(normed_a, w_qkv, preferred_element_type=jnp.float32).astype(jnp.bfloat16)
        mixed, logsum = lax.map(attend_row, (packed.reshape(row_count, SEQ, 3 * D), captions))
        mixed = mixed.reshape(-1, D).astype(jnp.bfloat16)
        middle = hidden + jnp.dot(mixed, w_out, preferred_element_type=jnp.float32)
        normed_f = layer_norm(middle, gains_full[1], shifts_full[1]).astype(jnp.bfloat16)
        preact = jnp.dot(normed_f, w_up, preferred_element_type=jnp.float32) + b_up.astype(
            jnp.float32
        )
        active = exact_gelu(preact).astype(jnp.bfloat16)
        output = (
            middle
            + jnp.dot(active, w_down, preferred_element_type=jnp.float32)
            + b_down.astype(jnp.float32)
        )
        weights_kept = None
        stored.append((hidden, packed, logsum, middle, normed_f, preact, active, weights_kept))
        hidden = output
    gradient = grad_out.astype(jnp.float32)
    settled = [None] * LAYERS
    kept, sums = [None] * LAYERS, [None] * LAYERS
    for layer_number in reversed(range(LAYERS)):
        layer_in, packed, logsum, middle, normed_f, preact, active, weights_kept = stored[
            layer_number
        ]
        if near:
            fetched = (*weights[layer_number], *short[layer_number][:2])
        else:
            fetched = fetch_backward(
                qkv_weight[layer_number],
                out_weight[layer_number],
                up_weight[layer_number],
                down_weight[layer_number],
                norm_gain[layer_number],
                norm_bias[layer_number],
            )
        w_qkv, w_out, w_up, w_down, gains, shifts = fetched
        gains_full = gains.astype(jnp.float32)
        shifts_full = shifts.astype(jnp.float32)
        grad_low = gradient.astype(jnp.bfloat16)
        d_bdown = jnp.sum(grad_low.astype(jnp.float32), axis=0)
        d_down = None if near else transposed_left(active, grad_low)
        d_active = transposed_right(grad_low, w_down)
        gelu_value, gelu_back = jax.vjp(exact_gelu, preact)
        d_preact = gelu_back(d_active)[0].astype(jnp.bfloat16)
        d_bup = jnp.sum(d_preact.astype(jnp.float32), axis=0)
        d_up = None if near else transposed_left(normed_f, d_preact)
        d_normed_f = transposed_right(d_preact, w_up)
        norm_value, norm_back = jax.vjp(layer_norm, middle, gains_full[1], shifts_full[1])
        d_middle_ln, d_gain_f, d_shift_f = norm_back(d_normed_f)
        d_middle = gradient + d_middle_ln
        d_mixed = transposed_right(d_middle.astype(jnp.bfloat16), w_out).astype(jnp.bfloat16)
        d_packed = lax.map(
            attend_back,
            (
                packed.reshape(row_count, SEQ, 3 * D),
                captions,
                logsum,
                d_mixed.reshape(row_count, SEQ, D),
            ),
        )
        d_normed_a = transposed_right(d_packed.reshape(-1, 3 * D), w_qkv)
        first_value, first_back = jax.vjp(layer_norm, layer_in, gains_full[0], shifts_full[0])
        d_input_ln, d_gain_a, d_shift_a = first_back(d_normed_a)
        gradient = d_middle + d_input_ln
        if near:
            kept[layer_number] = (active, grad_low, normed_f, d_preact)
            sums[layer_number] = (
                jnp.stack([d_gain_a, d_gain_f]), jnp.stack([d_shift_a, d_shift_f]), d_bup, d_bdown
            )
            continue
        settled[layer_number] = settle(
            d_up,
            d_down,
            jnp.stack([d_gain_a, d_gain_f]),
            jnp.stack([d_shift_a, d_shift_f]),
            d_bup,
            d_bdown,
        )
    if near:
        d_up_all, d_down_all, short = scatter_all(*[jnp.stack(v) for v in zip(*kept)], pack_sums(sums))
        short = short.reshape(LAYERS, 8, 128)
        return (hidden, gradient, short[:, 0:2, :24], short[:, 2:4, :24], d_up_all, short[:, 5, :96], d_down_all, short[:, 4, :24])
    d_gains = jnp.stack([settled[number][2] for number in range(LAYERS)])
    d_shifts = jnp.stack([settled[number][3] for number in range(LAYERS)])
    d_up_all = jnp.stack([settled[number][0] for number in range(LAYERS)])
    d_bup_all = jnp.stack([settled[number][4] for number in range(LAYERS)])
    d_down_all = jnp.stack([settled[number][1] for number in range(LAYERS)])
    d_bdown_all = jnp.stack([settled[number][5] for number in range(LAYERS)])
    return (hidden, gradient, d_gains, d_shifts, d_up_all, d_bup_all, d_down_all, d_bdown_all)


def solution(mesh):
    in_specs = (
        P(("fsdp", "rep"), None),
        P(("fsdp", "rep"), None),
        P(None, None, ("fsdp", "rep")),
        P(None, None, ("fsdp", "rep")),
        P(None, ("fsdp", "rep"), None),
        P(None, ("fsdp", "rep"), None),
        P(None, ("fsdp", "rep"), None),
        P(None, ("fsdp", "rep")),
        P(None, ("fsdp", "rep"), None),
        P(None, ("fsdp", "rep")),
        P(("fsdp", "rep"), None),
    )
    out_specs = (
        P(("fsdp", "rep"), None),
        P(("fsdp", "rep"), None),
        P(None, None, ("fsdp", "rep")),
        P(None, None, ("fsdp", "rep")),
        P(None, ("fsdp", "rep"), None),
        P(None, ("fsdp", "rep")),
        P(None, ("fsdp", "rep"), None),
        P(None, ("fsdp", "rep")),
    )
    return jax.shard_map(
        per_device, mesh=mesh, in_specs=in_specs, out_specs=out_specs, check_vma=False
    )
```

```python
import jax
import jax.numpy as jnp
from jax import lax
from jax.sharding import PartitionSpec as P
from jax.experimental import pallas as pl
from jax.experimental.pallas import tpu as pltpu

D = 768
FF = 3072
HEADS = 12
SEQ = 512
LAYERS = 2


EPSILON = 1e-05
SCALE = 0.125


def layer_norm(values, gain, shift):
    centre = jnp.mean(values, axis=-1, keepdims=True)
    centred = values - centre
    spread = jnp.mean(centred * centred, axis=-1, keepdims=True)
    return centred * lax.rsqrt(spread + EPSILON) * gain + shift


def exact_gelu(values):
    return jax.nn.gelu(values, approximate=False)


def caption_ids(lengths):
    starts = jnp.cumsum(lengths, axis=-1) - lengths
    places = jnp.arange(SEQ, dtype=jnp.int32)
    passed = (places[None, :, None] >= starts[:, None, :]).astype(jnp.int32)
    return jnp.sum(passed, axis=-1) - 1


def transposed_left(left, right):
    return lax.dot_general(
        left, right, (((0,), (0,)), ((), ())), preferred_element_type=jnp.float32
    )


def transposed_right(left, right):
    return lax.dot_general(
        left, right, (((1,), (1,)), ((), ())), preferred_element_type=jnp.float32
    )


def split_heads(packed):
    width = D // HEADS
    queries = packed[:, :D].reshape(SEQ, HEADS, width)
    keys_part = packed[:, D : 2 * D].reshape(SEQ, HEADS, width)
    values_part = packed[:, 2 * D :].reshape(SEQ, HEADS, width)
    return (queries, keys_part, values_part)


def masked_scores(queries, keys_part, caption):
    scores = (
        jnp.einsum("qhd,khd->hqk", queries, keys_part, preferred_element_type=jnp.float32) * SCALE
    )
    same = caption[:, None] == caption[None, :]
    return jnp.where(same[None], scores, -1e30)


def attend_row(inputs):
    packed, caption = inputs
    queries, keys_part, values_part = split_heads(packed)
    scores = masked_scores(queries, keys_part, caption)
    highest = jnp.max(scores, axis=-1, keepdims=True)
    weights = jnp.exp(scores - highest)
    totals = jnp.sum(weights, axis=-1, keepdims=True)
    probs = (weights / totals).astype(jnp.bfloat16)
    mixed = jnp.einsum("hqk,khd->qhd", probs, values_part, preferred_element_type=jnp.float32)
    return (mixed.reshape(SEQ, D), highest + jnp.log(totals))


def attend_back(inputs):
    packed, caption, logsum, d_mixed = inputs
    queries, keys_part, values_part = split_heads(packed)
    probs = jnp.exp(masked_scores(queries, keys_part, caption) - logsum)
    d_heads = d_mixed.reshape(SEQ, HEADS, D // HEADS)
    d_values = jnp.einsum(
        "hqk,qhd->khd", probs.astype(jnp.bfloat16), d_heads, preferred_element_type=jnp.float32
    )
    d_probs = jnp.einsum("qhd,khd->hqk", d_heads, values_part, preferred_element_type=jnp.float32)
    centre = jnp.sum(d_probs * probs, axis=-1, keepdims=True)
    d_scores = (probs * (d_probs - centre)).astype(jnp.bfloat16)
    d_queries = (
        jnp.einsum("hqk,khd->qhd", d_scores, keys_part, preferred_element_type=jnp.float32) * SCALE
    )
    d_keys = (
        jnp.einsum("hqk,qhd->khd", d_scores, queries, preferred_element_type=jnp.float32) * SCALE
    )
    joined = jnp.concatenate(
        [d_queries.reshape(SEQ, D), d_keys.reshape(SEQ, D), d_values.reshape(SEQ, D)], axis=1
    )
    return joined.astype(jnp.bfloat16)


def fetch_forward(w_qkv, w_out, w_up, w_down, gains, shifts, b_up, b_down):
    return (
        lax.all_gather(w_qkv, ("fsdp", "rep"), axis=0, tiled=True),
        lax.all_gather(w_out, ("fsdp", "rep"), axis=0, tiled=True),
        lax.all_gather(w_up, ("fsdp", "rep"), axis=0, tiled=True),
        lax.all_gather(w_down, ("fsdp", "rep"), axis=0, tiled=True),
        lax.all_gather(gains, ("fsdp", "rep"), axis=1, tiled=True),
        lax.all_gather(shifts, ("fsdp", "rep"), axis=1, tiled=True),
        lax.all_gather(b_up, ("fsdp", "rep"), axis=0, tiled=True),
        lax.all_gather(b_down, ("fsdp", "rep"), axis=0, tiled=True),
    )


def fetch_backward(w_qkv, w_out, w_up, w_down, gains, shifts):
    return (
        lax.all_gather(w_qkv, ("fsdp", "rep"), axis=0, tiled=True),
        lax.all_gather(w_out, ("fsdp", "rep"), axis=0, tiled=True),
        lax.all_gather(w_up, ("fsdp", "rep"), axis=0, tiled=True),
        lax.all_gather(w_down, ("fsdp", "rep"), axis=0, tiled=True),
        lax.all_gather(gains, ("fsdp", "rep"), axis=1, tiled=True),
        lax.all_gather(shifts, ("fsdp", "rep"), axis=1, tiled=True),
    )


def owner_major(matrix, owners):
    width = matrix.shape[1] // owners
    return matrix.reshape(matrix.shape[0], owners, width).transpose(1, 0, 2).reshape(owners, -1)


def settle(d_up, d_down, d_gains, d_shifts, d_bup, d_bdown):
    owners = lax.axis_size("fsdp") * lax.axis_size("rep")
    members = [
        d_up.reshape(owners, -1),
        d_down.reshape(owners, -1),
        owner_major(d_gains, owners),
        owner_major(d_shifts, owners),
        d_bup.reshape(owners, -1),
        d_bdown.reshape(owners, -1),
    ]
    flat = jnp.concatenate(members, axis=1)
    mine = lax.psum_scatter(flat, ("fsdp", "rep"), scatter_dimension=0, tiled=True)
    mine = mine.reshape(-1)
    up_rows = D // owners
    down_rows = FF // owners
    norm_cols = D // owners
    sizes = [up_rows * FF, down_rows * D, 2 * norm_cols, 2 * norm_cols, down_rows, norm_cols]
    pieces = []
    begin = 0
    for length in sizes:
        pieces.append(mine[begin : begin + length])
        begin = begin + length
    return (
        pieces[0].reshape(up_rows, FF),
        pieces[1].reshape(down_rows, D),
        pieces[2].reshape(2, norm_cols),
        pieces[3].reshape(2, norm_cols),
        pieces[4],
        pieces[5],
    )


def per_device(
    hidden_in,
    caption_lengths,
    norm_gain,
    norm_bias,
    qkv_weight,
    out_weight,
    up_weight,
    up_bias,
    down_weight,
    down_bias,
    grad_out,
):
    row_count = caption_lengths.shape[0]
    captions = caption_ids(caption_lengths)
    hidden = hidden_in.astype(jnp.float32)
    stored = []
    for layer_number in range(LAYERS):
        fetched = fetch_forward(
            qkv_weight[layer_number],
            out_weight[layer_number],
            up_weight[layer_number],
            down_weight[layer_number],
            norm_gain[layer_number],
            norm_bias[layer_number],
            up_bias[layer_number],
            down_bias[layer_number],
        )
        w_qkv, w_out, w_up, w_down, gains, shifts, b_up, b_down = fetched
        gains_full = gains.astype(jnp.float32)
        shifts_full = shifts.astype(jnp.float32)
        normed_a = layer_norm(hidden, gains_full[0], shifts_full[0]).astype(jnp.bfloat16)
        packed = jnp.dot(normed_a, w_qkv, preferred_element_type=jnp.float32).astype(jnp.bfloat16)
        mixed, logsum = lax.map(attend_row, (packed.reshape(row_count, SEQ, 3 * D), captions))
        mixed = mixed.reshape(-1, D).astype(jnp.bfloat16)
        middle = hidden + jnp.dot(mixed, w_out, preferred_element_type=jnp.float32)
        normed_f = layer_norm(middle, gains_full[1], shifts_full[1]).astype(jnp.bfloat16)
        preact = jnp.dot(normed_f, w_up, preferred_element_type=jnp.float32) + b_up.astype(
            jnp.float32
        )
        active = exact_gelu(preact).astype(jnp.bfloat16)
        output = (
            middle
            + jnp.dot(active, w_down, preferred_element_type=jnp.float32)
            + b_down.astype(jnp.float32)
        )
        weights_kept = None
        stored.append((hidden, packed, logsum, middle, normed_f, preact, active, weights_kept))
        hidden = output
    gradient = grad_out.astype(jnp.float32)
    settled = [None] * LAYERS
    for layer_number in reversed(range(LAYERS)):
        layer_in, packed, logsum, middle, normed_f, preact, active, weights_kept = stored[
            layer_number
        ]
        fetched = fetch_backward(
            qkv_weight[layer_number],
            out_weight[layer_number],
            up_weight[layer_number],
            down_weight[layer_number],
            norm_gain[layer_number],
            norm_bias[layer_number],
        )
        w_qkv, w_out, w_up, w_down, gains, shifts = fetched
        gains_full = gains.astype(jnp.float32)
        shifts_full = shifts.astype(jnp.float32)
        grad_low = gradient.astype(jnp.bfloat16)
        d_bdown = jnp.sum(grad_low.astype(jnp.float32), axis=0)
        d_down = transposed_left(active, grad_low)
        d_active = transposed_right(grad_low, w_down)
        gelu_value, gelu_back = jax.vjp(exact_gelu, preact)
        d_preact = gelu_back(d_active)[0].astype(jnp.bfloat16)
        d_bup = jnp.sum(d_preact.astype(jnp.float32), axis=0)
        d_up = transposed_left(normed_f, d_preact)
        d_normed_f = transposed_right(d_preact, w_up)
        norm_value, norm_back = jax.vjp(layer_norm, middle, gains_full[1], shifts_full[1])
        d_middle_ln, d_gain_f, d_shift_f = norm_back(d_normed_f)
        d_middle = gradient + d_middle_ln
        d_mixed = transposed_right(d_middle.astype(jnp.bfloat16), w_out).astype(jnp.bfloat16)
        d_packed = lax.map(
            attend_back,
            (
                packed.reshape(row_count, SEQ, 3 * D),
                captions,
                logsum,
                d_mixed.reshape(row_count, SEQ, D),
            ),
        )
        d_normed_a = transposed_right(d_packed.reshape(-1, 3 * D), w_qkv)
        first_value, first_back = jax.vjp(layer_norm, layer_in, gains_full[0], shifts_full[0])
        d_input_ln, d_gain_a, d_shift_a = first_back(d_normed_a)
        gradient = d_middle + d_input_ln
        settled[layer_number] = settle(
            d_up,
            d_down,
            jnp.stack([d_gain_a, d_gain_f]),
            jnp.stack([d_shift_a, d_shift_f]),
            d_bup,
            d_bdown,
        )
    d_gains = jnp.stack([settled[number][2] for number in range(LAYERS)])
    d_shifts = jnp.stack([settled[number][3] for number in range(LAYERS)])
    d_up_all = jnp.stack([settled[number][0] for number in range(LAYERS)])
    d_bup_all = jnp.stack([settled[number][4] for number in range(LAYERS)])
    d_down_all = jnp.stack([settled[number][1] for number in range(LAYERS)])
    d_bdown_all = jnp.stack([settled[number][5] for number in range(LAYERS)])
    return (hidden, gradient, d_gains, d_shifts, d_up_all, d_bup_all, d_down_all, d_bdown_all)


MESH = pl.DeviceIdType.MESH
BF, F32 = jnp.bfloat16, jnp.float32
ZS, YS, XS = 4, 2, 2
QKV, OUT, UP, DOWN = range(4)
WIDTHS = (3 * D, D, FF)
HALF = sum(WIDTHS) // 2
PLANES = (3, 0, 2, 1)
UP_SHARD = (48, FF // 2)
DOWN_SHARD = (192, D // 2)
SMALL_SHARD = (16, 128)


class Place:
    def __init__(self):
        f = lax.axis_index("fsdp")
        c = lax.axis_index("rep")
        self.f, self.c = f, c
        self.x = f % 2
        self.y = (f // 2) % 2
        self.z = f // 4
        fx = f + 1 - 2 * self.x
        fy = f + 2 - 4 * self.y
        self.fa = fx + c * (fy - fx)
        self.fb = fy + c * (fx - fy)
        self.ya = (self.fa // 2) % 2
        self.xa = self.fa % 2
        self.yb = (self.fb // 2) % 2
        self.xb = self.fb % 2
        self.A = (self.fa, c)
        self.B = (self.fb, c)
        self.C = (f, 1 - c)
        self.UP = (f + 4, c)
        self.DN = (f - 4, c)
        self.has_up = self.z < 3
        self.has_dn = self.z > 0
        z = self.z
        self.order = [z]
        tables = [(0, 1, 2, 3), (1, 0, 2, 3), (2, 1, 3, 0), (3, 2, 1, 0)]
        for i in range(1, 4):
            v = jnp.int32(tables[3][i])
            for zz in (2, 1, 0):
                v = jnp.where(z == zz, tables[zz][i], v)
            self.order.append(v)

    def barrier(self):
        bar = pltpu.get_barrier_semaphore()
        for d in (self.A, self.B, self.C):
            pl.semaphore_signal(bar, inc=1, device_id=d, device_id_type=MESH)

        @pl.when(self.has_up)
        def _():
            pl.semaphore_signal(bar, inc=1, device_id=self.UP, device_id_type=MESH)

        @pl.when(self.has_dn)
        def _():
            pl.semaphore_signal(bar, inc=1, device_id=self.DN, device_id_type=MESH)

        count = 3 + self.has_up.astype(jnp.int32) + self.has_dn.astype(jnp.int32)
        pl.semaphore_wait(bar, count)


class Gather:
    def __init__(self, place, ref, rows, k, sems, by_core=False):
        self.p, self.ref, self.rows, self.k, self.by_core = place, ref, rows, k, by_core
        (self.zs, self.as_, self.bs, self.cs, self.zr, self.ar, self.br, self.cr) = sems

    def block(self, start, rows, c=None):
        c = self.p.c if c is None else c
        if self.by_core:
            return self.ref.at[c, pl.ds(start, rows)]
        half = self.ref.shape[-1] // 2
        return self.ref.at[pl.ds(start, rows), pl.ds(pl.multiple_of(c * half, 128), half)]

    def cut(self, zi, yi, xi):
        return self.block(pl.multiple_of((zi * 4 + yi * 2 + xi) * self.rows, 16), self.rows)

    def plane(self, zi, c=None):
        return self.block(pl.multiple_of(zi * 4 * self.rows, 16), 4 * self.rows, c)

    def send(self, piece, to, ssem, rsem):
        return pltpu.make_async_remote_copy(
            src_ref=piece, dst_ref=piece, send_sem=ssem, recv_sem=rsem, device_id=to, device_id_type=MESH)

    def wait(self, piece, sem):
        pltpu.make_async_copy(piece, piece, sem).wait()

    def own(self):
        p, k = self.p, self.k
        mine = self.cut(p.z, p.y, p.x)

        @pl.when(p.has_up)
        def _():
            self.send(mine, p.UP, self.zs.at[k, 0], self.zr.at[k, p.z]).start()

        @pl.when(p.has_dn)
        def _():
            self.send(mine, p.DN, self.zs.at[k, 1], self.zr.at[k, p.z]).start()

        self.send(mine, p.A, self.as_.at[k], self.ar.at[k, p.z]).start()
        self.send(mine, p.B, self.bs.at[k], self.br.at[k, p.z]).start()

    def forward(self, i):
        p = self.p
        zi = p.order[i]
        return zi, (zi < p.z) & p.has_up, (zi > p.z) & p.has_dn

    def zvisit(self, i):
        p, k = self.p, self.k
        zi, up, dn = self.forward(i)
        piece = self.cut(zi, p.y, p.x)
        self.wait(piece, self.zr.at[k, zi])

        @pl.when(up)
        def _():
            self.send(piece, p.UP, self.zs.at[k, 1 + i], self.zr.at[k, zi]).start()

        @pl.when(dn)
        def _():
            self.send(piece, p.DN, self.zs.at[k, 1 + i], self.zr.at[k, zi]).start()

        self.send(piece, p.A, self.as_.at[k], self.ar.at[k, zi]).start()
        self.send(piece, p.B, self.bs.at[k], self.br.at[k, zi]).start()

    def avisit(self, i):
        p, k = self.p, self.k
        zi = p.order[i]
        piece = self.cut(zi, p.ya, p.xa)
        self.wait(piece, self.ar.at[k, zi])
        self.send(piece, p.B, self.bs.at[k], self.br.at[k, zi]).start()

    def bvisit(self, i):
        p, k = self.p, self.k
        zi = p.order[i]
        self.wait(self.block(0, 2 * self.rows), self.br.at[k, zi])
        block = self.plane(zi)
        self.send(block, p.C, self.cs.at[k], self.cr.at[k, zi]).start()

    def cvisit(self, i):
        p, k = self.p, self.k
        zi = p.order[i]
        self.wait(self.plane(zi, 1 - p.c), self.cr.at[k, zi])

    def finish(self):
        p, k = self.p, self.k
        one = self.block(0, self.rows)

        @pl.when(p.has_up)
        def _():
            self.wait(one, self.zs.at[k, 0])

        @pl.when(p.has_dn)
        def _():
            self.wait(one, self.zs.at[k, 1])

        for i in range(1, 4):
            zi, up, dn = self.forward(i)

            @pl.when(up | dn)
            def _():
                self.wait(one, self.zs.at[k, 1 + i])

        self.wait(self.block(0, 4 * self.rows), self.as_.at[k])
        self.wait(self.block(0, 8 * self.rows), self.bs.at[k])
        self.wait(self.block(0, 16 * self.rows), self.cs.at[k])


def gather_sems(n):
    dma = pltpu.SemaphoreType.DMA
    return [dma((n, 5)), dma((n,)), dma((n,)), dma((n,)), dma((n, 4)), dma((n, 4)), dma((n, 4)), dma((n, 4))]


class Scatter:
    def __init__(self, place, k, grad, total, pass_a, pass_z, from_b, from_a, from_dn, from_up, sems, credit, owed):
        self.p, self.k = place, k
        self.grad, self.total, self.pass_a, self.pass_z = grad, total, pass_a, pass_z
        self.from_b, self.from_a, self.from_dn, self.from_up = from_b, from_a, from_dn, from_up
        self.sb, self.sa, self.sz, self.rb, self.ra, self.rdn, self.rup = sems
        self.credit, self.owed = credit, owed

    def send(self, src, dst, to, ssem, rsem):
        pltpu.make_async_remote_copy(
            src_ref=src, dst_ref=dst, send_sem=ssem, recv_sem=rsem, device_id=to, device_id_type=MESH).start()

    def wait(self, piece, sem):
        pltpu.make_async_copy(piece, piece, sem).wait()

    def bsend(self, zi, first):
        p, k = self.p, self.k
        if first and self.owed:
            pl.semaphore_wait(self.credit.at[1], 1)
        self.send(self.grad.at[zi, p.yb, p.xb], self.from_b.at[zi, 0], p.B, self.sb.at[k], self.rb.at[k, zi])
        self.send(self.grad.at[zi, 1 - p.y, 1 - p.x], self.from_b.at[zi, 1], p.B, self.sb.at[k], self.rb.at[k, zi])

    def bwait(self, zi, first):
        p, k = self.p, self.k
        if first and self.owed:
            pl.semaphore_wait(self.credit.at[0], 1)
        self.wait(self.from_b.at[zi], self.rb.at[k, zi])
        part = self.grad[zi, p.ya, p.xa].astype(jnp.float32) + self.from_b[zi, 1].astype(jnp.float32)
        self.pass_a[zi] = part.astype(self.pass_a.dtype)
        self.send(self.pass_a.at[zi], self.from_a.at[zi], p.A, self.sa.at[k], self.ra.at[k, zi])

    def await_(self, zi):
        p, k = self.p, self.k
        self.wait(self.from_a.at[zi], self.ra.at[k, zi])
        self.total[zi] = (self.grad[zi, p.y, p.x].astype(jnp.float32)
                          + self.from_b[zi, 0].astype(jnp.float32)
                          + self.from_a[zi].astype(jnp.float32))

    def zstep(self, tau):
        p, k = self.p, self.k
        z = p.z
        if tau == 0 and self.owed:
            @pl.when(p.has_up)
            def _():
                pl.semaphore_wait(self.credit.at[2], 1)

            @pl.when(p.has_dn)
            def _():
                pl.semaphore_wait(self.credit.at[3], 1)

        @pl.when((z <= tau) & (z < 3))
        def _():
            d = 3 - tau + z

            @pl.when(z > 0)
            def _():
                self.wait(self.from_dn.at[d], self.rdn.at[k, d])
                self.pass_z[d] = (self.total[d] + self.from_dn[d].astype(jnp.float32)).astype(self.pass_z.dtype)

            @pl.when(z == 0)
            def _():
                self.pass_z[d] = self.total[d].astype(self.pass_z.dtype)

            self.send(self.pass_z.at[d], self.from_dn.at[d], p.UP, self.sz.at[k], self.rdn.at[k, d])

        @pl.when((3 - z <= tau) & (z > 0))
        def _():
            d = tau - 3 + z

            @pl.when(z < 3)
            def _():
                self.wait(self.from_up.at[d], self.rup.at[k, d])
                self.pass_z[d] = (self.total[d] + self.from_up[d].astype(jnp.float32)).astype(self.pass_z.dtype)

            @pl.when(z == 3)
            def _():
                self.pass_z[d] = self.total[d].astype(self.pass_z.dtype)

            self.send(self.pass_z.at[d], self.from_up.at[d], p.DN, self.sz.at[k], self.rup.at[k, d])

    def last(self):
        p, k = self.p, self.k
        z = p.z

        @pl.when(z > 0)
        def _():
            self.wait(self.from_dn.at[z], self.rdn.at[k, z])
            self.total[z] = self.total[z] + self.from_dn[z].astype(jnp.float32)

        @pl.when(z < 3)
        def _():
            self.wait(self.from_up.at[z], self.rup.at[k, z])
            self.total[z] = self.total[z] + self.from_up[z].astype(jnp.float32)

        if self.credit is not None and not self.owed:
            def free(at, to):
                pl.semaphore_signal(self.credit.at[at], inc=1, device_id=to, device_id_type=MESH)

            free(0, p.A)
            free(1, p.B)

            @pl.when(p.has_up)
            def _():
                free(3, p.UP)

            @pl.when(p.has_dn)
            def _():
                free(2, p.DN)

    def sent_b(self):
        self.wait(self.from_b, self.sb.at[self.k])

    def sent_a(self):
        self.wait(self.from_a, self.sa.at[self.k])

    def sent_z(self):
        self.wait(self.pass_z.at[pl.ds(0, 3)], self.sz.at[self.k])

    def sent(self):
        self.sent_b()
        self.sent_a()
        self.sent_z()


def scatter_sems(n):
    dma = pltpu.SemaphoreType.DMA
    return [dma((n,)), dma((n,)), dma((n,)), dma((n, 4)), dma((n, 4)), dma((n, 4)), dma((n, 4))]


def landing(shard, dtype):
    return [pltpu.VMEM(s + shard, dtype) for s in ((4, 2), (4,), (4,), (4,))]


def passing(shard, dtype):
    return [pltpu.VMEM((4, 2, 2) + shard, dtype), pltpu.VMEM((4,) + shard, jnp.float32),
            pltpu.VMEM((4,) + shard, dtype), pltpu.VMEM((4,) + shard, dtype)]


def transposed_dot(left, right):
    return lax.dot_general(left, right, (((0,), (0,)), ((), ())), preferred_element_type=F32)


def dot_transposed(left, right):
    return lax.dot_general(left, right, (((1,), (1,)), ((), ())), preferred_element_type=F32)


def dot(left, right):
    return jnp.dot(left, right, preferred_element_type=F32)


def loop(n, body):
    def step(i, carry):
        body(i)
        return carry
    lax.fori_loop(0, n, step, 0)


def gelu_both(v):
    size = jnp.abs(v) * 0.7071067811865476
    t = 1.0 / (1.0 + 0.3275911 * size)
    poly = t * (0.254829592 + t * (-0.284496736 + t * (1.421413741 + t * (-1.453152027 + t * 1.061405429))))
    bell = jnp.exp(-0.5 * v * v)
    tail = 0.5 * poly * bell
    below = jnp.where(v >= 0, 1.0 - tail, tail)
    return v * below, below + v * (bell * 0.3989422804014327)


def iota(shape, dim):
    return lax.broadcasted_iota(jnp.int32, shape, dim)


ROW = 64


def rows_at(i, n=ROW):
    return pl.ds(pl.multiple_of(i * n, n), n)


def col_at(i, n):
    return pl.ds(pl.multiple_of(i * n, 128), n)


def fold8(v):
    return jnp.sum(v.reshape(v.shape[0] // 8, 8, v.shape[1]), axis=0)


def stats(v):
    centre = jnp.mean(v, axis=-1, keepdims=True)
    centred = v - centre
    spread = jnp.mean(centred * centred, axis=-1, keepdims=True)
    return centred, lax.rsqrt(spread + EPSILON)


def layers_kernel(hid, lengths, pin, down_in, small_in, gout, *refs):
    (hid_out, dhid, dgain, dshift, dup, dbup, ddown, dbdown,
     sp_qkv, sp_x, sp_mid, sp_act, sp_gp, sp_nf) = refs[:14]
    refs = refs[14:]
    W = [refs[0:4], refs[4:8]]
    vec, rows_v, bup_v, sums, sbup = refs[8:13]
    X, MID, TMP, ACT, ACTP, GP, DPP, NF, NFP, G, GPN = refs[13:24]
    idc, idk, idq = refs[24:27]
    ka, va = TMP.at[:, 0:128], TMP.at[:, 128:256]
    landing_sets = [refs[27:31], refs[31:35]]
    passing_sets = [refs[35:39], refs[39:43]]
    small_land, small_pass = refs[43:47], refs[47:51]
    small_from_c, small_to = refs[51:53]
    loc, swp, credit = refs[53:56]
    gsems = refs[56:64]
    ssems = refs[64:71]
    p = Place()
    c = p.c

    def local(src, dst, i):
        return pltpu.make_async_copy(src, dst, loc.at[i])

    def swap(src, dst, i):
        return pltpu.make_async_remote_copy(src_ref=src, dst_ref=dst, send_sem=swp.at[0, i], recv_sem=swp.at[1, i],
                                            device_id=p.C, device_id_type=MESH)

    def half_of(n, cc):
        return pl.ds(pl.multiple_of(cc * (n // 2), 128), n // 2)

    load_pin = local(pin, ACT.at[0:128], 0)
    load_pin.start()
    load_x = local(hid, G, 1)
    load_x.start()
    down_own = []
    for l in range(LAYERS):
        rows = pl.ds(pl.multiple_of(p.f * 192 + c * 96, 16), 96)
        cp = local(down_in.at[l, :, half_of(D, c)], W[l][DOWN].at[rows, half_of(D, c)], 2 + l)
        cp.start()
        down_own.append(cp)
    vec[c, pl.ds(pl.multiple_of(p.f * 16, 16), 16)] = small_in[...]
    p.barrier()
    down_swap = []
    for l in range(LAYERS):
        rows = pl.ds(pl.multiple_of(p.f * 192 + c * 96, 16), 96)
        cp = swap(down_in.at[l, :, half_of(D, 1 - c)], W[l][DOWN].at[rows, half_of(D, 1 - c)], l)
        down_swap.append(cp)
    load_pin.wait()
    pin_swap = []
    for l in range(LAYERS):
        cp = swap(ACT.at[pl.ds(pl.multiple_of((1 - c) * 64 + l * 32, 16), 32)], ACTP.at[pl.ds(l * 32, 32)], 2 + l)
        cp.start()
        pin_swap.append(cp)
    for cp in down_swap:
        cp.start()

    chunks = [Gather(p, vec, 16, 0, gsems, by_core=True)]
    for l in range(LAYERS):
        for j in range(4):
            chunks.append(Gather(p, W[l][j], 192 if j == DOWN else 48, 1 + l * 4 + j, gsems))

    def assemble(l):
        pin_swap[l].wait()
        off = 0
        for j, n in enumerate(WIDTHS):
            half = n // 2
            rows = pl.ds(pl.multiple_of(p.f * 48, 16), 48)
            for cc in range(2):
                @pl.when(c == cc)
                def _():
                    mine = ACT[cc * 64 + l * 32:cc * 64 + l * 32 + 24, off:off + half]
                    other = ACTP[l * 32:l * 32 + 24, off:off + half]
                    pair = [mine, other] if cc == 0 else [other, mine]
                    W[l][j][rows, cc * half:(cc + 1) * half] = jnp.concatenate(pair, axis=0)
            off += half

    chunks[0].own()
    assemble(0)
    for k in (1, 2):
        chunks[k].own()
    assemble(1)
    for l in range(LAYERS):
        down_own[l].wait()
        down_swap[l].wait()

    starts, total = [], jnp.int32(0)
    for j in range(16):
        starts.append(total)
        total = total + lengths[0, j]

    def numbers(places):
        ids = jnp.zeros(places.shape, jnp.int32)
        for s in starts:
            ids = ids + (places >= s).astype(jnp.int32)
        return ids

    def caption_numbers():
        def body(i):
            idc[rows_at(i)] = numbers(iota((ROW, 128), 0) + i * ROW)
        loop(SEQ // ROW, body)
        for i in range(4):
            idk[i] = numbers(iota((8, 256), 1) + WINDOWS[i])
            idq[i] = numbers(iota((8, 128), 1) + 128 * i)

    def unpack_vectors():
        whole = vec[...].reshape(512, 128)

        def spread(per):
            return (iota((128, D), 1) % per == iota((128, D), 0)).astype(BF)

        for l in range(LAYERS):
            for j in range(6):
                per = 96 if j == 5 else 24
                dev = iota((32, 512), 0)
                pick = iota((32, 512), 1) == (dev % 2) * 256 + (dev // 2) * 16 + (l * 8 + j)
                wide = dot(dot(pick.astype(BF), whole).astype(BF), spread(per))
                for q in range(per // 24):
                    own = iota((32, D), 0) == (iota((32, D), 1) + q * D) // per
                    line = jnp.sum(jnp.where(own, wide, 0.0), axis=0, keepdims=True)
                    if j == 5:
                        bup_v[l, 0:1, q * D:(q + 1) * D] = line
                    else:
                        rows_v[l, j:j + 1] = line

    def ln_forward(src, l, j, dst):
        def body(i):
            centred, inverse = stats(src[rows_at(i)])
            dst[rows_at(i)] = (centred * inverse * rows_v[l, j:j + 1] + rows_v[l, 2 + j:3 + j]).astype(BF)
        loop(SEQ // ROW, body)

    def first_input():
        load_x.wait()

        def body(i):
            X[rows_at(i)] = G[rows_at(i)].astype(F32)
        loop(SEQ // ROW, body)
        local(gout, G, 4).start()

    def qkv_tile(l, t):
        cols = slice(768 * t, 768 * (t + 1))
        for h in range(3):
            cc = slice(768 * t + 256 * h, 768 * t + 256 * (h + 1))
            GP[:, cc] = dot(NF[...], W[l][QKV][:, cc]).astype(BF)

    left = None

    def lanes(v, keep_left):
        lane = iota(v.shape, 1)
        return jnp.where((lane < 64) if keep_left else (lane >= 64), v, jnp.zeros_like(v))

    def stacked(v):
        return jnp.concatenate([lanes(v, True), lanes(v, False)], axis=0)

    def unstacked(v):
        top, bottom = v[:128], v[128:]
        return jnp.where(iota(top.shape, 1) < 64, top, bottom)

    def attend(j):
        for i in range(4):
            r, w = 128 * i, WINDOWS[i]
            q = GP[r:r + 128, col_at(j, 128)]
            k = GP[w:w + 256, col_at(j + 6, 128)]
            v = GP[w:w + 256, col_at(j + 12, 128)]
            scores = dot_transposed(stacked(q), k) * SCALE
            one = idc[r:r + 128]
            same = jnp.concatenate([one, one], axis=1) == idk[i, 0:1]
            same = jnp.concatenate([same, same], axis=0)
            scores = jnp.where(same, scores, -1e30)
            weights = jnp.exp(scores - jnp.max(scores, axis=1, keepdims=True))
            probs = weights * (1.0 / jnp.sum(weights, axis=1, keepdims=True))
            DPP[r:r + 128, col_at(j, 128)] = unstacked(dot(probs.astype(BF), v)).astype(BF)

    def out_tile(l, t):
        cols = slice(256 * t, 256 * (t + 1))
        MID[:, cols] = X[:, cols] + dot(DPP[:, 0:D], W[l][OUT][:, cols])

    def up_tiles(l, first, count):
        def body(t):
            cols = col_at(t + first, 256)
            for h in range(2):
                rr = slice(256 * h, 256 * (h + 1))
                pre = dot(NF[rr], W[l][UP][:, cols]) + bup_v[l, 0:1, cols]
                act, slope = gelu_both(pre)
                ACT[rr, cols] = act.astype(BF)
                GP[rr, cols] = slope.astype(BF)
        loop(count, body)

    def down_tile(l, t):
        cols = slice(256 * t, 256 * (t + 1))
        X[:, cols] = MID[:, cols] + dot(ACT[...], W[l][DOWN][:, cols]) + rows_v[l, 4:5, cols]

    def start(src, dst, i):
        return lambda: local(src, dst, i).start()

    def forward_pieces(l):
        base = 1 + 4 * l
        todo = []
        if l == 0:
            todo += [(0, caption_numbers), (0, unpack_vectors), (0, first_input)]
            todo += [(0, lambda: ln_forward(X, 0, 0, NF))]
        else:
            def begin():
                local(NF, sp_nf, 10).wait()
                local(GP, sp_gp, 9).wait()
                ln_forward(X, 1, 0, NF)
                local(X, sp_x, 11).start()
            todo += [(0, begin)]
        for t in range(3):
            todo.append((base, lambda t=t: qkv_tile(l, t)))
        todo.append((base, start(GP.at[:, 0:3 * D], sp_qkv.at[l], 5 + l)))
        for t in range(3):
            todo.append((base, lambda t=t: loop(2, lambda j: attend(2 * t + j))))

        def middle(t):
            if l == 1 and t == 0:
                local(MID, sp_mid, 7).wait()
            out_tile(l, t)
        for t in range(3):
            todo.append((base + 1, lambda t=t: middle(t)))
        todo.append((base + 1, lambda: ln_forward(MID, l, 1, NF)))

        def widen(t):
            if t == 0:
                local(GP.at[:, 0:3 * D], sp_qkv.at[l], 5 + l).wait()
                if l == 1:
                    local(ACT, sp_act, 8).wait()
            up_tiles(l, 2 * t, 2)
        for t in range(6):
            todo.append((base + 2, lambda t=t: widen(t)))
        if l == 0:
            for src, dst, i in ((MID, sp_mid, 7), (ACT, sp_act, 8), (GP, sp_gp, 9), (NF, sp_nf, 10)):
                todo.append((base + 2, start(src, dst, i)))
        else:
            todo.append((base + 2, send_act))

        def narrow(t):
            if l == 1 and t == 0:
                local(X, sp_x, 11).wait()
            down_tile(l, t)
        for t in range(3):
            todo.append((base + 3, lambda t=t: narrow(t)))
        if l == 1:
            todo.append((base + 3, start(X, hid_out, 12)))
        return todo

    def act_swap(l):
        return [swap(ACT, ACTP, 4 + 4 * l), swap(G.at[:, half_of(D, 1 - c)], GPN, 5 + 4 * l)]

    def pre_swap(l):
        return [swap(GP.at[:, half_of(FF, 1 - c)], DPP, 6 + 4 * l), swap(NF, NFP, 7 + 4 * l)]

    def send_act():
        local(gout, G, 4).wait()
        for cp in act_swap(1):
            cp.start()

    scatters = []
    for k in range(4):
        scatters.append(Scatter(p, k, *passing_sets[k % 2], *landing_sets[k % 2], ssems, credit.at[k % 2], k >= 2))
    small = Scatter(p, 4, *small_pass, *small_land, ssems, None, False)

    def down_block(l, k, zi):
        for yi in range(2):
            cols = slice(768 * zi + 384 * yi, 768 * zi + 384 * (yi + 1))
            acc = transposed_dot(ACT[:, cols], G[:, half_of(D, c)]) + transposed_dot(ACTP[:, cols], GPN[...])
            scatters[k].grad[zi, yi] = acc.astype(BF).reshape(2, 192, 384)

    def up_block(l, k, zi):
        rows = slice(192 * zi, 192 * (zi + 1))
        for t in range(3):
            cols = pl.ds(pl.multiple_of(c * (FF // 2) + 512 * t, 128), 512)
            acc = transposed_dot(NF[:, rows], GP[:, cols]) + transposed_dot(NFP[:, rows], DPP[:, 512 * t:512 * (t + 1)])
            scatters[k].grad[zi, :, :, :, 512 * t:512 * (t + 1)] = acc.astype(BF).reshape(2, 2, 48, 512)

    def out_rows(k):
        return (ddown, 96, D) if k % 2 == 0 else (dup, 24, FF)

    def deliver(k):
        s, l = scatters[k], 1 - k // 2
        s.last()
        out, n, wide = out_rows(k)
        for cc in range(2):
            @pl.when(c == cc)
            def _():
                cols = pl.ds(wide // 2 * cc, wide // 2)
                swap(s.total.at[p.z, pl.ds(n * (1 - cc), n)], out.at[l, :, cols], 12 + k).start()
                local(s.total.at[p.z, pl.ds(n * cc, n)], out.at[l, :, cols], 20 + k).start()

    def delivered(k):
        s, l = scatters[k], 1 - k // 2
        out, n, wide = out_rows(k)
        cols = pl.ds(0, wide // 2)
        cp = swap(s.total.at[0, pl.ds(0, n)], out.at[l, :, cols], 12 + k)
        cp.wait_send()
        cp.wait_recv()
        local(s.total.at[0, pl.ds(0, n)], out.at[l, :, cols], 20 + k).wait()

    def d_down_bias(l):
        acc = jnp.zeros((8, D), F32)
        for i in range(SEQ // ROW):
            acc = acc + fold8(G[i * ROW:(i + 1) * ROW].astype(F32))
        sums[l, 4] = acc

    def d_pre_tiles(l, first, count):
        def body(t):
            cols = col_at(t + first, 256)
            rows = pl.ds(pl.multiple_of((t + first) * 256, 256), 256)
            acc = jnp.zeros((8, 256), F32)
            for h in range(2):
                rr = slice(256 * h, 256 * (h + 1))
                d = (dot_transposed(G[rr], W[l][DOWN][rows]) * GP[rr, cols].astype(F32)).astype(BF)
                GP[rr, cols] = d
                acc = acc + fold8(d.astype(F32))
            sbup[l, :, cols] = acc
        loop(count, body)

    def d_normed_f_tile(l, t):
        TMP[:, 256 * t:256 * (t + 1)] = dot_transposed(GP[...], W[l][UP][256 * t:256 * (t + 1)])

    def ln_backward(src, grad, add, l, j, dst, low, convert=None):
        sums[l, j] = jnp.zeros((8, D), F32)
        sums[l, 2 + j] = jnp.zeros((8, D), F32)

        def body(i):
            rr = rows_at(i)
            centred, inverse = stats(src[rr].astype(F32))
            unit = centred * inverse
            d = grad[rr]
            sums[l, j] += fold8(d * unit)
            sums[l, 2 + j] += fold8(d)
            scaled = d * rows_v[l, j:j + 1]
            mean_d = jnp.mean(scaled, axis=-1, keepdims=True)
            mean_u = jnp.mean(scaled * unit, axis=-1, keepdims=True)
            result = add[rr].astype(F32) + inverse * (scaled - mean_d - unit * mean_u)
            dst[rr] = result
            if low is not None:
                low[rr, 0:D] = result.astype(BF)
        loop(SEQ // ROW, body)

    def d_mixed_tile(l, t):
        ACT[:, 3 * D + 256 * t:3 * D + 256 * (t + 1)] = dot_transposed(ACT[:, 0:D], W[l][OUT][256 * t:256 * (t + 1)]).astype(BF)

    def attend_back(j):
        ka[...] = jnp.zeros((SEQ, 128), F32)
        va[...] = jnp.zeros((SEQ, 128), F32)
        for i in range(4):
            r, w = 128 * i, WINDOWS[i]
            q = stacked(GP[r:r + 128, col_at(j, 128)])
            k = GP[w:w + 256, col_at(j + 6, 128)]
            v = GP[w:w + 256, col_at(j + 12, 128)]
            d = stacked(ACT[r:r + 128, col_at(j + 18, 128)])
            scores = dot_transposed(k, q) * SCALE
            same = idc[w:w + 256] == idq[i, 0:1]
            same = jnp.concatenate([same, same], axis=1)
            scores = jnp.where(same, scores, -1e30)
            weights = jnp.exp(scores - jnp.max(scores, axis=0, keepdims=True))
            probs = weights * (1.0 / jnp.sum(weights, axis=0, keepdims=True))
            va[w:w + 256] += dot(probs.astype(BF), d)
            d_probs = dot_transposed(v, d)
            centre = jnp.sum(d_probs * probs, axis=0, keepdims=True)
            d_scores = (probs * (d_probs - centre)).astype(BF)
            ka[w:w + 256] += dot(d_scores, q)
            d_q = transposed_dot(d_scores, k) * SCALE
            ACT[r:r + 128, col_at(j, 128)] = unstacked(d_q).astype(BF)
        ACT[:, col_at(j + 6, 128)] = (ka[...] * SCALE).astype(BF)
        ACT[:, col_at(j + 12, 128)] = va[...].astype(BF)

    def d_normed_a_tile(l, t):
        TMP[:, 256 * t:256 * (t + 1)] = dot_transposed(ACT[:, 0:3 * D], W[l][QKV][256 * t:256 * (t + 1)])

    def pack_small():
        def spread(per):
            return (iota((D, 128), 0) % per == iota((D, 128), 1)).astype(F32)

        for l in range(LAYERS):
            for j in range(6):
                per = 96 if j == 5 else 24
                dev = iota((32, D), 0)
                number = (dev % 16) * 2 + dev // 16
                picked = jnp.zeros((32, D), F32)
                for q in range(per // 24):
                    full = sbup[l, :, q * D:(q + 1) * D] if j == 5 else sums[l, j]
                    line = jnp.sum(full, axis=0, keepdims=True)
                    own = number == (iota((32, D), 1) + q * D) // per
                    picked = picked + jnp.where(own, line, 0.0)
                part = jnp.dot(picked, spread(per), precision=lax.Precision.HIGHEST, preferred_element_type=F32)
                small_to[:, :, l * 8 + j, :] = part.reshape(2, 16, 128)

    now = [0]
    events = []

    def later(delay, k, fn):
        events.append((now[0] + delay, len(events), k, fn))

    done = [0]

    def run_events(limit=None, upto=None):
        pending = sorted(e for e in events if e is not None)
        ran = 0
        for e in pending:
            if upto is not None:
                if e[2] > upto:
                    continue
            elif e[0] > now[0]:
                break
            if limit is not None and ran >= limit:
                break
            events[e[1]] = None
            e[3]()
            ran += 1

    def piece(fn):
        fn()
        now[0] += 1
        run_events()

    def block(k, zi, fn):
        l = 1 - k // 2
        s = scatters[k]
        first = zi == PLANES[0]
        if first and k >= 2:
            run_events(upto=k - 2)
            scatters[k - 2].sent()
            delivered(k - 2)
        fn(l, k, zi)
        s.bsend(zi, first)
        later(LB, k, lambda: s.bwait(zi, first))
        later(LA, k, lambda: s.await_(zi))
        if zi == PLANES[-1]:
            for j in range(3):
                later(LA + 1 + LZ * j, k, lambda j=j: s.zstep(j))
            later(LA + 1 + LZ * 3, k, lambda: deliver(k))
        now[0] += 1
        run_events()

    def blocks(k):
        for zi in PLANES:
            block(k, zi, down_block if k % 2 == 0 else up_block)

    todo = forward_pieces(0) + forward_pieces(1)
    at = [0]
    arrived = -1

    def run_forward(count):
        while count > 0 and at[0] < len(todo) and todo[at[0]][0] <= arrived:
            todo[at[0]][1]()
            at[0] += 1
            count -= 1

    n = len(chunks)
    for t in range(n + 3):
        if t + 3 < n:
            chunks[t + 3].own()
        if t < n:
            for i in range(1, 4):
                chunks[t].zvisit(i)
            run_forward(1)
        if 0 <= t - 1 < n:
            for i in range(4):
                chunks[t - 1].avisit(i)
            run_forward(1)
        if 0 <= t - 2 < n:
            for i in range(4):
                chunks[t - 2].bvisit(i)
            run_forward(1)
        if 0 <= t - 3 < n:
            for i in range(4):
                chunks[t - 3].cvisit(i)
            arrived = t - 3
            run_forward(PER)
    run_forward(1000)
    for ch in chunks:
        ch.finish()

    for l in (1, 0):
        k = 2 * (1 - l)
        for cp in act_swap(l):
            if l == 0:
                cp.start()
        piece(lambda: d_down_bias(l))
        for cp in act_swap(l):
            cp.wait_recv()
        blocks(k)
        for t in range(6):
            piece(lambda t=t: d_pre_tiles(l, 2 * t, 2))
        for cp in pre_swap(l):
            cp.start()
        for t in range(3):
            piece(lambda t=t: d_normed_f_tile(l, t))
        for cp in pre_swap(l):
            cp.wait_recv()
        blocks(k + 1)
        for cp in act_swap(l) + pre_swap(l):
            cp.wait_send()
        local(sp_qkv.at[l], GP.at[:, 0:3 * D], 13 + l).start()
        if l == 1:
            local(X, hid_out, 12).wait()
            local(sp_x, X, 15).start()
            local(sp_nf, NF, 17).start()
        else:
            local(hid, NF, 16).start()
        piece(lambda: ln_backward(MID, TMP, G if l == 1 else X, l, 1, MID, ACT))
        for t in range(3):
            piece(lambda t=t: d_mixed_tile(l, t))
        local(sp_qkv.at[l], GP.at[:, 0:3 * D], 13 + l).wait()
        for j in range(3):
            piece(lambda j=j: loop(2, lambda i: attend_back(2 * j + i)))
        if l == 1:
            local(sp_gp, GP, 18).start()
        for t in range(3):
            piece(lambda t=t: d_normed_a_tile(l, t))
        if l == 1:
            local(sp_act, ACT, 19).start()
            local(sp_x, X, 15).wait()
            piece(lambda: ln_backward(X, TMP, MID, l, 0, X, G))
            local(sp_mid, MID, 24).start()
            for cp, i in ((local(sp_act, ACT, 19), 0), (local(sp_gp, GP, 18), 0), (local(sp_nf, NF, 17), 0), (local(sp_mid, MID, 24), 0)):
                cp.wait()
        else:
            local(hid, NF, 16).wait()
            piece(lambda: ln_backward(NF, TMP, MID, l, 0, X, None))
            local(X, dhid, 25).start()
    pack_small()
    cp = swap(small_to.at[1 - c], small_from_c, 16)
    cp.start()
    cp.wait()
    small.grad[...] = (small_to[c] + small_from_c[...]).reshape(ZS, YS, XS, 16, 128)
    for zi in PLANES:
        small.bsend(zi, False)
    run_events(upto=3)
    for zi in PLANES:
        small.bwait(zi, False)
    for zi in PLANES:
        small.await_(zi)
    for j in range(3):
        small.zstep(j)
    small.last()
    for l in range(LAYERS):
        dgain[l] = small.total[p.z, l * 8:l * 8 + 2, 0:24]
        dshift[l] = small.total[p.z, l * 8 + 2:l * 8 + 4, 0:24]
        dbdown[l:l + 1] = small.total[p.z, l * 8 + 4:l * 8 + 5, 0:24]
        dbup[l:l + 1] = small.total[p.z, l * 8 + 5:l * 8 + 6, 0:96]
    small.sent()
    for k in (2, 3):
        scatters[k].sent()
        delivered(k)
    local(X, dhid, 25).wait()


WINDOWS = (0, 64, 192, 256)
LB, LA, LZ = 3, 6, 1
PER = 2


def pack_rows(qkv, out, up):
    parts = []
    for h in range(2):
        parts.append(jnp.concatenate([w[:, :, h * (w.shape[-1] // 2):(h + 1) * (w.shape[-1] // 2)] for w in (qkv, out, up)], axis=-1))
    both = jnp.stack(parts)
    return jnp.pad(both, ((0, 0), (0, 0), (0, 8), (0, 0))).reshape(128, HALF)


def pack_short(gains, shifts, b_up, b_down):
    wide = lambda v: jnp.pad(v, ((0, 0), (0, 0), (0, 128 - v.shape[-1])))
    rows = [wide(gains), wide(shifts), wide(b_down[:, None]), wide(b_up[:, None])]
    rows.append(jnp.zeros((LAYERS, 2, 128), gains.dtype))
    return jnp.concatenate(rows, axis=1).reshape(16, 128)


def layers_on_slice(hidden_in, caption_lengths, norm_gain, norm_bias, qkv_weight, out_weight, up_weight, up_bias, down_weight, down_bias, grad_out):
    shape = jax.ShapeDtypeStruct
    vm, hbm, sm = [pl.BlockSpec(memory_space=s) for s in (pltpu.VMEM, pl.ANY, pltpu.SMEM)]
    outs = [
        (shape((SEQ, D), F32), hbm), (shape((SEQ, D), F32), hbm),
        (shape((2, 2, 24), F32), vm), (shape((2, 2, 24), F32), vm),
        (shape((2, 24, FF), F32), hbm), (shape((2, 96), F32), vm),
        (shape((2, 96, D), F32), hbm), (shape((2, 24), F32), vm),
        (shape((2, SEQ, 3 * D), BF), hbm), (shape((SEQ, D), F32), hbm), (shape((SEQ, D), F32), hbm),
        (shape((SEQ, FF), BF), hbm), (shape((SEQ, FF), BF), hbm), (shape((SEQ, D), BF), hbm),
    ]
    v = pltpu.VMEM
    scratch = []
    for l in range(LAYERS):
        scratch += [v((D, 3 * D), BF), v((D, D), BF), v((D, FF), BF), v((FF, D), BF)]
    scratch += [v((2, 256, 128), BF), v((2, 8, D), F32), v((2, 1, FF), F32), v((2, 5, 8, D), F32), v((2, 8, FF), F32)]
    scratch += [v((SEQ, D), F32)] * 3
    scratch += [v((SEQ, FF), BF)] * 3
    scratch += [v((SEQ, FF // 2), BF), v((SEQ, D), BF), v((SEQ, D), BF), v((SEQ, D), BF), v((SEQ, D // 2), BF)]
    scratch += [v((SEQ, 128), jnp.int32), v((4, 8, 256), jnp.int32), v((4, 8, 128), jnp.int32)]
    scratch += landing(DOWN_SHARD, BF) + landing(UP_SHARD, BF)
    scratch += passing(DOWN_SHARD, BF) + passing(UP_SHARD, BF)
    scratch += landing(SMALL_SHARD, F32) + passing(SMALL_SHARD, F32)
    scratch += [v((16, 16, 128), F32), v((2, 16, 16, 128), F32)]
    scratch += [pltpu.SemaphoreType.DMA((26,)), pltpu.SemaphoreType.DMA((2, 17)), pltpu.SemaphoreType.REGULAR((2, 4))]
    scratch += gather_sems(9) + scatter_sems(5)
    got = pl.pallas_call(
        layers_kernel,
        out_shape=[o[0] for o in outs],
        in_specs=[hbm, sm, hbm, hbm, vm, hbm],
        out_specs=[o[1] for o in outs],
        scratch_shapes=scratch,
        compiler_params=pltpu.CompilerParams(collective_id=0, has_side_effects=True, vmem_limit_bytes=VMEM_LIMIT),
    )(hidden_in, caption_lengths, pack_rows(qkv_weight, out_weight, up_weight), down_weight,
      pack_short(norm_gain, norm_bias, up_bias, down_bias), grad_out)
    return tuple(got[:8])


VMEM_LIMIT = 64 * 2**20


def solution(mesh):
    in_specs = (
        P(("fsdp", "rep"), None),
        P(("fsdp", "rep"), None),
        P(None, None, ("fsdp", "rep")),
        P(None, None, ("fsdp", "rep")),
        P(None, ("fsdp", "rep"), None),
        P(None, ("fsdp", "rep"), None),
        P(None, ("fsdp", "rep"), None),
        P(None, ("fsdp", "rep")),
        P(None, ("fsdp", "rep"), None),
        P(None, ("fsdp", "rep")),
        P(("fsdp", "rep"), None),
    )
    out_specs = (
        P(("fsdp", "rep"), None),
        P(("fsdp", "rep"), None),
        P(None, None, ("fsdp", "rep")),
        P(None, None, ("fsdp", "rep")),
        P(None, ("fsdp", "rep"), None),
        P(None, ("fsdp", "rep")),
        P(None, ("fsdp", "rep"), None),
        P(None, ("fsdp", "rep")),
    )
    near = dict(mesh.shape) == {"fsdp": 16, "rep": 2}
    return jax.shard_map(
        layers_on_slice if near else per_device, mesh=mesh, in_specs=in_specs, out_specs=out_specs, check_vma=False
    )
```

```python
import jax
import jax.numpy as jnp
from jax import lax
from jax.sharding import PartitionSpec as P
from jax.experimental import pallas as pl
from jax.experimental.pallas import tpu as pltpu

D = 768
FF = 3072
HEADS = 12
SEQ = 512
LAYERS = 2


EPSILON = 1e-05
SCALE = 0.125


def layer_norm(values, gain, shift):
    centre = jnp.mean(values, axis=-1, keepdims=True)
    centred = values - centre
    spread = jnp.mean(centred * centred, axis=-1, keepdims=True)
    return centred * lax.rsqrt(spread + EPSILON) * gain + shift


def exact_gelu(values):
    return jax.nn.gelu(values, approximate=False)


def caption_ids(lengths):
    starts = jnp.cumsum(lengths, axis=-1) - lengths
    places = jnp.arange(SEQ, dtype=jnp.int32)
    passed = (places[None, :, None] >= starts[:, None, :]).astype(jnp.int32)
    return jnp.sum(passed, axis=-1) - 1


def transposed_left(left, right):
    return lax.dot_general(
        left, right, (((0,), (0,)), ((), ())), preferred_element_type=jnp.float32
    )


def transposed_right(left, right):
    return lax.dot_general(
        left, right, (((1,), (1,)), ((), ())), preferred_element_type=jnp.float32
    )


def split_heads(packed):
    width = D // HEADS
    queries = packed[:, :D].reshape(SEQ, HEADS, width)
    keys_part = packed[:, D : 2 * D].reshape(SEQ, HEADS, width)
    values_part = packed[:, 2 * D :].reshape(SEQ, HEADS, width)
    return (queries, keys_part, values_part)


def masked_scores(queries, keys_part, caption):
    scores = (
        jnp.einsum("qhd,khd->hqk", queries, keys_part, preferred_element_type=jnp.float32) * SCALE
    )
    same = caption[:, None] == caption[None, :]
    return jnp.where(same[None], scores, -1e30)


def attend_row(inputs):
    packed, caption = inputs
    queries, keys_part, values_part = split_heads(packed)
    scores = masked_scores(queries, keys_part, caption)
    highest = jnp.max(scores, axis=-1, keepdims=True)
    weights = jnp.exp(scores - highest)
    totals = jnp.sum(weights, axis=-1, keepdims=True)
    probs = (weights / totals).astype(jnp.bfloat16)
    mixed = jnp.einsum("hqk,khd->qhd", probs, values_part, preferred_element_type=jnp.float32)
    return (mixed.reshape(SEQ, D), highest + jnp.log(totals))


def attend_back(inputs):
    packed, caption, logsum, d_mixed = inputs
    queries, keys_part, values_part = split_heads(packed)
    probs = jnp.exp(masked_scores(queries, keys_part, caption) - logsum)
    d_heads = d_mixed.reshape(SEQ, HEADS, D // HEADS)
    d_values = jnp.einsum(
        "hqk,qhd->khd", probs.astype(jnp.bfloat16), d_heads, preferred_element_type=jnp.float32
    )
    d_probs = jnp.einsum("qhd,khd->hqk", d_heads, values_part, preferred_element_type=jnp.float32)
    centre = jnp.sum(d_probs * probs, axis=-1, keepdims=True)
    d_scores = (probs * (d_probs - centre)).astype(jnp.bfloat16)
    d_queries = (
        jnp.einsum("hqk,khd->qhd", d_scores, keys_part, preferred_element_type=jnp.float32) * SCALE
    )
    d_keys = (
        jnp.einsum("hqk,qhd->khd", d_scores, queries, preferred_element_type=jnp.float32) * SCALE
    )
    joined = jnp.concatenate(
        [d_queries.reshape(SEQ, D), d_keys.reshape(SEQ, D), d_values.reshape(SEQ, D)], axis=1
    )
    return joined.astype(jnp.bfloat16)


def fetch_forward(w_qkv, w_out, w_up, w_down, gains, shifts, b_up, b_down):
    return (
        lax.all_gather(w_qkv, ("fsdp", "rep"), axis=0, tiled=True),
        lax.all_gather(w_out, ("fsdp", "rep"), axis=0, tiled=True),
        lax.all_gather(w_up, ("fsdp", "rep"), axis=0, tiled=True),
        lax.all_gather(w_down, ("fsdp", "rep"), axis=0, tiled=True),
        lax.all_gather(gains, ("fsdp", "rep"), axis=1, tiled=True),
        lax.all_gather(shifts, ("fsdp", "rep"), axis=1, tiled=True),
        lax.all_gather(b_up, ("fsdp", "rep"), axis=0, tiled=True),
        lax.all_gather(b_down, ("fsdp", "rep"), axis=0, tiled=True),
    )


def fetch_backward(w_qkv, w_out, w_up, w_down, gains, shifts):
    return (
        lax.all_gather(w_qkv, ("fsdp", "rep"), axis=0, tiled=True),
        lax.all_gather(w_out, ("fsdp", "rep"), axis=0, tiled=True),
        lax.all_gather(w_up, ("fsdp", "rep"), axis=0, tiled=True),
        lax.all_gather(w_down, ("fsdp", "rep"), axis=0, tiled=True),
        lax.all_gather(gains, ("fsdp", "rep"), axis=1, tiled=True),
        lax.all_gather(shifts, ("fsdp", "rep"), axis=1, tiled=True),
    )


def owner_major(matrix, owners):
    width = matrix.shape[1] // owners
    return matrix.reshape(matrix.shape[0], owners, width).transpose(1, 0, 2).reshape(owners, -1)


def settle(d_up, d_down, d_gains, d_shifts, d_bup, d_bdown):
    owners = lax.axis_size("fsdp") * lax.axis_size("rep")
    members = [
        d_up.reshape(owners, -1),
        d_down.reshape(owners, -1),
        owner_major(d_gains, owners),
        owner_major(d_shifts, owners),
        d_bup.reshape(owners, -1),
        d_bdown.reshape(owners, -1),
    ]
    flat = jnp.concatenate(members, axis=1)
    mine = lax.psum_scatter(flat, ("fsdp", "rep"), scatter_dimension=0, tiled=True)
    mine = mine.reshape(-1)
    up_rows = D // owners
    down_rows = FF // owners
    norm_cols = D // owners
    sizes = [up_rows * FF, down_rows * D, 2 * norm_cols, 2 * norm_cols, down_rows, norm_cols]
    pieces = []
    begin = 0
    for length in sizes:
        pieces.append(mine[begin : begin + length])
        begin = begin + length
    return (
        pieces[0].reshape(up_rows, FF),
        pieces[1].reshape(down_rows, D),
        pieces[2].reshape(2, norm_cols),
        pieces[3].reshape(2, norm_cols),
        pieces[4],
        pieces[5],
    )


def per_device(
    hidden_in,
    caption_lengths,
    norm_gain,
    norm_bias,
    qkv_weight,
    out_weight,
    up_weight,
    up_bias,
    down_weight,
    down_bias,
    grad_out,
):
    row_count = caption_lengths.shape[0]
    captions = caption_ids(caption_lengths)
    hidden = hidden_in.astype(jnp.float32)
    stored = []
    for layer_number in range(LAYERS):
        fetched = fetch_forward(
            qkv_weight[layer_number],
            out_weight[layer_number],
            up_weight[layer_number],
            down_weight[layer_number],
            norm_gain[layer_number],
            norm_bias[layer_number],
            up_bias[layer_number],
            down_bias[layer_number],
        )
        w_qkv, w_out, w_up, w_down, gains, shifts, b_up, b_down = fetched
        gains_full = gains.astype(jnp.float32)
        shifts_full = shifts.astype(jnp.float32)
        normed_a = layer_norm(hidden, gains_full[0], shifts_full[0]).astype(jnp.bfloat16)
        packed = jnp.dot(normed_a, w_qkv, preferred_element_type=jnp.float32).astype(jnp.bfloat16)
        mixed, logsum = lax.map(attend_row, (packed.reshape(row_count, SEQ, 3 * D), captions))
        mixed = mixed.reshape(-1, D).astype(jnp.bfloat16)
        middle = hidden + jnp.dot(mixed, w_out, preferred_element_type=jnp.float32)
        normed_f = layer_norm(middle, gains_full[1], shifts_full[1]).astype(jnp.bfloat16)
        preact = jnp.dot(normed_f, w_up, preferred_element_type=jnp.float32) + b_up.astype(
            jnp.float32
        )
        active = exact_gelu(preact).astype(jnp.bfloat16)
        output = (
            middle
            + jnp.dot(active, w_down, preferred_element_type=jnp.float32)
            + b_down.astype(jnp.float32)
        )
        weights_kept = None
        stored.append((hidden, packed, logsum, middle, normed_f, preact, active, weights_kept))
        hidden = output
    gradient = grad_out.astype(jnp.float32)
    settled = [None] * LAYERS
    for layer_number in reversed(range(LAYERS)):
        layer_in, packed, logsum, middle, normed_f, preact, active, weights_kept = stored[
            layer_number
        ]
        fetched = fetch_backward(
            qkv_weight[layer_number],
            out_weight[layer_number],
            up_weight[layer_number],
            down_weight[layer_number],
            norm_gain[layer_number],
            norm_bias[layer_number],
        )
        w_qkv, w_out, w_up, w_down, gains, shifts = fetched
        gains_full = gains.astype(jnp.float32)
        shifts_full = shifts.astype(jnp.float32)
        grad_low = gradient.astype(jnp.bfloat16)
        d_bdown = jnp.sum(grad_low.astype(jnp.float32), axis=0)
        d_down = transposed_left(active, grad_low)
        d_active = transposed_right(grad_low, w_down)
        gelu_value, gelu_back = jax.vjp(exact_gelu, preact)
        d_preact = gelu_back(d_active)[0].astype(jnp.bfloat16)
        d_bup = jnp.sum(d_preact.astype(jnp.float32), axis=0)
        d_up = transposed_left(normed_f, d_preact)
        d_normed_f = transposed_right(d_preact, w_up)
        norm_value, norm_back = jax.vjp(layer_norm, middle, gains_full[1], shifts_full[1])
        d_middle_ln, d_gain_f, d_shift_f = norm_back(d_normed_f)
        d_middle = gradient + d_middle_ln
        d_mixed = transposed_right(d_middle.astype(jnp.bfloat16), w_out).astype(jnp.bfloat16)
        d_packed = lax.map(
            attend_back,
            (
                packed.reshape(row_count, SEQ, 3 * D),
                captions,
                logsum,
                d_mixed.reshape(row_count, SEQ, D),
            ),
        )
        d_normed_a = transposed_right(d_packed.reshape(-1, 3 * D), w_qkv)
        first_value, first_back = jax.vjp(layer_norm, layer_in, gains_full[0], shifts_full[0])
        d_input_ln, d_gain_a, d_shift_a = first_back(d_normed_a)
        gradient = d_middle + d_input_ln
        settled[layer_number] = settle(
            d_up,
            d_down,
            jnp.stack([d_gain_a, d_gain_f]),
            jnp.stack([d_shift_a, d_shift_f]),
            d_bup,
            d_bdown,
        )
    d_gains = jnp.stack([settled[number][2] for number in range(LAYERS)])
    d_shifts = jnp.stack([settled[number][3] for number in range(LAYERS)])
    d_up_all = jnp.stack([settled[number][0] for number in range(LAYERS)])
    d_bup_all = jnp.stack([settled[number][4] for number in range(LAYERS)])
    d_down_all = jnp.stack([settled[number][1] for number in range(LAYERS)])
    d_bdown_all = jnp.stack([settled[number][5] for number in range(LAYERS)])
    return (hidden, gradient, d_gains, d_shifts, d_up_all, d_bup_all, d_down_all, d_bdown_all)


MESH = pl.DeviceIdType.MESH
BF, F32 = jnp.bfloat16, jnp.float32
ZS, YS, XS = 4, 2, 2
QKV, OUT, UP, DOWN = range(4)
WIDTHS = (3 * D, D, FF)
HALF = sum(WIDTHS) // 2
PLANES = (3, 0, 2, 1)
UP_SHARD = (48, FF // 2)
DOWN_SHARD = (192, D // 2)
SMALL_SHARD = (16, 128)


class Place:
    def __init__(self):
        f = lax.axis_index("fsdp")
        c = lax.axis_index("rep")
        self.f, self.c = f, c
        self.x = f % 2
        self.y = (f // 2) % 2
        self.z = f // 4
        fx = f + 1 - 2 * self.x
        fy = f + 2 - 4 * self.y
        self.fa = fx + c * (fy - fx)
        self.fb = fy + c * (fx - fy)
        self.ya = (self.fa // 2) % 2
        self.xa = self.fa % 2
        self.yb = (self.fb // 2) % 2
        self.xb = self.fb % 2
        self.A = (self.fa, c)
        self.B = (self.fb, c)
        self.C = (f, 1 - c)
        self.UP = (f + 4, c)
        self.DN = (f - 4, c)
        self.has_up = self.z < 3
        self.has_dn = self.z > 0

    def barrier(self):
        bar = pltpu.get_barrier_semaphore()
        for d in (self.A, self.B, self.C):
            pl.semaphore_signal(bar, inc=1, device_id=d, device_id_type=MESH)

        @pl.when(self.has_up)
        def _():
            pl.semaphore_signal(bar, inc=1, device_id=self.UP, device_id_type=MESH)

        @pl.when(self.has_dn)
        def _():
            pl.semaphore_signal(bar, inc=1, device_id=self.DN, device_id_type=MESH)

        count = 3 + self.has_up.astype(jnp.int32) + self.has_dn.astype(jnp.int32)
        pl.semaphore_wait(bar, count)


class Gather:
    def __init__(self, place, ref, rows, k, sems, by_core=False):
        self.p, self.ref, self.rows, self.k, self.by_core = place, ref, rows, k, by_core
        self.planes_first = k in PLANES_FIRST
        (self.zs, self.as_, self.bs, self.cs, self.zr, self.ar, self.br, self.cr) = sems

    def block(self, start, rows, c=None):
        c = self.p.c if c is None else c
        if self.by_core:
            return self.ref.at[c, pl.ds(start, rows)]
        half = self.ref.shape[-1] // 2
        return self.ref.at[pl.ds(start, rows), pl.ds(pl.multiple_of(c * half, 128), half)]

    def cut(self, zi, yi, xi):
        return self.block(pl.multiple_of((zi * 4 + yi * 2 + xi) * self.rows, 16), self.rows)

    def plane(self, zi, c=None):
        return self.block(pl.multiple_of(zi * 4 * self.rows, 16), 4 * self.rows, c)

    def send(self, piece, to, ssem, rsem):
        pltpu.make_async_remote_copy(
            src_ref=piece, dst_ref=piece, send_sem=ssem, recv_sem=rsem, device_id=to, device_id_type=MESH).start()

    def wait(self, piece, sem):
        pltpu.make_async_copy(piece, piece, sem).wait()

    def unit(self, zi):
        return self.plane(zi) if self.planes_first else self.cut(zi, self.p.y, self.p.x)

    def each(self, d, fn):
        z = self.p.z
        if d == 0:
            fn(z, False, False)
            return

        @pl.when(z >= d)
        def _():
            fn(z - d, True, False)

        @pl.when(z + d <= 3)
        def _():
            fn(z + d, False, True)

    def start_z(self):
        p, k = self.p, self.k
        mine = self.unit(p.z)

        @pl.when(p.has_up)
        def _():
            self.send(mine, p.UP, self.zs.at[k, 0], self.zr.at[k, p.z])

        @pl.when(p.has_dn)
        def _():
            self.send(mine, p.DN, self.zs.at[k, 1], self.zr.at[k, p.z])

    def to_ab(self, zi):
        p, k = self.p, self.k
        piece = self.cut(zi, p.y, p.x)
        self.send(piece, p.A, self.as_.at[k], self.ar.at[k, zi])
        self.send(piece, p.B, self.bs.at[k], self.br.at[k, zi])

    def to_c(self, zi):
        self.send(self.plane(zi), self.p.C, self.cs.at[self.k], self.cr.at[self.k, zi])

    def own(self):
        if self.planes_first:
            self.to_ab(self.p.z)
        else:
            self.start_z()

    def zvisit(self, d):
        p, k = self.p, self.k

        def visit(zi, below, above):
            self.wait(self.unit(zi), self.zr.at[k, zi])
            if below and d < 3:
                @pl.when(p.has_up)
                def _():
                    self.send(self.unit(zi), p.UP, self.zs.at[k, 1 + d], self.zr.at[k, zi])
            if above and d < 3:
                @pl.when(p.has_dn)
                def _():
                    self.send(self.unit(zi), p.DN, self.zs.at[k, 3 + d], self.zr.at[k, zi])
            if self.planes_first:
                self.to_c(zi)
        self.each(d, visit)

    def xvisit(self, d):
        self.each(d, lambda zi, below, above: self.to_ab(zi))

    def avisit(self, d):
        p, k = self.p, self.k

        def visit(zi, below, above):
            piece = self.cut(zi, p.ya, p.xa)
            self.wait(piece, self.ar.at[k, zi])
            self.send(piece, p.B, self.bs.at[k], self.br.at[k, zi])
        self.each(d, visit)

    def bvisit(self, d):
        def visit(zi, below, above):
            self.wait(self.block(0, 2 * self.rows), self.br.at[self.k, zi])
            self.to_c(zi)
            if self.planes_first:
                self.start_z()
        self.each(d, visit)

    def cvisit(self, d):
        def visit(zi, below, above):
            self.wait(self.plane(zi, 1 - self.p.c), self.cr.at[self.k, zi])
        self.each(d, visit)

    def finish(self):
        p, k = self.p, self.k
        unit = self.block(0, (4 if self.planes_first else 1) * self.rows)
        shards = 1 if self.planes_first else 4

        def wait_if(cond, i):
            @pl.when(cond)
            def _():
                self.wait(unit, self.zs.at[k, i])

        wait_if(p.has_up, 0)
        wait_if(p.has_dn, 1)
        for d in (1, 2):
            wait_if((p.z >= d) & p.has_up, 1 + d)
            wait_if((p.z + d <= 3) & p.has_dn, 3 + d)
        self.wait(self.block(0, shards * self.rows), self.as_.at[k])
        self.wait(self.block(0, 2 * shards * self.rows), self.bs.at[k])
        self.wait(self.block(0, 16 * self.rows), self.cs.at[k])


def gather_sems(n):
    dma = pltpu.SemaphoreType.DMA
    return [dma((n, 6)), dma((n,)), dma((n,)), dma((n,)), dma((n, 4)), dma((n, 4)), dma((n, 4)), dma((n, 4))]


class Scatter:
    def __init__(self, place, k, grad, total, pass_a, pass_z, from_b, from_a, from_z, sems, credit, owed):
        self.p, self.k = place, k
        self.grad, self.total, self.pass_a, self.pass_z = grad, total, pass_a, pass_z
        self.from_b, self.from_a, self.from_dn, self.from_up = from_b, from_a, from_z, from_z
        self.sb, self.sa, self.sz, self.rb, self.ra, self.rdn, self.rup = sems
        self.credit, self.owed = credit, owed

    def send(self, src, dst, to, ssem, rsem):
        pltpu.make_async_remote_copy(
            src_ref=src, dst_ref=dst, send_sem=ssem, recv_sem=rsem, device_id=to, device_id_type=MESH).start()

    def wait(self, piece, sem):
        pltpu.make_async_copy(piece, piece, sem).wait()

    def bsend(self, zi, first):
        p, k = self.p, self.k
        if first and self.owed:
            pl.semaphore_wait(self.credit.at[1], 1)
        self.send(self.grad.at[zi, p.yb, p.xb], self.from_b.at[zi, 0], p.B, self.sb.at[k], self.rb.at[k, zi])
        self.send(self.grad.at[zi, 1 - p.y, 1 - p.x], self.from_b.at[zi, 1], p.B, self.sb.at[k], self.rb.at[k, zi])

    def bwait(self, zi, first):
        p, k = self.p, self.k
        if first and self.owed:
            pl.semaphore_wait(self.credit.at[0], 1)
        self.wait(self.from_b.at[zi], self.rb.at[k, zi])
        part = self.grad[zi, p.ya, p.xa].astype(jnp.float32) + self.from_b[zi, 1].astype(jnp.float32)
        self.pass_a[zi] = part.astype(self.pass_a.dtype)
        self.send(self.pass_a.at[zi], self.from_a.at[zi], p.A, self.sa.at[k], self.ra.at[k, zi])

    def await_(self, zi):
        p, k = self.p, self.k
        self.wait(self.from_a.at[zi], self.ra.at[k, zi])
        self.total[zi] = (self.grad[zi, p.y, p.x].astype(jnp.float32)
                          + self.from_b[zi, 0].astype(jnp.float32)
                          + self.from_a[zi].astype(jnp.float32))

    def zstep(self, tau):
        p, k = self.p, self.k
        z = p.z
        if tau == 0 and self.owed:
            @pl.when(p.has_up)
            def _():
                pl.semaphore_wait(self.credit.at[2], 1)

            @pl.when(p.has_dn)
            def _():
                pl.semaphore_wait(self.credit.at[3], 1)

        @pl.when((z <= tau) & (z < 3))
        def _():
            d = 3 - tau + z

            @pl.when(z > 0)
            def _():
                self.wait(self.from_dn.at[d], self.rdn.at[k, d])
                self.pass_z[d] = (self.total[d] + self.from_dn[d].astype(jnp.float32)).astype(self.pass_z.dtype)

            @pl.when(z == 0)
            def _():
                self.pass_z[d] = self.total[d].astype(self.pass_z.dtype)

            self.send(self.pass_z.at[d], self.from_dn.at[d], p.UP, self.sz.at[k], self.rdn.at[k, d])

        @pl.when((3 - z <= tau) & (z > 0))
        def _():
            d = tau - 3 + z

            @pl.when(z < 3)
            def _():
                self.wait(self.from_up.at[d], self.rup.at[k, d])
                self.pass_z[d] = (self.total[d] + self.from_up[d].astype(jnp.float32)).astype(self.pass_z.dtype)

            @pl.when(z == 3)
            def _():
                self.pass_z[d] = self.total[d].astype(self.pass_z.dtype)

            self.send(self.pass_z.at[d], self.from_up.at[jnp.where(d == z - 1, 4, d)], p.DN, self.sz.at[k], self.rup.at[k, d])

    def last(self):
        p, k = self.p, self.k
        z = p.z

        @pl.when(z > 0)
        def _():
            self.wait(self.from_dn.at[z], self.rdn.at[k, z])
            self.total[z] = self.total[z] + self.from_dn[z].astype(jnp.float32)

        @pl.when(z < 3)
        def _():
            self.wait(self.from_up.at[4], self.rup.at[k, z])
            self.total[z] = self.total[z] + self.from_up[4].astype(jnp.float32)

        if self.credit is not None and not self.owed:
            def free(at, to):
                pl.semaphore_signal(self.credit.at[at], inc=1, device_id=to, device_id_type=MESH)

            free(0, p.A)
            free(1, p.B)

            @pl.when(p.has_up)
            def _():
                free(3, p.UP)

            @pl.when(p.has_dn)
            def _():
                free(2, p.DN)

    def sent_b(self):
        self.wait(self.from_b, self.sb.at[self.k])

    def sent_a(self):
        self.wait(self.from_a, self.sa.at[self.k])

    def sent_z(self):
        self.wait(self.pass_z.at[pl.ds(0, 3)], self.sz.at[self.k])

    def sent(self):
        self.sent_b()
        self.sent_a()
        self.sent_z()


def scatter_sems(n):
    dma = pltpu.SemaphoreType.DMA
    return [dma((n,)), dma((n,)), dma((n,)), dma((n, 4)), dma((n, 4)), dma((n, 4)), dma((n, 4))]


def landing(shard, dtype):
    return [pltpu.VMEM(s + shard, dtype) for s in ((4, 2), (4,), (5,))]


def passing(shard, dtype):
    return [pltpu.VMEM((4, 2, 2) + shard, dtype), pltpu.VMEM((4,) + shard, jnp.float32),
            pltpu.VMEM((4,) + shard, dtype), pltpu.VMEM((4,) + shard, dtype)]


def transposed_dot(left, right):
    return lax.dot_general(left, right, (((0,), (0,)), ((), ())), preferred_element_type=F32)


def dot_transposed(left, right):
    return lax.dot_general(left, right, (((1,), (1,)), ((), ())), preferred_element_type=F32)


def dot(left, right):
    return jnp.dot(left, right, preferred_element_type=F32)


def loop(n, body):
    def step(i, carry):
        body(i)
        return carry
    lax.fori_loop(0, n, step, 0)


def gelu_both(v):
    size = jnp.abs(v) * 0.7071067811865476
    t = 1.0 / (1.0 + 0.3275911 * size)
    poly = t * (0.254829592 + t * (-0.284496736 + t * (1.421413741 + t * (-1.453152027 + t * 1.061405429))))
    bell = jnp.exp(-0.5 * v * v)
    tail = 0.5 * poly * bell
    below = jnp.where(v >= 0, 1.0 - tail, tail)
    return v * below, below + v * (bell * 0.3989422804014327)


def iota(shape, dim):
    return lax.broadcasted_iota(jnp.int32, shape, dim)


ROW = 64


def rows_at(i, n=ROW):
    return pl.ds(pl.multiple_of(i * n, n), n)


def col_at(i, n):
    return pl.ds(pl.multiple_of(i * n, 128), n)


def fold8(v):
    return jnp.sum(v.reshape(v.shape[0] // 8, 8, v.shape[1]), axis=0)


def stats(v):
    centre = jnp.mean(v, axis=-1, keepdims=True)
    centred = v - centre
    spread = jnp.mean(centred * centred, axis=-1, keepdims=True)
    return centred, lax.rsqrt(spread + EPSILON)


def layers_kernel(hid, lengths, gains_in, shifts_in, qkv_in, out_in, up_in, b_up_in, down_in, b_down_in, gout, *refs):
    (hid_out, dhid, dgain, dshift, dup, dbup, ddown, dbdown,
     sp_qkv, sp_x, sp_mid, sp_act, sp_gp, sp_nf) = refs[:14]
    refs = refs[14:]
    W = [refs[0:4], refs[4:8]]
    vec, rows_v, bup_v, sums, sbup = refs[8:13]
    X, MID, TMP, ACT, ACTP, GP, DPP, NF, NFP, G, GPN = refs[13:24]
    idc, idk, idq = refs[24:27]
    landing_sets = [refs[27:30], refs[30:33]]
    passing_sets = [refs[33:37], refs[37:41]]
    small_land, small_pass = refs[41:44], refs[44:48]
    small_from_c, small_to = refs[48:50]
    loc, swp, credit = refs[50:53]
    gsems = refs[53:61]
    ssems = refs[61:68]
    p = Place()
    c = p.c

    def local(src, dst, i):
        return pltpu.make_async_copy(src, dst, loc.at[i])

    def swap(src, dst, i):
        return pltpu.make_async_remote_copy(src_ref=src, dst_ref=dst, send_sem=swp.at[0, i], recv_sem=swp.at[1, i],
                                            device_id=p.C, device_id_type=MESH)

    def half_of(n, cc):
        return pl.ds(pl.multiple_of(cc * (n // 2), 128), n // 2)

    def stage_short():
        block = small_from_c.at[0]
        block[...] = jnp.zeros((16, 128), F32)
        b_up, b_down = b_up_in[...].astype(F32), b_down_in[...].astype(F32)
        for l in range(LAYERS):
            block[l * 8:l * 8 + 2, 0:24] = gains_in[l].astype(F32)
            block[l * 8 + 2:l * 8 + 4, 0:24] = shifts_in[l].astype(F32)
            block[l * 8 + 4:l * 8 + 5, 0:24] = b_down[l:l + 1]
            block[l * 8 + 5:l * 8 + 6, 0:96] = b_up[l:l + 1]
        vec[c, pl.ds(pl.multiple_of(p.f * 16, 16), 16)] = block[...].astype(BF)

    load_x = local(hid, G, 1)
    load_x.start()
    down_own = []
    for l in range(LAYERS):
        rows = pl.ds(pl.multiple_of(p.f * 192 + c * 96, 16), 96)
        cp = local(down_in.at[l, :, half_of(D, c)], W[l][DOWN].at[rows, half_of(D, c)], 2 + l)
        cp.start()
        down_own.append(cp)
    stage_short()
    for cc in range(2):
        @pl.when(c == cc)
        def _():
            for l in range(LAYERS):
                off = 0
                for w, n in zip((qkv_in, out_in, up_in), WIDTHS):
                    ACT[32 * l:32 * l + 24, off:off + n // 2] = w[l, :, (1 - cc) * (n // 2):(2 - cc) * (n // 2)]
                    off += n // 2
    p.barrier()
    down_swap = []
    for l in range(LAYERS):
        rows = pl.ds(pl.multiple_of(p.f * 192 + c * 96, 16), 96)
        cp = swap(down_in.at[l, :, half_of(D, 1 - c)], W[l][DOWN].at[rows, half_of(D, 1 - c)], l)
        down_swap.append(cp)
    pin_swap = []
    for l in range(LAYERS):
        cp = swap(ACT.at[pl.ds(l * 32, 32)], ACTP.at[pl.ds(l * 32, 32)], 2 + l)
        cp.start()
        pin_swap.append(cp)
    for cp in down_swap:
        cp.start()

    chunks = [Gather(p, vec, 16, 0, gsems, by_core=True)]
    for l in range(LAYERS):
        for j in range(4):
            chunks.append(Gather(p, W[l][j], 192 if j == DOWN else 48, 1 + l * 4 + j, gsems))

    def assemble(l):
        pin_swap[l].wait()
        off = 0
        for j, n in enumerate(WIDTHS):
            half = n // 2
            rows = pl.ds(pl.multiple_of(p.f * 48, 16), 48)
            for cc in range(2):
                @pl.when(c == cc)
                def _():
                    mine = (qkv_in, out_in, up_in)[j][l, :, cc * half:(cc + 1) * half]
                    other = ACTP[l * 32:l * 32 + 24, off:off + half]
                    pair = [mine, other] if cc == 0 else [other, mine]
                    W[l][j][rows, cc * half:(cc + 1) * half] = jnp.concatenate(pair, axis=0)
            off += half

    def ready(k):
        if k in (1, 2):
            assemble(k - 1)
        if k in (4, 8):
            down_own[k // 8].wait()
            down_swap[k // 8].wait()

    starts, total = [], jnp.int32(0)
    for j in range(16):
        starts.append(total)
        total = total + lengths[0, j]

    def numbers(places):
        ids = jnp.zeros(places.shape, jnp.int32)
        for s in starts:
            ids = ids + (places >= s).astype(jnp.int32)
        return ids

    def caption_numbers():
        def body(i):
            idc[rows_at(i)] = numbers(iota((ROW, 128), 0) + i * ROW)
        loop(SEQ // ROW, body)
        for i in range(4):
            idk[i] = numbers(iota((8, 256), 1) + WINDOWS[i])
            idq[i] = numbers(iota((8, 128), 1) + 128 * i)

    def unpack_vectors():
        whole = vec[...].reshape(512, 128)

        def spread(per):
            return (iota((128, D), 1) % per == iota((128, D), 0)).astype(BF)

        for l in range(LAYERS):
            for j in range(6):
                per = 96 if j == 5 else 24
                dev = iota((32, 512), 0)
                pick = iota((32, 512), 1) == (dev % 2) * 256 + (dev // 2) * 16 + (l * 8 + j)
                wide = dot(dot(pick.astype(BF), whole).astype(BF), spread(per))
                for q in range(per // 24):
                    own = iota((32, D), 0) == (iota((32, D), 1) + q * D) // per
                    line = jnp.sum(jnp.where(own, wide, 0.0), axis=0, keepdims=True)
                    if j == 5:
                        bup_v[l, 0:1, q * D:(q + 1) * D] = line
                    else:
                        rows_v[l, j:j + 1] = line

    def ln_forward(src, l, j, dst):
        def body(i):
            centred, inverse = stats(src[rows_at(i)])
            dst[rows_at(i)] = (centred * inverse * rows_v[l, j:j + 1] + rows_v[l, 2 + j:3 + j]).astype(BF)
        loop(SEQ // ROW, body)

    def first_input():
        load_x.wait()

        def body(i):
            X[rows_at(i)] = G[rows_at(i)].astype(F32)
        loop(SEQ // ROW, body)
        local(gout, G, 4).start()

    def qkv_tile(l, t):
        cols = slice(768 * t, 768 * (t + 1))
        for h in range(3):
            cc = slice(768 * t + 256 * h, 768 * t + 256 * (h + 1))
            GP[:, cc] = dot(NF[...], W[l][QKV][:, cc]).astype(BF)

    left = None

    def lanes(v, keep_left):
        lane = iota(v.shape, 1)
        return jnp.where((lane < 64) if keep_left else (lane >= 64), v, jnp.zeros_like(v))

    def stacked(v):
        return jnp.concatenate([lanes(v, True), lanes(v, False)], axis=0)

    def unstacked(v):
        top, bottom = v[:128], v[128:]
        return jnp.where(iota(top.shape, 1) < 64, top, bottom)

    def heads_pair(j):
        return [(stacked(GP[128 * i:128 * i + 128, col_at(j, 128)] * jnp.asarray(SCALE, BF)),
                 GP[WINDOWS[i]:WINDOWS[i] + 256, col_at(j + 6, 128)],
                 GP[WINDOWS[i]:WINDOWS[i] + 256, col_at(j + 12, 128)]) for i in range(4)]

    def attend(j):
        mixed = []
        for i, (q, k, v) in enumerate(heads_pair(j)):
            scores = dot_transposed(q, k)
            one = idc[128 * i:128 * i + 128]
            same = jnp.concatenate([one, one], axis=1) == idk[i, 0:1]
            same = jnp.concatenate([same, same], axis=0)
            scores = jnp.where(same, scores, -1e30)
            weights = jnp.exp(scores - jnp.max(scores, axis=1, keepdims=True))
            probs = weights * (1.0 / jnp.sum(weights, axis=1, keepdims=True))
            mixed.append(unstacked(dot(probs.astype(BF), v)).astype(BF))
        for i in range(4):
            DPP[128 * i:128 * i + 128, col_at(j, 128)] = mixed[i]

    def out_tile(l, t):
        cols = slice(256 * t, 256 * (t + 1))
        MID[:, cols] = X[:, cols] + dot(DPP[:, 0:D], W[l][OUT][:, cols])

    def up_tiles(l, first, count):
        def body(t):
            cols = col_at(t + first, 256)
            for h in range(2):
                rr = slice(256 * h, 256 * (h + 1))
                pre = dot(NF[rr], W[l][UP][:, cols]) + bup_v[l, 0:1, cols]
                act, slope = gelu_both(pre)
                ACT[rr, cols] = act.astype(BF)
                GP[rr, cols] = slope.astype(BF)
        loop(count, body)

    def down_tile(l, t):
        cols = slice(256 * t, 256 * (t + 1))
        X[:, cols] = MID[:, cols] + dot(ACT[...], W[l][DOWN][:, cols]) + rows_v[l, 4:5, cols]

    def start(src, dst, i):
        return lambda: local(src, dst, i).start()

    def forward_pieces(l):
        todo = []
        if l == 0:
            todo += [("cap", caption_numbers), ("unpack", unpack_vectors), ("first", first_input)]
            todo += [("ln", lambda: ln_forward(X, 0, 0, NF))]
        else:
            def begin():
                local(NF, sp_nf, 10).wait()
                local(GP, sp_gp, 9).wait()
                ln_forward(X, 1, 0, NF)
                local(X, sp_x, 11).start()
            todo += [("ln", begin)]
        for t in range(3):
            todo.append(("qkv", lambda t=t: qkv_tile(l, t)))
        todo.append(("spill", start(GP.at[:, 0:3 * D], sp_qkv.at[l], 5 + l)))
        for t in range(3):
            todo.append(("att", lambda t=t: loop(2, lambda j: attend(2 * t + j))))

        def middle(t):
            if l == 1 and t == 0:
                local(MID, sp_mid, 7).wait()
            out_tile(l, t)
        for t in range(3):
            todo.append(("out", lambda t=t: middle(t)))
        todo.append(("ln", lambda: ln_forward(MID, l, 1, NF)))

        def widen(zi):
            if zi == PLANES[0]:
                local(GP.at[:, 0:3 * D], sp_qkv.at[l], 5 + l).wait()
                if l == 1:
                    local(ACT, sp_act, 8).wait()
                    local(gout, G, 4).wait()
                    g_swap(1).start()
                    nf_swap(1).start()
            up_tiles(l, 3 * zi, 3)
            if l == 1:
                act_swap(1, zi).start()
        for zi in PLANES:
            todo.append(("up", lambda zi=zi: widen(zi)))
        if l == 0:
            for src, dst, i in ((MID, sp_mid, 7), (ACT, sp_act, 8), (GP, sp_gp, 9), (NF, sp_nf, 10)):
                todo.append(("spill", start(src, dst, i)))
        else:
            todo += down_blocks(1)

        def narrow(t):
            if l == 1 and t == 0:
                local(X, sp_x, 11).wait()
            down_tile(l, t)
        for t in range(3):
            todo.append(("down", lambda t=t: narrow(t)))
        if l == 1:
            todo.append(("spill", start(X, hid_out, 12)))
        return todo

    def act_swap(l, zi):
        cols = slice(D * zi, D * (zi + 1))
        return swap((sp_act, ACT)[l].at[:, cols], ACTP.at[:, cols], 8 + 4 * l + zi)

    def g_swap(l):
        return swap(G.at[:, half_of(D, 1 - c)], GPN, 4 + l)

    def nf_swap(l):
        return swap(NF, NFP, 6 + l)

    def pre_swap(l):
        return swap(GP.at[:, half_of(FF, 1 - c)], DPP, 16 + l)

    scatters = []
    for k in range(4):
        scatters.append(Scatter(p, k, *passing_sets[k % 2], *landing_sets[k % 2], ssems, credit.at[k % 2], k >= 2))
    small = Scatter(p, 4, *small_pass, *small_land, ssems, None, False)

    def down_block(l, k, zi):
        for yi in range(2):
            cols = slice(768 * zi + 384 * yi, 768 * zi + 384 * (yi + 1))
            acc = transposed_dot(ACT[:, cols], G[:, half_of(D, c)]) + transposed_dot(ACTP[:, cols], GPN[...])
            scatters[k].grad[zi, yi] = acc.astype(BF).reshape(2, 192, 384)

    def up_block(l, k, zi):
        rows = slice(192 * zi, 192 * (zi + 1))
        for t in range(3):
            cols = pl.ds(pl.multiple_of(c * (FF // 2) + 512 * t, 128), 512)
            acc = transposed_dot(NF[:, rows], GP[:, cols]) + transposed_dot(NFP[:, rows], DPP[:, 512 * t:512 * (t + 1)])
            scatters[k].grad[zi, :, :, :, 512 * t:512 * (t + 1)] = acc.astype(BF).reshape(2, 2, 48, 512)

    def out_rows(k):
        return (ddown, 96, D) if k % 2 == 0 else (dup, 24, FF)

    def deliver(k):
        s, l = scatters[k], 1 - k // 2
        s.last()
        out, n, wide = out_rows(k)
        for cc in range(2):
            @pl.when(c == cc)
            def _():
                cols = pl.ds(wide // 2 * cc, wide // 2)
                swap(s.total.at[p.z, pl.ds(n * (1 - cc), n)], out.at[l, :, cols], 18 + k).start()
                local(s.total.at[p.z, pl.ds(n * cc, n)], out.at[l, :, cols], 20 + k).start()

    def delivered(k):
        s, l = scatters[k], 1 - k // 2
        out, n, wide = out_rows(k)
        cols = pl.ds(0, wide // 2)
        cp = swap(s.total.at[0, pl.ds(0, n)], out.at[l, :, cols], 18 + k)
        cp.wait_send()
        cp.wait_recv()
        local(s.total.at[0, pl.ds(0, n)], out.at[l, :, cols], 20 + k).wait()

    def d_down_bias(l):
        acc = jnp.zeros((8, D), F32)
        for i in range(SEQ // ROW):
            acc = acc + fold8(G[i * ROW:(i + 1) * ROW].astype(F32))
        sums[l, 4] = acc

    def d_pre_tiles(l, first, count):
        def body(t):
            cols = col_at(t + first, 256)
            rows = pl.ds(pl.multiple_of((t + first) * 256, 256), 256)
            acc = jnp.zeros((8, 256), F32)
            for h in range(2):
                rr = slice(256 * h, 256 * (h + 1))
                d = (dot_transposed(G[rr], W[l][DOWN][rows]) * GP[rr, cols].astype(F32)).astype(BF)
                GP[rr, cols] = d
                acc = acc + fold8(d.astype(F32))
            sbup[l, :, cols] = acc
        loop(count, body)

    def d_normed_f_tile(l, t):
        TMP[:, 256 * t:256 * (t + 1)] = dot_transposed(GP[...], W[l][UP][256 * t:256 * (t + 1)])

    def ln_backward(src, grad, add, l, j, dst, low, convert=None):
        sums[l, j] = jnp.zeros((8, D), F32)
        sums[l, 2 + j] = jnp.zeros((8, D), F32)

        def body(i):
            rr = rows_at(i)
            centred, inverse = stats(src[rr].astype(F32))
            unit = centred * inverse
            d = grad[rr]
            sums[l, j] += fold8(d * unit)
            sums[l, 2 + j] += fold8(d)
            scaled = d * rows_v[l, j:j + 1]
            mean_d = jnp.mean(scaled, axis=-1, keepdims=True)
            mean_u = jnp.mean(scaled * unit, axis=-1, keepdims=True)
            result = add[rr].astype(F32) + inverse * (scaled - mean_d - unit * mean_u)
            dst[rr] = result
            if low is not None:
                low[rr, 0:D] = result.astype(BF)
        loop(SEQ // ROW, body)

    def d_mixed_tile(l, t):
        ACT[:, 3 * D + 256 * t:3 * D + 256 * (t + 1)] = dot_transposed(ACT[:, 0:D], W[l][OUT][256 * t:256 * (t + 1)]).astype(BF)

    def attend_back(j):
        d_q, d_k, d_v = [], [], []
        d_out = [stacked(ACT[128 * i:128 * i + 128, col_at(j + 18, 128)]) for i in range(4)]
        for i, (q, k, v) in enumerate(heads_pair(j)):
            w = WINDOWS[i]
            scores = dot_transposed(k, q)
            same = idc[w:w + 256] == idq[i, 0:1]
            same = jnp.concatenate([same, same], axis=1)
            scores = jnp.where(same, scores, -1e30)
            weights = jnp.exp(scores - jnp.max(scores, axis=0, keepdims=True))
            probs = weights * (1.0 / jnp.sum(weights, axis=0, keepdims=True))
            d_v.append(dot(probs.astype(BF), d_out[i]))
            d_probs = dot_transposed(v, d_out[i])
            centre = jnp.sum(d_probs * probs, axis=0, keepdims=True)
            d_scores = (probs * (d_probs - centre)).astype(BF)
            d_k.append(dot(d_scores, q))
            d_q.append((unstacked(transposed_dot(d_scores, k)) * SCALE).astype(BF))

        def joined(parts):
            rows = []
            for b in range(8):
                held = [parts[i][64 * b - WINDOWS[i]:64 * b - WINDOWS[i] + 64] for i in range(4)
                        if 0 <= 64 * b - WINDOWS[i] < 256]
                rows.append(sum(held[1:], held[0]))
            return jnp.concatenate(rows, axis=0).astype(BF)

        for i in range(4):
            ACT[128 * i:128 * i + 128, col_at(j, 128)] = d_q[i]
        ACT[:, col_at(j + 6, 128)] = joined(d_k)
        ACT[:, col_at(j + 12, 128)] = joined(d_v)

    def d_normed_a_tile(l, t):
        TMP[:, 256 * t:256 * (t + 1)] = dot_transposed(ACT[:, 0:3 * D], W[l][QKV][256 * t:256 * (t + 1)])

    def pack_small(late):
        def spread(per):
            return (iota((D, 128), 0) % per == iota((D, 128), 1)).astype(F32)

        for l in range(LAYERS):
            for j in range(6):
                if (l == 0 and j in (0, 2)) != late:
                    continue
                per = 96 if j == 5 else 24
                dev = iota((32, D), 0)
                number = (dev % 16) * 2 + dev // 16
                picked = jnp.zeros((32, D), F32)
                for q in range(per // 24):
                    full = sbup[l, :, q * D:(q + 1) * D] if j == 5 else sums[l, j]
                    line = jnp.sum(full, axis=0, keepdims=True)
                    own = number == (iota((32, D), 1) + q * D) // per
                    picked = picked + jnp.where(own, line, 0.0)
                part = jnp.dot(picked, spread(per), precision=lax.Precision.HIGHEST, preferred_element_type=F32)
                small_to[:, :, l * 8 + j, :] = part.reshape(2, 16, 128)

    def gradient_block(k, zi, fn):
        l = 1 - k // 2
        first = zi == PLANES[0]
        if k % 2 == 0:
            act_swap(l, zi).wait_recv()
        if first:
            for cp in ([g_swap(l)], [nf_swap(l), pre_swap(l)])[k % 2]:
                cp.wait_recv()
            if k >= 2:
                scatters[k - 2].sent()
                delivered(k - 2)
        fn(l, k, zi)
        scatters[k].bsend(zi, first)

    def down_blocks(l):
        k = 2 * (1 - l)
        return [("dbias", lambda: d_down_bias(l))] + [("ddown", lambda zi=zi: gradient_block(k, zi, down_block)) for zi in PLANES]

    def up_blocks(l):
        k = 2 * (1 - l) + 1
        return [("dup", lambda zi=zi: gradient_block(k, zi, up_block)) for zi in PLANES]

    def backward_pieces(l):
        todo = []
        if l == 0:
            def begin():
                g_swap(0).start()
                for src, dst, i in ((sp_act, ACT, 19), (sp_gp, GP, 18), (sp_nf, NF, 17), (sp_mid, MID, 24)):
                    local(src, dst, i).wait()
            todo += [("sendg", begin)] + down_blocks(0)
        todo += [("dpre", lambda t=t: d_pre_tiles(l, (1 - c) * 6 + 2 * t, 2)) for t in range(3)]

        def send_pre():
            if l == 0:
                nf_swap(0).start()
            pre_swap(l).start()
        todo.append(("sendpre", send_pre))
        todo += [("dpre", lambda t=t: d_pre_tiles(l, c * 6 + 2 * t, 2)) for t in range(3)]
        todo += [("dnf", lambda t=t: d_normed_f_tile(l, t)) for t in range(3)]
        todo += up_blocks(l)
        if l == 1:
            def send_act():
                for zi in PLANES:
                    act_swap(0, zi).start()
            todo.append(("sendact", send_act))

        def at_middle():
            for cp in [g_swap(l), nf_swap(l), pre_swap(l)] + [act_swap(l, zi) for zi in PLANES]:
                cp.wait_send()
            local(sp_qkv.at[l], GP.at[:, 0:3 * D], 13 + l).start()
            if l == 1:
                local(X, hid_out, 12).wait()
                local(sp_x, X, 15).start()
                local(sp_nf, NF, 17).start()
            else:
                local(hid, NF, 16).start()
            ln_backward(MID, TMP, G if l == 1 else X, l, 1, MID, ACT)
        todo.append(("lnb", at_middle))
        todo += [("dmix", lambda t=t: d_mixed_tile(l, t)) for t in range(3)]

        def attention_back(t):
            if t == 0:
                local(sp_qkv.at[l], GP.at[:, 0:3 * D], 13 + l).wait()
            loop(2, lambda i: attend_back(2 * t + i))
            if l == 1 and t == 2:
                local(sp_gp, GP, 18).start()
        todo += [("attb", lambda t=t: attention_back(t)) for t in range(3)]
        todo += [("dna", lambda t=t: d_normed_a_tile(l, t)) for t in range(3)]
        if l == 0:
            todo.append(("prepack", lambda: pack_small(False)))

        def at_input():
            if l == 1:
                local(sp_act, ACT, 19).start()
                local(sp_x, X, 15).wait()
                ln_backward(X, TMP, MID, l, 0, X, G)
                local(sp_mid, MID, 24).start()
            else:
                local(hid, NF, 16).wait()
                ln_backward(NF, TMP, MID, l, 0, X, None)
                local(X, dhid, 25).start()
        todo.append(("lnb", at_input))
        return todo

    small_swap = swap(small_to.at[1 - c], small_from_c, 22)

    def pack():
        pack_small(True)
        small_swap.start()

    def send_small():
        small_swap.wait()
        small.grad[...] = (small_to[c] + small_from_c[...]).reshape(ZS, YS, XS, 16, 128)
        for zi in range(4):
            small.bsend(zi, False)

    def finish_small():
        small.last()
        for l in range(LAYERS):
            dgain[l] = small.total[p.z, l * 8:l * 8 + 2, 0:24]
            dshift[l] = small.total[p.z, l * 8 + 2:l * 8 + 4, 0:24]
            dbdown[l:l + 1] = small.total[p.z, l * 8 + 4:l * 8 + 5, 0:24]
            dbup[l:l + 1] = small.total[p.z, l * 8 + 5:l * 8 + 6, 0:96]

    pieces = forward_pieces(0) + forward_pieces(1) + backward_pieces(1) + backward_pieces(0)
    pieces += [("pack", pack), ("small", send_small)]
    sums_of = scatters + [small]
    begun = set()

    def first_wait(k, zi):
        sums_of[k].bwait(zi, k not in begun)
        begun.add(k)

    def start_chunk(k, _):
        ready(k)
        chunks[k].own()

    steps = (
        start_chunk,
        lambda k, d: chunks[k].zvisit(d),
        lambda k, d: chunks[k].xvisit(d),
        lambda k, d: chunks[k].avisit(d),
        lambda k, d: chunks[k].bvisit(d),
        lambda k, d: chunks[k].cvisit(d),
        first_wait,
        lambda k, zi: sums_of[k].await_(zi),
        lambda k, tau: sums_of[k].zstep(tau),
        lambda k, _: finish_small() if k == 4 else deliver(k),
        lambda i, j: pieces[10 * i + j][1](),
    )
    for code in ORDER:
        steps[code // 1000](code // 10 % 100, code % 10)
    for ch in chunks:
        ch.finish()
    small.sent()
    for k in (2, 3):
        scatters[k].sent()
        delivered(k)
    local(X, dhid, 25).wait()


ORDER = (
    0, 10, 2000, 2010, 20, 1001, 30, 2001, 3000, 2020, 2030, 3010, 1011, 3001, 4000, 3020,
    1021, 1002, 2002, 5000, 3030, 1031, 4010, 4001, 3002, 2011, 4020, 40, 50, 1012, 1022, 1003,
    2003, 2012, 4002, 5001, 5010, 5020, 4030, 5002, 1032, 5030, 3011, 3003, 1041, 3050, 1013, 4003,
    2013, 2021, 2022, 1023, 2023, 2031, 5003, 10000, 10001, 3012, 3013, 1033, 10002, 10003, 3023, 4011,
    60, 1042, 4050, 3021, 2032, 3022, 5011, 5050, 1043, 4013, 4023, 1061, 5013, 5023, 3031, 4012,
    2033, 2040, 4021, 3032, 5012, 10004, 70, 5021, 2041, 10005, 4022, 10006, 3033, 10007, 80, 10008,
    5022, 4031, 2042, 3040, 1051, 1062, 10009, 4032, 5031, 1071, 10010, 5032, 2043, 5051, 2060, 1081,
    10011, 3041, 10012, 10013, 4033, 10014, 2061, 2062, 3042, 5033, 10015, 10016, 4040, 10017, 3043, 1052,
    1063, 2063, 2070, 3060, 10018, 5040, 5052, 2071, 4041, 1072, 3061, 10019, 10020, 10021, 10022, 3062,
    4042, 5041, 1082, 4043, 3063, 3070, 5043, 5042, 10023, 2072, 10024, 4060, 10025, 10026, 5060, 1053,
    4063, 3071, 5053, 10027, 5063, 1073, 10028, 2073, 2080, 10029, 4061, 4062, 10030, 10031, 5061, 5062,
    3072, 3073, 4070, 1083, 2081, 10032, 5070, 10033, 4071, 2082, 3080, 10034, 10035, 10036, 10037, 4073,
    4072, 5071, 5073, 5072, 2083, 10038, 10039, 3081, 10040, 3083, 10041, 3082, 10042, 10043, 4080, 10044,
    4083, 10045, 5080, 10046, 4081, 5083, 4082, 5081, 6003, 5082, 10047, 10048, 10049, 6000, 10050, 10051,
    10052, 10053, 6002, 10054, 10055, 10056, 10057, 6001, 10058, 7003, 10059, 10060, 7000, 8000, 10061, 7002,
    10062, 7001, 10063, 10064, 10065, 10066, 8001, 6013, 10067, 10068, 6010, 10069, 10070, 8002, 6012, 10071,
    7013, 7010, 6011, 9000, 7012, 8010, 10072, 7011, 10073, 10074, 8011, 10075, 10076, 10077, 10078, 8012,
    10079, 10080, 10081, 10082, 9010, 10083, 6023, 10084, 10085, 10086, 10087, 6020, 10088, 10089, 10090, 6022,
    10091, 10092, 10093, 6021, 10094, 7023, 10095, 10096, 7020, 8020, 10097, 7022, 10098, 10099, 6033, 10100,
    10101, 7021, 8021, 6030, 10102, 6032, 10103, 8022, 7033, 7030, 7032, 6031, 8030, 10104, 10105, 10106,
    10107, 9020, 7031, 10108, 8031, 10109, 10110, 6040, 6041, 6042, 6043, 8032, 7040, 7041, 7042, 7043,
    8040, 9030, 8041, 8042, 9040,
)
PLANES_FIRST = (5,)
WINDOWS = (0, 64, 192, 256)


def layers_on_slice(hidden_in, caption_lengths, norm_gain, norm_bias, qkv_weight, out_weight, up_weight, up_bias, down_weight, down_bias, grad_out):
    shape = jax.ShapeDtypeStruct
    vm, hbm, sm = [pl.BlockSpec(memory_space=s) for s in (pltpu.VMEM, pl.ANY, pltpu.SMEM)]
    outs = [
        (shape((SEQ, D), F32), hbm), (shape((SEQ, D), F32), hbm),
        (shape((2, 2, 24), F32), vm), (shape((2, 2, 24), F32), vm),
        (shape((2, 24, FF), F32), hbm), (shape((2, 96), F32), vm),
        (shape((2, 96, D), F32), hbm), (shape((2, 24), F32), vm),
        (shape((2, SEQ, 3 * D), BF), hbm), (shape((SEQ, D), F32), hbm), (shape((SEQ, D), F32), hbm),
        (shape((SEQ, FF), BF), hbm), (shape((SEQ, FF), BF), hbm), (shape((SEQ, D), BF), hbm),
    ]
    v = pltpu.VMEM
    scratch = []
    for l in range(LAYERS):
        scratch += [v((D, 3 * D), BF), v((D, D), BF), v((D, FF), BF), v((FF, D), BF)]
    scratch += [v((2, 256, 128), BF), v((2, 8, D), F32), v((2, 1, FF), F32), v((2, 5, 8, D), F32), v((2, 8, FF), F32)]
    scratch += [v((SEQ, D), F32)] * 3
    scratch += [v((SEQ, FF), BF)] * 3
    scratch += [v((SEQ, FF // 2), BF), v((SEQ, D), BF), v((SEQ, D), BF), v((SEQ, D), BF), v((SEQ, D // 2), BF)]
    scratch += [v((SEQ, 128), jnp.int32), v((4, 8, 256), jnp.int32), v((4, 8, 128), jnp.int32)]
    scratch += landing(DOWN_SHARD, BF) + landing(UP_SHARD, BF)
    scratch += passing(DOWN_SHARD, BF) + passing(UP_SHARD, BF)
    scratch += landing(SMALL_SHARD, F32) + passing(SMALL_SHARD, F32)
    scratch += [v((16, 16, 128), F32), v((2, 16, 16, 128), F32)]
    scratch += [pltpu.SemaphoreType.DMA((26,)), pltpu.SemaphoreType.DMA((2, 23)), pltpu.SemaphoreType.REGULAR((2, 4))]
    scratch += gather_sems(9) + scatter_sems(5)
    got = pl.pallas_call(
        layers_kernel,
        out_shape=[o[0] for o in outs],
        in_specs=[hbm, sm, vm, vm, vm, vm, vm, vm, hbm, vm, hbm],
        out_specs=[o[1] for o in outs],
        scratch_shapes=scratch,
        compiler_params=pltpu.CompilerParams(collective_id=0, has_side_effects=True, vmem_limit_bytes=VMEM_LIMIT),
    )(hidden_in, caption_lengths, norm_gain, norm_bias, qkv_weight, out_weight, up_weight, up_bias, down_weight,
      down_bias, grad_out)
    return tuple(got[:8])


VMEM_LIMIT = 64 * 2**20


def solution(mesh):
    in_specs = (
        P(("fsdp", "rep"), None),
        P(("fsdp", "rep"), None),
        P(None, None, ("fsdp", "rep")),
        P(None, None, ("fsdp", "rep")),
        P(None, ("fsdp", "rep"), None),
        P(None, ("fsdp", "rep"), None),
        P(None, ("fsdp", "rep"), None),
        P(None, ("fsdp", "rep")),
        P(None, ("fsdp", "rep"), None),
        P(None, ("fsdp", "rep")),
        P(("fsdp", "rep"), None),
    )
    out_specs = (
        P(("fsdp", "rep"), None),
        P(("fsdp", "rep"), None),
        P(None, None, ("fsdp", "rep")),
        P(None, None, ("fsdp", "rep")),
        P(None, ("fsdp", "rep"), None),
        P(None, ("fsdp", "rep")),
        P(None, ("fsdp", "rep"), None),
        P(None, ("fsdp", "rep")),
    )
    near = dict(mesh.shape) == {"fsdp": 16, "rep": 2}
    return jax.shard_map(
        layers_on_slice if near else per_device, mesh=mesh, in_specs=in_specs, out_specs=out_specs, check_vma=False
    )
```

```python
import jax
import jax.numpy as jnp
from jax import lax
from jax.sharding import PartitionSpec as P
from jax.experimental import pallas as pl
from jax.experimental.pallas import tpu as pltpu

D = 768
FF = 3072
HEADS = 12
SEQ = 512
LAYERS = 2


EPSILON = 1e-05
SCALE = 0.125


def layer_norm(values, gain, shift):
    centre = jnp.mean(values, axis=-1, keepdims=True)
    centred = values - centre
    spread = jnp.mean(centred * centred, axis=-1, keepdims=True)
    return centred * lax.rsqrt(spread + EPSILON) * gain + shift


def exact_gelu(values):
    return jax.nn.gelu(values, approximate=False)


def caption_ids(lengths):
    starts = jnp.cumsum(lengths, axis=-1) - lengths
    places = jnp.arange(SEQ, dtype=jnp.int32)
    passed = (places[None, :, None] >= starts[:, None, :]).astype(jnp.int32)
    return jnp.sum(passed, axis=-1) - 1


def transposed_left(left, right):
    return lax.dot_general(
        left, right, (((0,), (0,)), ((), ())), preferred_element_type=jnp.float32
    )


def transposed_right(left, right):
    return lax.dot_general(
        left, right, (((1,), (1,)), ((), ())), preferred_element_type=jnp.float32
    )


def split_heads(packed):
    width = D // HEADS
    queries = packed[:, :D].reshape(SEQ, HEADS, width)
    keys_part = packed[:, D : 2 * D].reshape(SEQ, HEADS, width)
    values_part = packed[:, 2 * D :].reshape(SEQ, HEADS, width)
    return (queries, keys_part, values_part)


def masked_scores(queries, keys_part, caption):
    scores = (
        jnp.einsum("qhd,khd->hqk", queries, keys_part, preferred_element_type=jnp.float32) * SCALE
    )
    same = caption[:, None] == caption[None, :]
    return jnp.where(same[None], scores, -1e30)


def attend_row(inputs):
    packed, caption = inputs
    queries, keys_part, values_part = split_heads(packed)
    scores = masked_scores(queries, keys_part, caption)
    highest = jnp.max(scores, axis=-1, keepdims=True)
    weights = jnp.exp(scores - highest)
    totals = jnp.sum(weights, axis=-1, keepdims=True)
    probs = (weights / totals).astype(jnp.bfloat16)
    mixed = jnp.einsum("hqk,khd->qhd", probs, values_part, preferred_element_type=jnp.float32)
    return (mixed.reshape(SEQ, D), highest + jnp.log(totals))


def attend_back(inputs):
    packed, caption, logsum, d_mixed = inputs
    queries, keys_part, values_part = split_heads(packed)
    probs = jnp.exp(masked_scores(queries, keys_part, caption) - logsum)
    d_heads = d_mixed.reshape(SEQ, HEADS, D // HEADS)
    d_values = jnp.einsum(
        "hqk,qhd->khd", probs.astype(jnp.bfloat16), d_heads, preferred_element_type=jnp.float32
    )
    d_probs = jnp.einsum("qhd,khd->hqk", d_heads, values_part, preferred_element_type=jnp.float32)
    centre = jnp.sum(d_probs * probs, axis=-1, keepdims=True)
    d_scores = (probs * (d_probs - centre)).astype(jnp.bfloat16)
    d_queries = (
        jnp.einsum("hqk,khd->qhd", d_scores, keys_part, preferred_element_type=jnp.float32) * SCALE
    )
    d_keys = (
        jnp.einsum("hqk,qhd->khd", d_scores, queries, preferred_element_type=jnp.float32) * SCALE
    )
    joined = jnp.concatenate(
        [d_queries.reshape(SEQ, D), d_keys.reshape(SEQ, D), d_values.reshape(SEQ, D)], axis=1
    )
    return joined.astype(jnp.bfloat16)


def fetch_forward(w_qkv, w_out, w_up, w_down, gains, shifts, b_up, b_down):
    return (
        lax.all_gather(w_qkv, ("fsdp", "rep"), axis=0, tiled=True),
        lax.all_gather(w_out, ("fsdp", "rep"), axis=0, tiled=True),
        lax.all_gather(w_up, ("fsdp", "rep"), axis=0, tiled=True),
        lax.all_gather(w_down, ("fsdp", "rep"), axis=0, tiled=True),
        lax.all_gather(gains, ("fsdp", "rep"), axis=1, tiled=True),
        lax.all_gather(shifts, ("fsdp", "rep"), axis=1, tiled=True),
        lax.all_gather(b_up, ("fsdp", "rep"), axis=0, tiled=True),
        lax.all_gather(b_down, ("fsdp", "rep"), axis=0, tiled=True),
    )


def fetch_backward(w_qkv, w_out, w_up, w_down, gains, shifts):
    return (
        lax.all_gather(w_qkv, ("fsdp", "rep"), axis=0, tiled=True),
        lax.all_gather(w_out, ("fsdp", "rep"), axis=0, tiled=True),
        lax.all_gather(w_up, ("fsdp", "rep"), axis=0, tiled=True),
        lax.all_gather(w_down, ("fsdp", "rep"), axis=0, tiled=True),
        lax.all_gather(gains, ("fsdp", "rep"), axis=1, tiled=True),
        lax.all_gather(shifts, ("fsdp", "rep"), axis=1, tiled=True),
    )


def owner_major(matrix, owners):
    width = matrix.shape[1] // owners
    return matrix.reshape(matrix.shape[0], owners, width).transpose(1, 0, 2).reshape(owners, -1)


def settle(d_up, d_down, d_gains, d_shifts, d_bup, d_bdown):
    owners = lax.axis_size("fsdp") * lax.axis_size("rep")
    members = [
        d_up.reshape(owners, -1),
        d_down.reshape(owners, -1),
        owner_major(d_gains, owners),
        owner_major(d_shifts, owners),
        d_bup.reshape(owners, -1),
        d_bdown.reshape(owners, -1),
    ]
    flat = jnp.concatenate(members, axis=1)
    mine = lax.psum_scatter(flat, ("fsdp", "rep"), scatter_dimension=0, tiled=True)
    mine = mine.reshape(-1)
    up_rows = D // owners
    down_rows = FF // owners
    norm_cols = D // owners
    sizes = [up_rows * FF, down_rows * D, 2 * norm_cols, 2 * norm_cols, down_rows, norm_cols]
    pieces = []
    begin = 0
    for length in sizes:
        pieces.append(mine[begin : begin + length])
        begin = begin + length
    return (
        pieces[0].reshape(up_rows, FF),
        pieces[1].reshape(down_rows, D),
        pieces[2].reshape(2, norm_cols),
        pieces[3].reshape(2, norm_cols),
        pieces[4],
        pieces[5],
    )


def per_device(
    hidden_in,
    caption_lengths,
    norm_gain,
    norm_bias,
    qkv_weight,
    out_weight,
    up_weight,
    up_bias,
    down_weight,
    down_bias,
    grad_out,
):
    row_count = caption_lengths.shape[0]
    captions = caption_ids(caption_lengths)
    hidden = hidden_in.astype(jnp.float32)
    stored = []
    for layer_number in range(LAYERS):
        fetched = fetch_forward(
            qkv_weight[layer_number],
            out_weight[layer_number],
            up_weight[layer_number],
            down_weight[layer_number],
            norm_gain[layer_number],
            norm_bias[layer_number],
            up_bias[layer_number],
            down_bias[layer_number],
        )
        w_qkv, w_out, w_up, w_down, gains, shifts, b_up, b_down = fetched
        gains_full = gains.astype(jnp.float32)
        shifts_full = shifts.astype(jnp.float32)
        normed_a = layer_norm(hidden, gains_full[0], shifts_full[0]).astype(jnp.bfloat16)
        packed = jnp.dot(normed_a, w_qkv, preferred_element_type=jnp.float32).astype(jnp.bfloat16)
        mixed, logsum = lax.map(attend_row, (packed.reshape(row_count, SEQ, 3 * D), captions))
        mixed = mixed.reshape(-1, D).astype(jnp.bfloat16)
        middle = hidden + jnp.dot(mixed, w_out, preferred_element_type=jnp.float32)
        normed_f = layer_norm(middle, gains_full[1], shifts_full[1]).astype(jnp.bfloat16)
        preact = jnp.dot(normed_f, w_up, preferred_element_type=jnp.float32) + b_up.astype(
            jnp.float32
        )
        active = exact_gelu(preact).astype(jnp.bfloat16)
        output = (
            middle
            + jnp.dot(active, w_down, preferred_element_type=jnp.float32)
            + b_down.astype(jnp.float32)
        )
        weights_kept = None
        stored.append((hidden, packed, logsum, middle, normed_f, preact, active, weights_kept))
        hidden = output
    gradient = grad_out.astype(jnp.float32)
    settled = [None] * LAYERS
    for layer_number in reversed(range(LAYERS)):
        layer_in, packed, logsum, middle, normed_f, preact, active, weights_kept = stored[
            layer_number
        ]
        fetched = fetch_backward(
            qkv_weight[layer_number],
            out_weight[layer_number],
            up_weight[layer_number],
            down_weight[layer_number],
            norm_gain[layer_number],
            norm_bias[layer_number],
        )
        w_qkv, w_out, w_up, w_down, gains, shifts = fetched
        gains_full = gains.astype(jnp.float32)
        shifts_full = shifts.astype(jnp.float32)
        grad_low = gradient.astype(jnp.bfloat16)
        d_bdown = jnp.sum(grad_low.astype(jnp.float32), axis=0)
        d_down = transposed_left(active, grad_low)
        d_active = transposed_right(grad_low, w_down)
        gelu_value, gelu_back = jax.vjp(exact_gelu, preact)
        d_preact = gelu_back(d_active)[0].astype(jnp.bfloat16)
        d_bup = jnp.sum(d_preact.astype(jnp.float32), axis=0)
        d_up = transposed_left(normed_f, d_preact)
        d_normed_f = transposed_right(d_preact, w_up)
        norm_value, norm_back = jax.vjp(layer_norm, middle, gains_full[1], shifts_full[1])
        d_middle_ln, d_gain_f, d_shift_f = norm_back(d_normed_f)
        d_middle = gradient + d_middle_ln
        d_mixed = transposed_right(d_middle.astype(jnp.bfloat16), w_out).astype(jnp.bfloat16)
        d_packed = lax.map(
            attend_back,
            (
                packed.reshape(row_count, SEQ, 3 * D),
                captions,
                logsum,
                d_mixed.reshape(row_count, SEQ, D),
            ),
        )
        d_normed_a = transposed_right(d_packed.reshape(-1, 3 * D), w_qkv)
        first_value, first_back = jax.vjp(layer_norm, layer_in, gains_full[0], shifts_full[0])
        d_input_ln, d_gain_a, d_shift_a = first_back(d_normed_a)
        gradient = d_middle + d_input_ln
        settled[layer_number] = settle(
            d_up,
            d_down,
            jnp.stack([d_gain_a, d_gain_f]),
            jnp.stack([d_shift_a, d_shift_f]),
            d_bup,
            d_bdown,
        )
    d_gains = jnp.stack([settled[number][2] for number in range(LAYERS)])
    d_shifts = jnp.stack([settled[number][3] for number in range(LAYERS)])
    d_up_all = jnp.stack([settled[number][0] for number in range(LAYERS)])
    d_bup_all = jnp.stack([settled[number][4] for number in range(LAYERS)])
    d_down_all = jnp.stack([settled[number][1] for number in range(LAYERS)])
    d_bdown_all = jnp.stack([settled[number][5] for number in range(LAYERS)])
    return (hidden, gradient, d_gains, d_shifts, d_up_all, d_bup_all, d_down_all, d_bdown_all)


MESH = pl.DeviceIdType.MESH
BF, F32 = jnp.bfloat16, jnp.float32
ZS, YS, XS = 4, 2, 2
QKV, OUT, UP, DOWN = range(4)
WIDTHS = (3 * D, D, FF)
HALF = sum(WIDTHS) // 2
PLANES = (3, 0, 2, 1)
UP_SHARD = (48, FF // 2)
DOWN_SHARD = (192, D // 2)
SMALL_SHARD = (16, 128)


class Place:
    def __init__(self):
        f = lax.axis_index("fsdp")
        c = lax.axis_index("rep")
        self.f, self.c = f, c
        self.x = f % 2
        self.y = (f // 2) % 2
        self.z = f // 4
        fx = f + 1 - 2 * self.x
        fy = f + 2 - 4 * self.y
        self.fa = fx + c * (fy - fx)
        self.fb = fy + c * (fx - fy)
        self.ya = (self.fa // 2) % 2
        self.xa = self.fa % 2
        self.yb = (self.fb // 2) % 2
        self.xb = self.fb % 2
        self.A = (self.fa, c)
        self.B = (self.fb, c)
        self.C = (f, 1 - c)
        self.UP = (f + 4, c)
        self.DN = (f - 4, c)
        self.has_up = self.z < 3
        self.has_dn = self.z > 0

    def barrier(self):
        bar = pltpu.get_barrier_semaphore()
        others = [self.A, self.B, self.C] + [self.column((self.z + hop) % 4) for hop in (1, 2, 3)]
        for d in others:
            pl.semaphore_signal(bar, inc=1, device_id=d, device_id_type=MESH)

    def met(self):
        pl.semaphore_wait(pltpu.get_barrier_semaphore(), 6)

    def column(self, zi):
        return (zi * 4 + self.f % 4, self.c)


class Gather:
    def __init__(self, place, ref, rows, k, sems, by_core=False):
        self.p, self.ref, self.rows, self.k, self.by_core = place, ref, rows, k, by_core
        self.planes_first = k in PLANES_FIRST
        (self.zs, self.as_, self.bs, self.cs, self.zr, self.ar, self.br, self.cr) = sems

    def block(self, start, rows, c=None):
        c = self.p.c if c is None else c
        if self.by_core:
            return self.ref.at[c, pl.ds(start, rows)]
        half = self.ref.shape[-1] // 2
        return self.ref.at[pl.ds(start, rows), pl.ds(pl.multiple_of(c * half, 128), half)]

    def cut(self, zi, yi, xi):
        return self.block(pl.multiple_of((zi * 4 + yi * 2 + xi) * self.rows, 16), self.rows)

    def plane(self, zi, c=None):
        return self.block(pl.multiple_of(zi * 4 * self.rows, 16), 4 * self.rows, c)

    def send(self, piece, to, ssem, rsem):
        pltpu.make_async_remote_copy(
            src_ref=piece, dst_ref=piece, send_sem=ssem, recv_sem=rsem, device_id=to, device_id_type=MESH).start()

    def wait(self, piece, sem):
        pltpu.make_async_copy(piece, piece, sem).wait()

    def unit(self, zi):
        return self.plane(zi) if self.planes_first else self.cut(zi, self.p.y, self.p.x)

    def each(self, d, fn):
        z = self.p.z
        if d == 0:
            fn(z, False, False)
            return

        @pl.when(z >= d)
        def _():
            fn(z - d, True, False)

        @pl.when(z + d <= 3)
        def _():
            fn(z + d, False, True)

    def start_z(self):
        p, k = self.p, self.k
        mine = self.unit(p.z)

        @pl.when(p.has_up)
        def _():
            self.send(mine, p.UP, self.zs.at[k, 0], self.zr.at[k, p.z])

        @pl.when(p.has_dn)
        def _():
            self.send(mine, p.DN, self.zs.at[k, 1], self.zr.at[k, p.z])

    def to_ab(self, zi):
        p, k = self.p, self.k
        piece = self.cut(zi, p.y, p.x)
        self.send(piece, p.A, self.as_.at[k], self.ar.at[k, zi])
        self.send(piece, p.B, self.bs.at[k], self.br.at[k, zi])

    def to_c(self, zi):
        self.send(self.plane(zi), self.p.C, self.cs.at[self.k], self.cr.at[self.k, zi])

    def own(self):
        if self.planes_first:
            self.to_ab(self.p.z)
        else:
            self.start_z()

    def zvisit(self, d):
        p, k = self.p, self.k

        def visit(zi, below, above):
            self.wait(self.unit(zi), self.zr.at[k, zi])
            if below and d < 3:
                @pl.when(p.has_up)
                def _():
                    self.send(self.unit(zi), p.UP, self.zs.at[k, 1 + d], self.zr.at[k, zi])
            if above and d < 3:
                @pl.when(p.has_dn)
                def _():
                    self.send(self.unit(zi), p.DN, self.zs.at[k, 3 + d], self.zr.at[k, zi])
            if self.planes_first:
                self.to_c(zi)
        self.each(d, visit)

    def xvisit(self, d):
        self.each(d, lambda zi, below, above: self.to_ab(zi))

    def avisit(self, d):
        p, k = self.p, self.k

        def visit(zi, below, above):
            piece = self.cut(zi, p.ya, p.xa)
            self.wait(piece, self.ar.at[k, zi])
            self.send(piece, p.B, self.bs.at[k], self.br.at[k, zi])
        self.each(d, visit)

    def bvisit(self, d):
        def visit(zi, below, above):
            self.wait(self.block(0, 2 * self.rows), self.br.at[self.k, zi])
            self.to_c(zi)
            if self.planes_first:
                self.start_z()
        self.each(d, visit)

    def cvisit(self, d):
        def visit(zi, below, above):
            self.wait(self.plane(zi, 1 - self.p.c), self.cr.at[self.k, zi])
        self.each(d, visit)

    def finish(self):
        p, k = self.p, self.k
        unit = self.block(0, (4 if self.planes_first else 1) * self.rows)
        shards = 1 if self.planes_first else 4

        def wait_if(cond, i):
            @pl.when(cond)
            def _():
                self.wait(unit, self.zs.at[k, i])

        wait_if(p.has_up, 0)
        wait_if(p.has_dn, 1)
        for d in (1, 2):
            wait_if((p.z >= d) & p.has_up, 1 + d)
            wait_if((p.z + d <= 3) & p.has_dn, 3 + d)
        self.wait(self.block(0, shards * self.rows), self.as_.at[k])
        self.wait(self.block(0, 2 * shards * self.rows), self.bs.at[k])
        self.wait(self.block(0, 16 * self.rows), self.cs.at[k])


def gather_sems(n):
    dma = pltpu.SemaphoreType.DMA
    return [dma((n, 6)), dma((n,)), dma((n,)), dma((n,)), dma((n, 4)), dma((n, 4)), dma((n, 4)), dma((n, 4))]


class Scatter:
    def __init__(self, place, k, grad, total, pass_a, pass_z, from_b, from_a, from_z, sems, credit, owed):
        self.p, self.k = place, k
        self.grad, self.total, self.pass_a, self.pass_z = grad, total, pass_a, pass_z
        self.from_b, self.from_a, self.from_z = from_b, from_a, from_z
        self.sb, self.sa, self.sz, self.rb, self.ra, self.rz = sems
        self.credit, self.owed = credit, owed

    def send(self, src, dst, to, ssem, rsem):
        pltpu.make_async_remote_copy(
            src_ref=src, dst_ref=dst, send_sem=ssem, recv_sem=rsem, device_id=to, device_id_type=MESH).start()

    def wait(self, piece, sem):
        pltpu.make_async_copy(piece, piece, sem).wait()

    def bsend(self, zi, first):
        p, k = self.p, self.k
        if first and self.owed:
            pl.semaphore_wait(self.credit.at[1], 1)
        self.send(self.grad.at[zi, p.yb, p.xb], self.from_b.at[zi, 0], p.B, self.sb.at[k], self.rb.at[k, zi])
        self.send(self.grad.at[zi, 1 - p.y, 1 - p.x], self.from_b.at[zi, 1], p.B, self.sb.at[k], self.rb.at[k, zi])

    def bwait(self, zi, first):
        p, k = self.p, self.k
        if first and self.owed:
            pl.semaphore_wait(self.credit.at[0], 1)
        self.wait(self.from_b.at[zi], self.rb.at[k, zi])
        part = self.grad[zi, p.ya, p.xa].astype(F32) + self.from_b[zi, 1].astype(F32)
        self.pass_a[zi] = part.astype(self.pass_a.dtype)
        self.send(self.pass_a.at[zi], self.from_a.at[zi], p.A, self.sa.at[k], self.ra.at[k, zi])

    def await_(self, zi):
        p, k = self.p, self.k
        self.wait(self.from_a.at[zi], self.ra.at[k, zi])
        whole = self.grad[zi, p.y, p.x].astype(F32) + self.from_b[zi, 0].astype(F32) + self.from_a[zi].astype(F32)

        @pl.when(p.z == zi)
        def _():
            self.total[...] = whole

        @pl.when(p.z != zi)
        def _():
            hop = (zi - p.z + 4) % 4 - 1
            if self.owed:
                pl.semaphore_wait(self.credit.at[2 + hop], 1)
            self.pass_z[zi] = whole.astype(self.pass_z.dtype)
            self.send(self.pass_z.at[zi], self.from_z.at[hop], p.column(zi), self.sz.at[k], self.rz.at[k, hop])

    def last(self):
        p, k = self.p, self.k
        for hop in range(3):
            self.wait(self.from_z.at[hop], self.rz.at[k, hop])
        self.total[...] += (self.from_z[0].astype(F32) + self.from_z[1].astype(F32)) + self.from_z[2].astype(F32)
        if self.credit is not None and not self.owed:
            def free(at, to):
                pl.semaphore_signal(self.credit.at[at], inc=1, device_id=to, device_id_type=MESH)

            free(0, p.A)
            free(1, p.B)
            for hop in range(3):
                free(2 + hop, p.column((p.z + 3 - hop) % 4))

    def sent(self):
        k = self.k
        self.wait(self.from_b, self.sb.at[k])
        self.wait(self.from_a, self.sa.at[k])
        self.wait(self.from_z, self.sz.at[k])


def scatter_sems(n):
    dma = pltpu.SemaphoreType.DMA
    return [dma((n,)), dma((n,)), dma((n,)), dma((n, 4)), dma((n, 4)), dma((n, 3))]


def landing(shard, dtype):
    return [pltpu.VMEM(s + shard, dtype) for s in ((4, 2), (4,), (3,))]


def passing(shard, dtype):
    return [pltpu.VMEM((4, 2, 2) + shard, dtype), pltpu.VMEM(shard, F32),
            pltpu.VMEM((4,) + shard, dtype), pltpu.VMEM((4,) + shard, dtype)]


def transposed_dot(left, right):
    return lax.dot_general(left, right, (((0,), (0,)), ((), ())), preferred_element_type=F32)


def dot_transposed(left, right):
    return lax.dot_general(left, right, (((1,), (1,)), ((), ())), preferred_element_type=F32)


def dot(left, right):
    return jnp.dot(left, right, preferred_element_type=F32)


def loop(n, body, unroll=1):
    def step(i, carry):
        body(i)
        return carry
    lax.fori_loop(0, n, step, 0, unroll=unroll)


def gelu_both(v):
    size = jnp.abs(v) * 0.7071067811865476
    t = 1.0 / (1.0 + 0.3275911 * size)
    poly = t * (0.254829592 + t * (-0.284496736 + t * (1.421413741 + t * (-1.453152027 + t * 1.061405429))))
    bell = jnp.exp(-0.5 * v * v)
    tail = 0.5 * poly * bell
    below = jnp.where(v >= 0, 1.0 - tail, tail)
    return v * below, below + v * (bell * 0.3989422804014327)


def iota(shape, dim):
    return lax.broadcasted_iota(jnp.int32, shape, dim)


ROW = 64


def rows_at(i, n=ROW):
    return pl.ds(pl.multiple_of(i * n, n), n)


def col_at(i, n):
    return pl.ds(pl.multiple_of(i * n, 128), n)


def fold8(v):
    return jnp.sum(v.reshape(v.shape[0] // 8, 8, v.shape[1]), axis=0)


def stats(v):
    centre = jnp.mean(v, axis=-1, keepdims=True)
    centred = v - centre
    spread = jnp.mean(centred * centred, axis=-1, keepdims=True)
    return centred, lax.rsqrt(spread + EPSILON)


def layers_kernel(hid, lengths, gains_in, shifts_in, qkv_in, out_in, up_in, b_up_in, down_in, b_down_in, gout, *refs):
    (hid_out, dhid, dgain, dshift, dup, dbup, ddown, dbdown,
     sp_qkv, sp_x, sp_mid, sp_act, sp_gp, sp_nf, sp_probs) = refs[:15]
    refs = refs[15:]
    W = [refs[0:4], refs[4:8]]
    vec, rows_v, bup_v, sums, sbup = refs[8:13]
    X, MID, TMP, ACT, ACTP, GP, DPP, NF, NFP, G, GPN = refs[13:24]
    idc, idq = refs[24:26]
    PROBS = W[1][UP]
    landing_sets = [refs[26:29], refs[29:32]]
    passing_sets = [refs[32:36], refs[36:40]]
    small_land, small_pass = refs[40:43], refs[43:47]
    small_from_c, small_to = refs[47:49]
    loc, swp, credit = refs[49:52]
    gsems = refs[52:60]
    ssems = refs[60:66]
    p = Place()
    p.barrier()
    c = p.c

    def local(src, dst, i):
        return pltpu.make_async_copy(src, dst, loc.at[i])

    def swap(src, dst, i):
        return pltpu.make_async_remote_copy(src_ref=src, dst_ref=dst, send_sem=swp.at[0, i], recv_sem=swp.at[1, i],
                                            device_id=p.C, device_id_type=MESH)

    def half_of(n, cc):
        return pl.ds(pl.multiple_of(cc * (n // 2), 128), n // 2)

    def stage_short():
        block = small_from_c.at[0]
        block[...] = jnp.zeros((16, 128), F32)
        b_up, b_down = b_up_in[...].astype(F32), b_down_in[...].astype(F32)
        for l in range(LAYERS):
            block[l * 8:l * 8 + 2, 0:24] = gains_in[l].astype(F32)
            block[l * 8 + 2:l * 8 + 4, 0:24] = shifts_in[l].astype(F32)
            block[l * 8 + 4:l * 8 + 5, 0:24] = b_down[l:l + 1]
            block[l * 8 + 5:l * 8 + 6, 0:96] = b_up[l:l + 1]
        vec[c, pl.ds(pl.multiple_of(p.f * 16, 16), 16)] = block[...].astype(BF)

    load_x = local(hid, G, 1)
    load_x.start()
    down_own = []
    for l in range(LAYERS):
        rows = pl.ds(pl.multiple_of(p.f * 192 + c * 96, 16), 96)
        cp = local(down_in.at[l, :, half_of(D, c)], W[l][DOWN].at[rows, half_of(D, c)], 2 + l)
        cp.start()
        down_own.append(cp)
    stage_short()
    for cc in range(2):
        @pl.when(c == cc)
        def _():
            for l in range(LAYERS):
                off = 0
                for w, n in zip((qkv_in, out_in, up_in), WIDTHS):
                    ACT[32 * l:32 * l + 24, off:off + n // 2] = w[l, :, (1 - cc) * (n // 2):(2 - cc) * (n // 2)]
                    off += n // 2
    p.met()
    down_swap = []
    for l in range(LAYERS):
        rows = pl.ds(pl.multiple_of(p.f * 192 + c * 96, 16), 96)
        cp = swap(down_in.at[l, :, half_of(D, 1 - c)], W[l][DOWN].at[rows, half_of(D, 1 - c)], l)
        down_swap.append(cp)
    pin_swap = []
    for l in range(LAYERS):
        cp = swap(ACT.at[pl.ds(l * 32, 32)], ACTP.at[pl.ds(l * 32, 32)], 2 + l)
        cp.start()
        pin_swap.append(cp)
    for cp in down_swap:
        cp.start()

    chunks = [Gather(p, vec, 16, 0, gsems, by_core=True)]
    for l in range(LAYERS):
        for j in range(4):
            chunks.append(Gather(p, W[l][j], 192 if j == DOWN else 48, 1 + l * 4 + j, gsems))

    def assemble(l):
        pin_swap[l].wait()
        off = 0
        for j, n in enumerate(WIDTHS):
            half = n // 2
            rows = pl.ds(pl.multiple_of(p.f * 48, 16), 48)
            for cc in range(2):
                @pl.when(c == cc)
                def _():
                    mine = (qkv_in, out_in, up_in)[j][l, :, cc * half:(cc + 1) * half]
                    other = ACTP[l * 32:l * 32 + 24, off:off + half]
                    pair = [mine, other] if cc == 0 else [other, mine]
                    W[l][j][rows, cc * half:(cc + 1) * half] = jnp.concatenate(pair, axis=0)
            off += half

    def ready(k):
        if k in (1, 2):
            assemble(k - 1)
        if k in (4, 8):
            down_own[k // 8].wait()
            down_swap[k // 8].wait()

    starts, total = [], jnp.int32(0)
    for j in range(16):
        starts.append(total)
        total = total + lengths[0, j]

    def numbers(places):
        ids = jnp.zeros(places.shape, jnp.int32)
        for s in starts:
            ids = ids + (places >= s).astype(jnp.int32)
        return ids

    def caption_numbers():
        def body(i):
            idc[rows_at(i)] = numbers(iota((ROW, 128), 0) + i * ROW)
        loop(SEQ // ROW, body)
        for i in range(4):
            idq[i] = numbers(iota((8, 128), 1) + 128 * i)

    def unpack_vectors():
        whole = vec[...].reshape(512, 128)

        def spread(per):
            return (iota((128, D), 1) % per == iota((128, D), 0)).astype(BF)

        for l in range(LAYERS):
            for j in range(6):
                per = 96 if j == 5 else 24
                dev = iota((32, 512), 0)
                pick = iota((32, 512), 1) == (dev % 2) * 256 + (dev // 2) * 16 + (l * 8 + j)
                wide = dot(dot(pick.astype(BF), whole).astype(BF), spread(per))
                for q in range(per // 24):
                    own = iota((32, D), 0) == (iota((32, D), 1) + q * D) // per
                    line = jnp.sum(jnp.where(own, wide, 0.0), axis=0, keepdims=True)
                    if j == 5:
                        bup_v[l, 0:1, q * D:(q + 1) * D] = line
                    else:
                        rows_v[l, j:j + 1] = line

    def ln_forward(src, l, j, dst):
        def body(i):
            centred, inverse = stats(src[rows_at(i)])
            dst[rows_at(i)] = (centred * inverse * rows_v[l, j:j + 1] + rows_v[l, 2 + j:3 + j]).astype(BF)
        loop(SEQ // ROW, body)

    def first_input():
        load_x.wait()

        def body(i):
            X[rows_at(i)] = G[rows_at(i)].astype(F32)
        loop(SEQ // ROW, body)
        local(gout, G, 4).start()

    def qkv_tile(l, t):
        cols = slice(768 * t, 768 * (t + 1))
        for h in range(3):
            cc = slice(768 * t + 256 * h, 768 * t + 256 * (h + 1))
            GP[:, cc] = dot(NF[...], W[l][QKV][:, cc]).astype(BF)

    left = None

    def lanes(v, keep_left):
        lane = iota(v.shape, 1)
        return jnp.where((lane < 64) if keep_left else (lane >= 64), v, jnp.zeros_like(v))

    def stacked(v):
        return jnp.concatenate([lanes(v, True), lanes(v, False)], axis=0)

    def unstacked(v):
        top, bottom = v[:128], v[128:]
        return jnp.where(iota(top.shape, 1) < 64, top, bottom)

    def heads_pair(j):
        return [(stacked(GP[128 * i:128 * i + 128, col_at(j, 128)] * jnp.asarray(SCALE, BF)),
                 GP[WINDOWS[i]:WINDOWS[i] + 256, col_at(j + 6, 128)],
                 GP[WINDOWS[i]:WINDOWS[i] + 256, col_at(j + 12, 128)]) for i in range(4)]

    def kept(ref, j, i):
        return ref.at[rows_at(j // 3, 256), pl.ds(pl.multiple_of((j % 3) * 1024 + 256 * i, 256), 256)]

    def attend(j):
        mixed, probs_of = [], []
        for i, (q, k, v) in enumerate(heads_pair(j)):
            w = WINDOWS[i]
            scores = dot_transposed(k, q)
            same = idc[w:w + 256] == idq[i, 0:1]
            same = jnp.concatenate([same, same], axis=1)
            scores = jnp.where(same, scores, -1e30)
            weights = jnp.exp(scores - jnp.max(scores, axis=0, keepdims=True))
            probs = (weights * (1.0 / jnp.sum(weights, axis=0, keepdims=True))).astype(BF)
            probs_of.append(probs)
            mixed.append(unstacked(transposed_dot(probs, v)).astype(BF))
        for i in range(4):
            DPP[128 * i:128 * i + 128, col_at(j, 128)] = mixed[i]
            kept(ACTP, j, i)[...] = probs_of[i]

    def out_tile(l, t):
        cols = slice(256 * t, 256 * (t + 1))
        MID[:, cols] = X[:, cols] + dot(DPP[:, 0:D], W[l][OUT][:, cols])

    def up_tiles(l, first, count):
        def body(t):
            cols = col_at(t + first, 256)
            for h in range(2):
                rr = slice(256 * h, 256 * (h + 1))
                pre = dot(NF[rr], W[l][UP][:, cols]) + bup_v[l, 0:1, cols]
                act, slope = gelu_both(pre)
                ACT[rr, cols] = act.astype(BF)
                GP[rr, cols] = slope.astype(BF)
        loop(count, body)

    def down_tile(l, t):
        cols = slice(256 * t, 256 * (t + 1))
        X[:, cols] = MID[:, cols] + dot(ACT[...], W[l][DOWN][:, cols]) + rows_v[l, 4:5, cols]

    def start(src, dst, i):
        return lambda: local(src, dst, i).start()

    def forward_pieces(l):
        todo = []
        if l == 0:
            todo += [("cap", caption_numbers), ("unpack", unpack_vectors), ("first", first_input)]
            todo += [("ln", lambda: ln_forward(X, 0, 0, NF))]
        else:
            def begin():
                local(NF, sp_nf, 10).wait()
                local(GP, sp_gp, 9).wait()
                ln_forward(X, 1, 0, NF)
                local(X, sp_x, 11).start()
            todo += [("ln", begin)]
        for t in range(3):
            todo.append(("qkv", lambda t=t: qkv_tile(l, t)))
        todo.append(("spill", start(GP.at[:, 0:3 * D], sp_qkv.at[l], 5 + l)))
        def attention(t):
            if l == 1 and t == 0:
                local(ACTP, sp_probs.at[0], 26).wait()
            loop(2, lambda j: attend(2 * t + j))
            if t == 2:
                local(ACTP, sp_probs.at[l], 26 + l).start()
        for t in range(3):
            todo.append(("att", lambda t=t: attention(t)))

        def middle(t):
            if l == 1 and t == 0:
                local(MID, sp_mid, 7).wait()
                local(ACTP, sp_probs.at[1], 27).wait()
            out_tile(l, t)
        for t in range(3):
            todo.append(("out", lambda t=t: middle(t)))
        todo.append(("ln", lambda: ln_forward(MID, l, 1, NF)))

        def widen(zi):
            if zi == PLANES[0]:
                local(GP.at[:, 0:3 * D], sp_qkv.at[l], 5 + l).wait()
                if l == 1:
                    local(ACT, sp_act, 8).wait()
                    local(gout, G, 4).wait()
                    g_swap(1).start()
                    nf_swap(1).start()
            up_tiles(l, 3 * zi, 3)
            if l == 1:
                act_swap(1, zi).start()
        for zi in PLANES:
            todo.append(("up", lambda zi=zi: widen(zi)))
        if l == 0:
            for src, dst, i in ((MID, sp_mid, 7), (ACT, sp_act, 8), (GP, sp_gp, 9), (NF, sp_nf, 10)):
                todo.append(("spill", start(src, dst, i)))
        else:
            todo += down_blocks(1)

        def narrow(t):
            if l == 1 and t == 0:
                local(X, sp_x, 11).wait()
            down_tile(l, t)
        for t in range(3):
            todo.append(("down", lambda t=t: narrow(t)))
        if l == 1:
            todo.append(("spill", start(X, hid_out, 12)))
        return todo

    def act_swap(l, zi):
        cols = slice(D * zi, D * (zi + 1))
        return swap((sp_act, ACT)[l].at[:, cols], ACTP.at[:, cols], 8 + 4 * l + zi)

    def g_swap(l):
        return swap(G.at[:, half_of(D, 1 - c)], GPN, 4 + l)

    def nf_swap(l):
        return swap(NF, NFP, 6 + l)

    def pre_swap(l):
        return swap(GP.at[:, half_of(FF, 1 - c)], DPP, 16 + l)

    scatters = []
    for k in range(4):
        scatters.append(Scatter(p, k, *passing_sets[k % 2], *landing_sets[k % 2], ssems, credit.at[k % 2], k >= 2))
    small = Scatter(p, 4, *small_pass, *small_land, ssems, None, False)

    def down_block(l, k, zi):
        for yi in range(2):
            cols = slice(768 * zi + 384 * yi, 768 * zi + 384 * (yi + 1))
            acc = transposed_dot(ACT[:, cols], G[:, half_of(D, c)]) + transposed_dot(ACTP[:, cols], GPN[...])
            scatters[k].grad[zi, yi] = acc.astype(BF).reshape(2, 192, 384)

    def up_block(l, k, zi):
        rows = slice(192 * zi, 192 * (zi + 1))
        for t in range(3):
            cols = pl.ds(pl.multiple_of(c * (FF // 2) + 512 * t, 128), 512)
            acc = transposed_dot(NF[:, rows], GP[:, cols]) + transposed_dot(NFP[:, rows], DPP[:, 512 * t:512 * (t + 1)])
            scatters[k].grad[zi, :, :, :, 512 * t:512 * (t + 1)] = acc.astype(BF).reshape(2, 2, 48, 512)

    def out_rows(k):
        return (ddown, 96, D) if k % 2 == 0 else (dup, 24, FF)

    def deliver(k):
        s, l = scatters[k], 1 - k // 2
        s.last()
        out, n, wide = out_rows(k)
        for cc in range(2):
            @pl.when(c == cc)
            def _():
                cols = pl.ds(wide // 2 * cc, wide // 2)
                swap(s.total.at[pl.ds(n * (1 - cc), n)], out.at[l, :, cols], 18 + k).start()
                local(s.total.at[pl.ds(n * cc, n)], out.at[l, :, cols], 20 + k).start()

    def delivered(k):
        s, l = scatters[k], 1 - k // 2
        out, n, wide = out_rows(k)
        cols = pl.ds(0, wide // 2)
        cp = swap(s.total.at[pl.ds(0, n)], out.at[l, :, cols], 18 + k)
        cp.wait_send()
        cp.wait_recv()
        local(s.total.at[pl.ds(0, n)], out.at[l, :, cols], 20 + k).wait()

    def d_down_bias(l):
        acc = jnp.zeros((8, D), F32)
        for i in range(SEQ // ROW):
            acc = acc + fold8(G[i * ROW:(i + 1) * ROW].astype(F32))
        sums[l, 4] = acc

    def d_pre_tiles(l, first, count):
        def body(t):
            cols = col_at(t + first, 256)
            rows = pl.ds(pl.multiple_of((t + first) * 256, 256), 256)
            acc = jnp.zeros((8, 256), F32)
            d_act = dot_transposed(G[...], W[l][DOWN][rows])
            for h in range(2):
                rr = slice(256 * h, 256 * (h + 1))
                d = (d_act[rr] * GP[rr, cols].astype(F32)).astype(BF)
                GP[rr, cols] = d
                acc = acc + fold8(d.astype(F32))
            sbup[l, :, cols] = acc
        loop(count, body)

    def d_normed_f_tile(l, t):
        TMP[:, 256 * t:256 * (t + 1)] = dot_transposed(GP[...], W[l][UP][256 * t:256 * (t + 1)])

    def ln_backward(src, grad, add, l, j, dst, low, convert=None):
        sums[l, j] = jnp.zeros((8, D), F32)
        sums[l, 2 + j] = jnp.zeros((8, D), F32)

        def body(i):
            rr = rows_at(i)
            centred, inverse = stats(src[rr].astype(F32))
            unit = centred * inverse
            d = grad[rr]
            sums[l, j] += fold8(d * unit)
            sums[l, 2 + j] += fold8(d)
            scaled = d * rows_v[l, j:j + 1]
            mean_d = jnp.mean(scaled, axis=-1, keepdims=True)
            mean_u = jnp.mean(scaled * unit, axis=-1, keepdims=True)
            result = add[rr].astype(F32) + inverse * (scaled - mean_d - unit * mean_u)
            dst[rr] = result
            if low is not None:
                low[rr, 0:D] = result.astype(BF)
        loop(SEQ // ROW, body, LN_UNROLL)

    def d_mixed_tile(l, t):
        ACT[:, 3 * D + 256 * t:3 * D + 256 * (t + 1)] = dot_transposed(ACT[:, 0:D], W[l][OUT][256 * t:256 * (t + 1)]).astype(BF)

    def attend_back(j):
        d_q, d_k, d_v = [], [], []
        d_out = [stacked(ACT[128 * i:128 * i + 128, col_at(j + 18, 128)]) for i in range(4)]
        probs_of = [kept(PROBS, j, i)[...] for i in range(4)]
        for i, (q, k, v) in enumerate(heads_pair(j)):
            probs = probs_of[i].astype(F32)
            d_v.append(dot(probs_of[i], d_out[i]))
            d_probs = dot_transposed(v, d_out[i])
            centre = jnp.sum(d_probs * probs, axis=0, keepdims=True)
            d_scores = (probs * (d_probs - centre)).astype(BF)
            d_k.append(dot(d_scores, q))
            d_q.append((unstacked(transposed_dot(d_scores, k)) * SCALE).astype(BF))

        def joined(parts):
            rows = []
            for b in range(8):
                held = [parts[i][64 * b - WINDOWS[i]:64 * b - WINDOWS[i] + 64] for i in range(4)
                        if 0 <= 64 * b - WINDOWS[i] < 256]
                rows.append(sum(held[1:], held[0]))
            return jnp.concatenate(rows, axis=0).astype(BF)

        for i in range(4):
            ACT[128 * i:128 * i + 128, col_at(j, 128)] = d_q[i]
        ACT[:, col_at(j + 6, 128)] = joined(d_k)
        ACT[:, col_at(j + 12, 128)] = joined(d_v)

    def d_normed_a_tile(l, t):
        TMP[:, 256 * t:256 * (t + 1)] = dot_transposed(ACT[:, 0:3 * D], W[l][QKV][256 * t:256 * (t + 1)])

    def pack_small(late):
        dev = iota((32, D), 0)
        number = (dev % 16) * 2 + dev // 16
        for per, group in ((24, (0, 1, 2, 3, 4)), (96, (5,))):
            chosen = [(l, j) for l in range(LAYERS) for j in group if (l == 0 and j in (0, 2)) == late]
            if not chosen:
                continue
            spread = (iota((D, 128), 0) % per == iota((D, 128), 1)).astype(F32)
            owns = [number == (iota((32, D), 1) + q * D) // per for q in range(per // 24)]
            lines = []
            for l, j in chosen:
                picked = jnp.zeros((32, D), F32)
                for q, own in enumerate(owns):
                    full = sbup[l, :, q * D:(q + 1) * D] if j == 5 else sums[l, j]
                    picked = picked + jnp.where(own, jnp.sum(full, axis=0, keepdims=True), 0.0)
                lines.append(picked)
            part = jnp.dot(jnp.concatenate(lines, axis=0), spread, precision=lax.Precision.HIGHEST, preferred_element_type=F32)
            for i, (l, j) in enumerate(chosen):
                small_to[:, :, l * 8 + j, :] = part[32 * i:32 * i + 32].reshape(2, 16, 128)

    def gradient_block(k, zi, fn):
        l = 1 - k // 2
        first = zi == PLANES[0]
        if k % 2 == 0:
            act_swap(l, zi).wait_recv()
        if first:
            for cp in ([g_swap(l)], [nf_swap(l), pre_swap(l)])[k % 2]:
                cp.wait_recv()
            if k >= 2:
                scatters[k - 2].sent()
                delivered(k - 2)
        fn(l, k, zi)
        scatters[k].bsend(zi, first)

    def down_blocks(l):
        k = 2 * (1 - l)
        return [("dbias", lambda: d_down_bias(l))] + [("ddown", lambda zi=zi: gradient_block(k, zi, down_block)) for zi in PLANES]

    def up_blocks(l):
        k = 2 * (1 - l) + 1
        return [("dup", lambda zi=zi: gradient_block(k, zi, up_block)) for zi in PLANES]

    def backward_pieces(l):
        todo = []
        if l == 0:
            def begin():
                g_swap(0).start()
                for src, dst, i in ((sp_act, ACT, 19), (sp_gp, GP, 18), (sp_nf, NF, 17), (sp_mid, MID, 24)):
                    local(src, dst, i).wait()
            todo += [("sendg", begin)] + down_blocks(0)
        todo += [("dpre", lambda t=t: d_pre_tiles(l, (1 - c) * 6 + 2 * t, 2)) for t in range(3)]

        def send_pre():
            if l == 0:
                nf_swap(0).start()
            pre_swap(l).start()
        todo.append(("sendpre", send_pre))
        todo += [("dpre", lambda t=t: d_pre_tiles(l, c * 6 + 2 * t, 2)) for t in range(3)]
        todo += [("dnf", lambda t=t: d_normed_f_tile(l, t)) for t in range(3)]
        todo += up_blocks(l)
        if l == 1:
            def send_act():
                for zi in PLANES:
                    act_swap(0, zi).start()
            todo.append(("sendact", send_act))

        def at_middle():
            for cp in [g_swap(l), nf_swap(l), pre_swap(l)] + [act_swap(l, zi) for zi in PLANES]:
                cp.wait_send()
            local(sp_qkv.at[l], GP.at[:, 0:3 * D], 13 + l).start()
            if l == 1:
                chunks[7].finish()
                local(sp_probs.at[1], PROBS.at[0:SEQ], 28).start()
                local(X, hid_out, 12).wait()
                local(sp_x, X, 15).start()
                local(sp_nf, NF, 17).start()
            else:
                local(hid, NF, 16).start()
            ln_backward(MID, TMP, G if l == 1 else X, l, 1, MID, ACT)
        todo.append(("lnb", at_middle))
        todo += [("dmix", lambda t=t: d_mixed_tile(l, t)) for t in range(3)]

        def attention_back(t):
            if t == 0:
                local(sp_qkv.at[l], GP.at[:, 0:3 * D], 13 + l).wait()
                local(sp_probs.at[l], PROBS.at[0:SEQ], 28 + (1 - l)).wait()
            loop(2, lambda i: attend_back(2 * t + i))
            if l == 1 and t == 2:
                local(sp_gp, GP, 18).start()
                local(sp_probs.at[0], PROBS.at[0:SEQ], 29).start()
        todo += [("attb", lambda t=t: attention_back(t)) for t in range(3)]
        todo += [("dna", lambda t=t: d_normed_a_tile(l, t)) for t in range(3)]
        if l == 0:
            todo.append(("prepack", lambda: pack_small(False)))

        def at_input():
            if l == 1:
                local(sp_act, ACT, 19).start()
                local(sp_x, X, 15).wait()
                ln_backward(X, TMP, MID, l, 0, X, G)
                local(sp_mid, MID, 24).start()
            else:
                local(hid, NF, 16).wait()
                ln_backward(NF, TMP, MID, l, 0, X, None)
                local(X, dhid, 25).start()
        todo.append(("lnb", at_input))
        return todo

    small_swap = swap(small_to.at[1 - c], small_from_c, 22)

    def pack():
        pack_small(True)
        small_swap.start()

    def send_small():
        small_swap.wait()
        small.grad[...] = (small_to[c] + small_from_c[...]).reshape(ZS, YS, XS, 16, 128)
        for zi in PLANES:
            small.bsend(zi, False)

    def finish_small():
        small.last()
        for l in range(LAYERS):
            dgain[l] = small.total[l * 8:l * 8 + 2, 0:24]
            dshift[l] = small.total[l * 8 + 2:l * 8 + 4, 0:24]
            dbdown[l:l + 1] = small.total[l * 8 + 4:l * 8 + 5, 0:24]
            dbup[l:l + 1] = small.total[l * 8 + 5:l * 8 + 6, 0:96]

    pieces = forward_pieces(0) + forward_pieces(1) + backward_pieces(1) + backward_pieces(0)
    pieces += [("pack", pack), ("small", send_small)]
    sums_of = scatters + [small]
    begun = set()

    def first_wait(k, zi):
        sums_of[k].bwait(zi, k not in begun)
        begun.add(k)

    def start_chunk(k, _):
        ready(k)
        chunks[k].own()

    steps = (
        start_chunk,
        lambda k, d: chunks[k].zvisit(d),
        lambda k, d: chunks[k].xvisit(d),
        lambda k, d: chunks[k].avisit(d),
        lambda k, d: chunks[k].bvisit(d),
        lambda k, d: chunks[k].cvisit(d),
        first_wait,
        lambda k, zi: sums_of[k].await_(zi),
        None,
        lambda k, _: finish_small() if k == 4 else deliver(k),
        lambda i, j: pieces[10 * i + j][1](),
    )
    for code in ORDER:
        steps[code // 1000](code // 10 % 100, code % 10)
    for k in range(len(chunks)):
        if k != 7:
            chunks[k].finish()
    small.sent()
    for k in (2, 3):
        scatters[k].sent()
        delivered(k)
    local(X, dhid, 25).wait()


ORDER = (
    0, 10, 20, 30, 2000, 40, 50, 60, 2010, 1001, 2001, 3000, 3050, 1011, 2011, 1021,
    3060, 3010, 3001, 70, 4000, 1031, 4050, 5000, 1041, 2020, 1002, 2002, 2021, 5050, 3011, 4060,
    4010, 4001, 3020, 2030, 3002, 1012, 5060, 1022, 3021, 5010, 5001, 4011, 2012, 4020, 1071, 3030,
    5011, 5020, 4002, 2022, 2031, 4021, 1032, 5002, 3012, 5021, 4030, 3022, 5030, 3031, 4012, 2032,
    4022, 1051, 5012, 2040, 5022, 4031, 5051, 3032, 1042, 1003, 2003, 5031, 2041, 3040, 1061, 5061,
    3003, 1013, 2013, 1023, 2023, 4032, 5032, 1072, 2042, 4003, 3013, 5003, 10000, 10001, 3023, 1033,
    2033, 3041, 10002, 10003, 4040, 4013, 4023, 3033, 5013, 10004, 80, 5023, 2070, 10005, 3042, 5040,
    1052, 10006, 10007, 10008, 4033, 1043, 2043, 5052, 2071, 4041, 10009, 5033, 1062, 2072, 3070, 10010,
    3043, 4042, 5041, 5062, 1073, 2073, 10011, 10012, 10013, 10014, 5042, 1081, 2080, 3071, 10015, 10016,
    3072, 10017, 10018, 4043, 4070, 2081, 10019, 10020, 10021, 10022, 3073, 1053, 5043, 10023, 10024, 5053,
    5070, 3080, 10025, 1063, 10026, 10027, 5063, 4071, 1082, 2082, 10028, 10029, 10030, 10031, 5071, 10032,
    4073, 1083, 2083, 3081, 10033, 5073, 4080, 10034, 4072, 3082, 10035, 10036, 3083, 10037, 5080, 5072,
    10038, 10039, 4081, 4082, 10040, 4083, 10041, 10042, 10043, 10044, 5081, 5082, 10045, 5083, 10046, 6003,
    10047, 10048, 10049, 6000, 10050, 10051, 10052, 10053, 6002, 10054, 10055, 10056, 10057, 6001, 10058, 7003,
    10059, 10060, 7000, 10061, 7002, 10062, 7001, 10063, 10064, 10065, 10066, 6013, 10067, 10068, 10069, 6010,
    10070, 6012, 10071, 6011, 10072, 9000, 7013, 7010, 7012, 10073, 7011, 10074, 10075, 10076, 10077, 10078,
    10079, 10080, 10081, 10082, 10083, 10084, 6023, 10085, 10086, 10087, 10088, 9010, 6020, 10089, 10090, 6022,
    10091, 10092, 10093, 6021, 10094, 7023, 10095, 7020, 10096, 10097, 7022, 10098, 10099, 6033, 10100, 10101,
    7021, 10102, 6030, 10103, 6032, 6031, 10104, 10105, 9020, 7033, 10106, 7030, 10107, 7032, 10108, 7031,
    10109, 10110, 6040, 6041, 6042, 6043, 7040, 7041, 7042, 7043, 9030, 9040,
)
PLANES_FIRST = (5, 6,)
WINDOWS = (0, 64, 192, 256)
LN_UNROLL = 1


def layers_on_slice(hidden_in, caption_lengths, norm_gain, norm_bias, qkv_weight, out_weight, up_weight, up_bias, down_weight, down_bias, grad_out):
    shape = jax.ShapeDtypeStruct
    vm, hbm, sm = [pl.BlockSpec(memory_space=s) for s in (pltpu.VMEM, pl.ANY, pltpu.SMEM)]
    outs = [
        (shape((SEQ, D), F32), hbm), (shape((SEQ, D), F32), hbm),
        (shape((2, 2, 24), F32), vm), (shape((2, 2, 24), F32), vm),
        (shape((2, 24, FF), F32), hbm), (shape((2, 96), F32), vm),
        (shape((2, 96, D), F32), hbm), (shape((2, 24), F32), vm),
        (shape((2, SEQ, 3 * D), BF), hbm), (shape((SEQ, D), F32), hbm), (shape((SEQ, D), F32), hbm),
        (shape((SEQ, FF), BF), hbm), (shape((SEQ, FF), BF), hbm), (shape((SEQ, D), BF), hbm), (shape((2, SEQ, FF), BF), hbm),
    ]
    v = pltpu.VMEM
    scratch = []
    for l in range(LAYERS):
        scratch += [v((D, 3 * D), BF), v((D, D), BF), v((D, FF), BF), v((FF, D), BF)]
    scratch += [v((2, 256, 128), BF), v((2, 8, D), F32), v((2, 1, FF), F32), v((2, 5, 8, D), F32), v((2, 8, FF), F32)]
    scratch += [v((SEQ, D), F32)] * 3
    scratch += [v((SEQ, FF), BF)] * 3
    scratch += [v((SEQ, FF // 2), BF), v((SEQ, D), BF), v((SEQ, D), BF), v((SEQ, D), BF), v((SEQ, D // 2), BF)]
    scratch += [v((SEQ, 128), jnp.int32), v((4, 8, 128), jnp.int32)]
    scratch += landing(DOWN_SHARD, BF) + landing(UP_SHARD, BF)
    scratch += passing(DOWN_SHARD, BF) + passing(UP_SHARD, BF)
    scratch += landing(SMALL_SHARD, F32) + passing(SMALL_SHARD, F32)
    scratch += [v((16, 16, 128), F32), v((2, 16, 16, 128), F32)]
    scratch += [pltpu.SemaphoreType.DMA((30,)), pltpu.SemaphoreType.DMA((2, 23)), pltpu.SemaphoreType.REGULAR((2, 5))]
    scratch += gather_sems(9) + scatter_sems(5)
    got = pl.pallas_call(
        layers_kernel,
        out_shape=[o[0] for o in outs],
        in_specs=[hbm, sm, vm, vm, vm, vm, vm, vm, hbm, vm, hbm],
        out_specs=[o[1] for o in outs],
        scratch_shapes=scratch,
        compiler_params=pltpu.CompilerParams(collective_id=0, has_side_effects=True, vmem_limit_bytes=VMEM_LIMIT),
    )(hidden_in, caption_lengths, norm_gain, norm_bias, qkv_weight, out_weight, up_weight, up_bias, down_weight,
      down_bias, grad_out)
    return tuple(got[:8])


VMEM_LIMIT = 64 * 2**20


def solution(mesh):
    in_specs = (
        P(("fsdp", "rep"), None),
        P(("fsdp", "rep"), None),
        P(None, None, ("fsdp", "rep")),
        P(None, None, ("fsdp", "rep")),
        P(None, ("fsdp", "rep"), None),
        P(None, ("fsdp", "rep"), None),
        P(None, ("fsdp", "rep"), None),
        P(None, ("fsdp", "rep")),
        P(None, ("fsdp", "rep"), None),
        P(None, ("fsdp", "rep")),
        P(("fsdp", "rep"), None),
    )
    out_specs = (
        P(("fsdp", "rep"), None),
        P(("fsdp", "rep"), None),
        P(None, None, ("fsdp", "rep")),
        P(None, None, ("fsdp", "rep")),
        P(None, ("fsdp", "rep"), None),
        P(None, ("fsdp", "rep")),
        P(None, ("fsdp", "rep"), None),
        P(None, ("fsdp", "rep")),
    )
    near = dict(mesh.shape) == {"fsdp": 16, "rep": 2}
    return jax.shard_map(
        layers_on_slice if near else per_device, mesh=mesh, in_specs=in_specs, out_specs=out_specs, check_vma=False
    )
```

```python
import jax
import jax.numpy as jnp
from jax import lax
from jax.sharding import PartitionSpec as P
from jax.experimental import pallas as pl
from jax.experimental.pallas import tpu as pltpu

D = 768
FF = 3072
HEADS = 12
SEQ = 512
LAYERS = 2


EPSILON = 1e-05
SCALE = 0.125


def layer_norm(values, gain, shift):
    centre = jnp.mean(values, axis=-1, keepdims=True)
    centred = values - centre
    spread = jnp.mean(centred * centred, axis=-1, keepdims=True)
    return centred * lax.rsqrt(spread + EPSILON) * gain + shift


def exact_gelu(values):
    return jax.nn.gelu(values, approximate=False)


def caption_ids(lengths):
    starts = jnp.cumsum(lengths, axis=-1) - lengths
    places = jnp.arange(SEQ, dtype=jnp.int32)
    passed = (places[None, :, None] >= starts[:, None, :]).astype(jnp.int32)
    return jnp.sum(passed, axis=-1) - 1


def transposed_left(left, right):
    return lax.dot_general(
        left, right, (((0,), (0,)), ((), ())), preferred_element_type=jnp.float32
    )


def transposed_right(left, right):
    return lax.dot_general(
        left, right, (((1,), (1,)), ((), ())), preferred_element_type=jnp.float32
    )


def split_heads(packed):
    width = D // HEADS
    queries = packed[:, :D].reshape(SEQ, HEADS, width)
    keys_part = packed[:, D : 2 * D].reshape(SEQ, HEADS, width)
    values_part = packed[:, 2 * D :].reshape(SEQ, HEADS, width)
    return (queries, keys_part, values_part)


def masked_scores(queries, keys_part, caption):
    scores = (
        jnp.einsum("qhd,khd->hqk", queries, keys_part, preferred_element_type=jnp.float32) * SCALE
    )
    same = caption[:, None] == caption[None, :]
    return jnp.where(same[None], scores, -1e30)


def attend_row(inputs):
    packed, caption = inputs
    queries, keys_part, values_part = split_heads(packed)
    scores = masked_scores(queries, keys_part, caption)
    highest = jnp.max(scores, axis=-1, keepdims=True)
    weights = jnp.exp(scores - highest)
    totals = jnp.sum(weights, axis=-1, keepdims=True)
    probs = (weights / totals).astype(jnp.bfloat16)
    mixed = jnp.einsum("hqk,khd->qhd", probs, values_part, preferred_element_type=jnp.float32)
    return (mixed.reshape(SEQ, D), highest + jnp.log(totals))


def attend_back(inputs):
    packed, caption, logsum, d_mixed = inputs
    queries, keys_part, values_part = split_heads(packed)
    probs = jnp.exp(masked_scores(queries, keys_part, caption) - logsum)
    d_heads = d_mixed.reshape(SEQ, HEADS, D // HEADS)
    d_values = jnp.einsum(
        "hqk,qhd->khd", probs.astype(jnp.bfloat16), d_heads, preferred_element_type=jnp.float32
    )
    d_probs = jnp.einsum("qhd,khd->hqk", d_heads, values_part, preferred_element_type=jnp.float32)
    centre = jnp.sum(d_probs * probs, axis=-1, keepdims=True)
    d_scores = (probs * (d_probs - centre)).astype(jnp.bfloat16)
    d_queries = (
        jnp.einsum("hqk,khd->qhd", d_scores, keys_part, preferred_element_type=jnp.float32) * SCALE
    )
    d_keys = (
        jnp.einsum("hqk,qhd->khd", d_scores, queries, preferred_element_type=jnp.float32) * SCALE
    )
    joined = jnp.concatenate(
        [d_queries.reshape(SEQ, D), d_keys.reshape(SEQ, D), d_values.reshape(SEQ, D)], axis=1
    )
    return joined.astype(jnp.bfloat16)


def fetch_forward(w_qkv, w_out, w_up, w_down, gains, shifts, b_up, b_down):
    return (
        lax.all_gather(w_qkv, ("fsdp", "rep"), axis=0, tiled=True),
        lax.all_gather(w_out, ("fsdp", "rep"), axis=0, tiled=True),
        lax.all_gather(w_up, ("fsdp", "rep"), axis=0, tiled=True),
        lax.all_gather(w_down, ("fsdp", "rep"), axis=0, tiled=True),
        lax.all_gather(gains, ("fsdp", "rep"), axis=1, tiled=True),
        lax.all_gather(shifts, ("fsdp", "rep"), axis=1, tiled=True),
        lax.all_gather(b_up, ("fsdp", "rep"), axis=0, tiled=True),
        lax.all_gather(b_down, ("fsdp", "rep"), axis=0, tiled=True),
    )


def fetch_backward(w_qkv, w_out, w_up, w_down, gains, shifts):
    return (
        lax.all_gather(w_qkv, ("fsdp", "rep"), axis=0, tiled=True),
        lax.all_gather(w_out, ("fsdp", "rep"), axis=0, tiled=True),
        lax.all_gather(w_up, ("fsdp", "rep"), axis=0, tiled=True),
        lax.all_gather(w_down, ("fsdp", "rep"), axis=0, tiled=True),
        lax.all_gather(gains, ("fsdp", "rep"), axis=1, tiled=True),
        lax.all_gather(shifts, ("fsdp", "rep"), axis=1, tiled=True),
    )


def owner_major(matrix, owners):
    width = matrix.shape[1] // owners
    return matrix.reshape(matrix.shape[0], owners, width).transpose(1, 0, 2).reshape(owners, -1)


def settle(d_up, d_down, d_gains, d_shifts, d_bup, d_bdown):
    owners = lax.axis_size("fsdp") * lax.axis_size("rep")
    members = [
        d_up.reshape(owners, -1),
        d_down.reshape(owners, -1),
        owner_major(d_gains, owners),
        owner_major(d_shifts, owners),
        d_bup.reshape(owners, -1),
        d_bdown.reshape(owners, -1),
    ]
    flat = jnp.concatenate(members, axis=1)
    mine = lax.psum_scatter(flat, ("fsdp", "rep"), scatter_dimension=0, tiled=True)
    mine = mine.reshape(-1)
    up_rows = D // owners
    down_rows = FF // owners
    norm_cols = D // owners
    sizes = [up_rows * FF, down_rows * D, 2 * norm_cols, 2 * norm_cols, down_rows, norm_cols]
    pieces = []
    begin = 0
    for length in sizes:
        pieces.append(mine[begin : begin + length])
        begin = begin + length
    return (
        pieces[0].reshape(up_rows, FF),
        pieces[1].reshape(down_rows, D),
        pieces[2].reshape(2, norm_cols),
        pieces[3].reshape(2, norm_cols),
        pieces[4],
        pieces[5],
    )


def per_device(
    hidden_in,
    caption_lengths,
    norm_gain,
    norm_bias,
    qkv_weight,
    out_weight,
    up_weight,
    up_bias,
    down_weight,
    down_bias,
    grad_out,
):
    row_count = caption_lengths.shape[0]
    captions = caption_ids(caption_lengths)
    hidden = hidden_in.astype(jnp.float32)
    stored = []
    for layer_number in range(LAYERS):
        fetched = fetch_forward(
            qkv_weight[layer_number],
            out_weight[layer_number],
            up_weight[layer_number],
            down_weight[layer_number],
            norm_gain[layer_number],
            norm_bias[layer_number],
            up_bias[layer_number],
            down_bias[layer_number],
        )
        w_qkv, w_out, w_up, w_down, gains, shifts, b_up, b_down = fetched
        gains_full = gains.astype(jnp.float32)
        shifts_full = shifts.astype(jnp.float32)
        normed_a = layer_norm(hidden, gains_full[0], shifts_full[0]).astype(jnp.bfloat16)
        packed = jnp.dot(normed_a, w_qkv, preferred_element_type=jnp.float32).astype(jnp.bfloat16)
        mixed, logsum = lax.map(attend_row, (packed.reshape(row_count, SEQ, 3 * D), captions))
        mixed = mixed.reshape(-1, D).astype(jnp.bfloat16)
        middle = hidden + jnp.dot(mixed, w_out, preferred_element_type=jnp.float32)
        normed_f = layer_norm(middle, gains_full[1], shifts_full[1]).astype(jnp.bfloat16)
        preact = jnp.dot(normed_f, w_up, preferred_element_type=jnp.float32) + b_up.astype(
            jnp.float32
        )
        active = exact_gelu(preact).astype(jnp.bfloat16)
        output = (
            middle
            + jnp.dot(active, w_down, preferred_element_type=jnp.float32)
            + b_down.astype(jnp.float32)
        )
        weights_kept = None
        stored.append((hidden, packed, logsum, middle, normed_f, preact, active, weights_kept))
        hidden = output
    gradient = grad_out.astype(jnp.float32)
    settled = [None] * LAYERS
    for layer_number in reversed(range(LAYERS)):
        layer_in, packed, logsum, middle, normed_f, preact, active, weights_kept = stored[
            layer_number
        ]
        fetched = fetch_backward(
            qkv_weight[layer_number],
            out_weight[layer_number],
            up_weight[layer_number],
            down_weight[layer_number],
            norm_gain[layer_number],
            norm_bias[layer_number],
        )
        w_qkv, w_out, w_up, w_down, gains, shifts = fetched
        gains_full = gains.astype(jnp.float32)
        shifts_full = shifts.astype(jnp.float32)
        grad_low = gradient.astype(jnp.bfloat16)
        d_bdown = jnp.sum(grad_low.astype(jnp.float32), axis=0)
        d_down = transposed_left(active, grad_low)
        d_active = transposed_right(grad_low, w_down)
        gelu_value, gelu_back = jax.vjp(exact_gelu, preact)
        d_preact = gelu_back(d_active)[0].astype(jnp.bfloat16)
        d_bup = jnp.sum(d_preact.astype(jnp.float32), axis=0)
        d_up = transposed_left(normed_f, d_preact)
        d_normed_f = transposed_right(d_preact, w_up)
        norm_value, norm_back = jax.vjp(layer_norm, middle, gains_full[1], shifts_full[1])
        d_middle_ln, d_gain_f, d_shift_f = norm_back(d_normed_f)
        d_middle = gradient + d_middle_ln
        d_mixed = transposed_right(d_middle.astype(jnp.bfloat16), w_out).astype(jnp.bfloat16)
        d_packed = lax.map(
            attend_back,
            (
                packed.reshape(row_count, SEQ, 3 * D),
                captions,
                logsum,
                d_mixed.reshape(row_count, SEQ, D),
            ),
        )
        d_normed_a = transposed_right(d_packed.reshape(-1, 3 * D), w_qkv)
        first_value, first_back = jax.vjp(layer_norm, layer_in, gains_full[0], shifts_full[0])
        d_input_ln, d_gain_a, d_shift_a = first_back(d_normed_a)
        gradient = d_middle + d_input_ln
        settled[layer_number] = settle(
            d_up,
            d_down,
            jnp.stack([d_gain_a, d_gain_f]),
            jnp.stack([d_shift_a, d_shift_f]),
            d_bup,
            d_bdown,
        )
    d_gains = jnp.stack([settled[number][2] for number in range(LAYERS)])
    d_shifts = jnp.stack([settled[number][3] for number in range(LAYERS)])
    d_up_all = jnp.stack([settled[number][0] for number in range(LAYERS)])
    d_bup_all = jnp.stack([settled[number][4] for number in range(LAYERS)])
    d_down_all = jnp.stack([settled[number][1] for number in range(LAYERS)])
    d_bdown_all = jnp.stack([settled[number][5] for number in range(LAYERS)])
    return (hidden, gradient, d_gains, d_shifts, d_up_all, d_bup_all, d_down_all, d_bdown_all)


MESH = pl.DeviceIdType.MESH
BF, F32 = jnp.bfloat16, jnp.float32
ZS, YS, XS = 4, 2, 2
QKV, OUT, UP, DOWN = range(4)
WIDTHS = (3 * D, D, FF)
HALF = sum(WIDTHS) // 2
PLANES = (3, 0, 2, 1)
UP_SHARD = (48, FF // 2)
DOWN_SHARD = (192, D // 2)
SMALL_SHARD = (16, 128)


class Place:
    def __init__(self):
        f = lax.axis_index("fsdp")
        c = lax.axis_index("rep")
        self.f, self.c = f, c
        self.x = f % 2
        self.y = (f // 2) % 2
        self.z = f // 4
        fx = f + 1 - 2 * self.x
        fy = f + 2 - 4 * self.y
        self.fa = fx + c * (fy - fx)
        self.fb = fy + c * (fx - fy)
        self.ya = (self.fa // 2) % 2
        self.xa = self.fa % 2
        self.yb = (self.fb // 2) % 2
        self.xb = self.fb % 2
        self.A = (self.fa, c)
        self.B = (self.fb, c)
        self.C = (f, 1 - c)
        self.UP = (f + 4, c)
        self.DN = (f - 4, c)
        self.has_up = self.z < 3
        self.has_dn = self.z > 0

    def barrier(self):
        bar = pltpu.get_barrier_semaphore()
        others = [self.A, self.B, self.C] + [self.column((self.z + hop) % 4) for hop in (1, 2, 3)]
        for d in others:
            pl.semaphore_signal(bar, inc=1, device_id=d, device_id_type=MESH)

    def met(self):
        pl.semaphore_wait(pltpu.get_barrier_semaphore(), 6)

    def column(self, zi):
        return (zi * 4 + self.f % 4, self.c)


class Gather:
    def __init__(self, place, ref, rows, k, sems, by_core=False):
        self.p, self.ref, self.rows, self.k, self.by_core = place, ref, rows, k, by_core
        self.planes_first = k in PLANES_FIRST
        (self.zs, self.as_, self.bs, self.cs, self.zr, self.ar, self.br, self.cr) = sems

    def block(self, start, rows, c=None):
        c = self.p.c if c is None else c
        if self.by_core:
            return self.ref.at[c, pl.ds(start, rows)]
        half = self.ref.shape[-1] // 2
        return self.ref.at[pl.ds(start, rows), pl.ds(pl.multiple_of(c * half, 128), half)]

    def cut(self, zi, yi, xi):
        return self.block(pl.multiple_of((zi * 4 + yi * 2 + xi) * self.rows, 16), self.rows)

    def plane(self, zi, c=None):
        return self.block(pl.multiple_of(zi * 4 * self.rows, 16), 4 * self.rows, c)

    def send(self, piece, to, ssem, rsem):
        pltpu.make_async_remote_copy(
            src_ref=piece, dst_ref=piece, send_sem=ssem, recv_sem=rsem, device_id=to, device_id_type=MESH).start()

    def wait(self, piece, sem):
        pltpu.make_async_copy(piece, piece, sem).wait()

    def unit(self, zi):
        return self.plane(zi) if self.planes_first else self.cut(zi, self.p.y, self.p.x)

    def each(self, d, fn):
        z = self.p.z
        if d == 0:
            fn(z, False, False)
            return

        @pl.when(z >= d)
        def _():
            fn(z - d, True, False)

        @pl.when(z + d <= 3)
        def _():
            fn(z + d, False, True)

    def start_z(self):
        p, k = self.p, self.k
        mine = self.unit(p.z)

        @pl.when(p.has_up)
        def _():
            self.send(mine, p.UP, self.zs.at[k, 0], self.zr.at[k, p.z])

        @pl.when(p.has_dn)
        def _():
            self.send(mine, p.DN, self.zs.at[k, 1], self.zr.at[k, p.z])

    def to_ab(self, zi):
        p, k = self.p, self.k
        piece = self.cut(zi, p.y, p.x)
        self.send(piece, p.A, self.as_.at[k], self.ar.at[k, zi])
        self.send(piece, p.B, self.bs.at[k], self.br.at[k, zi])

    def to_c(self, zi):
        self.send(self.plane(zi), self.p.C, self.cs.at[self.k], self.cr.at[self.k, zi])

    def own(self):
        if self.planes_first:
            self.to_ab(self.p.z)
        else:
            self.start_z()

    def zvisit(self, d):
        p, k = self.p, self.k

        def visit(zi, below, above):
            self.wait(self.unit(zi), self.zr.at[k, zi])
            if below and d < 3:
                @pl.when(p.has_up)
                def _():
                    self.send(self.unit(zi), p.UP, self.zs.at[k, 1 + d], self.zr.at[k, zi])
            if above and d < 3:
                @pl.when(p.has_dn)
                def _():
                    self.send(self.unit(zi), p.DN, self.zs.at[k, 3 + d], self.zr.at[k, zi])
            if self.planes_first:
                self.to_c(zi)
        self.each(d, visit)

    def xvisit(self, d):
        self.each(d, lambda zi, below, above: self.to_ab(zi))

    def avisit(self, d):
        p, k = self.p, self.k

        def visit(zi, below, above):
            piece = self.cut(zi, p.ya, p.xa)
            self.wait(piece, self.ar.at[k, zi])
            self.send(piece, p.B, self.bs.at[k], self.br.at[k, zi])
        self.each(d, visit)

    def bvisit(self, d):
        def visit(zi, below, above):
            self.wait(self.block(0, 2 * self.rows), self.br.at[self.k, zi])
            self.to_c(zi)
            if self.planes_first:
                self.start_z()
        self.each(d, visit)

    def cvisit(self, d):
        def visit(zi, below, above):
            self.wait(self.plane(zi, 1 - self.p.c), self.cr.at[self.k, zi])
        self.each(d, visit)

    def finish(self):
        p, k = self.p, self.k
        unit = self.block(0, (4 if self.planes_first else 1) * self.rows)
        shards = 1 if self.planes_first else 4

        def wait_if(cond, i):
            @pl.when(cond)
            def _():
                self.wait(unit, self.zs.at[k, i])

        wait_if(p.has_up, 0)
        wait_if(p.has_dn, 1)
        for d in (1, 2):
            wait_if((p.z >= d) & p.has_up, 1 + d)
            wait_if((p.z + d <= 3) & p.has_dn, 3 + d)
        self.wait(self.block(0, shards * self.rows), self.as_.at[k])
        self.wait(self.block(0, 2 * shards * self.rows), self.bs.at[k])
        self.wait(self.block(0, 16 * self.rows), self.cs.at[k])


def gather_sems(n):
    dma = pltpu.SemaphoreType.DMA
    return [dma((n, 6)), dma((n,)), dma((n,)), dma((n,)), dma((n, 4)), dma((n, 4)), dma((n, 4)), dma((n, 4))]


class Scatter:
    def __init__(self, place, k, grad, total, pass_a, pass_z, from_b, from_a, from_z, sems, credit, owed):
        self.p, self.k = place, k
        self.grad, self.total, self.pass_a, self.pass_z = grad, total, pass_a, pass_z
        self.from_b, self.from_a, self.from_z = from_b, from_a, from_z
        self.sb, self.sa, self.sz, self.rb, self.ra, self.rz = sems
        self.credit, self.owed = credit, owed

    def send(self, src, dst, to, ssem, rsem):
        pltpu.make_async_remote_copy(
            src_ref=src, dst_ref=dst, send_sem=ssem, recv_sem=rsem, device_id=to, device_id_type=MESH).start()

    def wait(self, piece, sem):
        pltpu.make_async_copy(piece, piece, sem).wait()

    def bsend(self, zi, first):
        p, k = self.p, self.k
        if first and self.owed:
            pl.semaphore_wait(self.credit.at[1], 1)
        self.send(self.grad.at[zi, p.yb, p.xb], self.from_b.at[zi, 0], p.B, self.sb.at[k], self.rb.at[k, zi])
        self.send(self.grad.at[zi, 1 - p.y, 1 - p.x], self.from_b.at[zi, 1], p.B, self.sb.at[k], self.rb.at[k, zi])

    def bwait(self, zi, first):
        p, k = self.p, self.k
        if first and self.owed:
            pl.semaphore_wait(self.credit.at[0], 1)
        self.wait(self.from_b.at[zi], self.rb.at[k, zi])
        part = self.grad[zi, p.ya, p.xa].astype(F32) + self.from_b[zi, 1].astype(F32)
        self.pass_a[zi] = part.astype(self.pass_a.dtype)
        self.send(self.pass_a.at[zi], self.from_a.at[zi], p.A, self.sa.at[k], self.ra.at[k, zi])

    def await_(self, zi):
        p, k = self.p, self.k
        self.wait(self.from_a.at[zi], self.ra.at[k, zi])
        whole = self.grad[zi, p.y, p.x].astype(F32) + self.from_b[zi, 0].astype(F32) + self.from_a[zi].astype(F32)

        @pl.when(p.z == zi)
        def _():
            self.total[...] = whole

        @pl.when(p.z != zi)
        def _():
            hop = (zi - p.z + 4) % 4 - 1
            if self.owed:
                pl.semaphore_wait(self.credit.at[2 + hop], 1)
            self.pass_z[zi] = whole.astype(self.pass_z.dtype)
            self.send(self.pass_z.at[zi], self.from_z.at[hop], p.column(zi), self.sz.at[k], self.rz.at[k, hop])

    def last(self):
        p, k = self.p, self.k
        for hop in range(3):
            self.wait(self.from_z.at[hop], self.rz.at[k, hop])
        self.total[...] += (self.from_z[0].astype(F32) + self.from_z[1].astype(F32)) + self.from_z[2].astype(F32)
        if self.credit is not None and not self.owed:
            def free(at, to):
                pl.semaphore_signal(self.credit.at[at], inc=1, device_id=to, device_id_type=MESH)

            free(0, p.A)
            free(1, p.B)
            for hop in range(3):
                free(2 + hop, p.column((p.z + 3 - hop) % 4))

    def sent(self):
        k = self.k
        self.wait(self.from_b, self.sb.at[k])
        self.wait(self.from_a, self.sa.at[k])
        self.wait(self.from_z, self.sz.at[k])


def scatter_sems(n):
    dma = pltpu.SemaphoreType.DMA
    return [dma((n,)), dma((n,)), dma((n,)), dma((n, 4)), dma((n, 4)), dma((n, 3))]


def landing(shard, dtype):
    return [pltpu.VMEM(s + shard, dtype) for s in ((4, 2), (4,), (3,))]


def passing(shard, dtype):
    return [pltpu.VMEM((4, 2, 2) + shard, dtype), pltpu.VMEM(shard, F32),
            pltpu.VMEM((4,) + shard, dtype), pltpu.VMEM((4,) + shard, dtype)]


def transposed_dot(left, right):
    return lax.dot_general(left, right, (((0,), (0,)), ((), ())), preferred_element_type=F32)


def dot_transposed(left, right):
    return lax.dot_general(left, right, (((1,), (1,)), ((), ())), preferred_element_type=F32)


def dot(left, right):
    return jnp.dot(left, right, preferred_element_type=F32)


def loop(n, body, unroll=1):
    def step(i, carry):
        body(i)
        return carry
    lax.fori_loop(0, n, step, 0, unroll=unroll)


def gelu_both(v):
    size = jnp.abs(v) * 0.7071067811865476
    t = 1.0 / (1.0 + 0.3275911 * size)
    poly = t * (0.254829592 + t * (-0.284496736 + t * (1.421413741 + t * (-1.453152027 + t * 1.061405429))))
    bell = jnp.exp(-0.5 * v * v)
    tail = 0.5 * poly * bell
    below = jnp.where(v >= 0, 1.0 - tail, tail)
    return v * below, below + v * (bell * 0.3989422804014327)


def iota(shape, dim):
    return lax.broadcasted_iota(jnp.int32, shape, dim)


ROW = 64


def rows_at(i, n=ROW):
    return pl.ds(pl.multiple_of(i * n, n), n)


def col_at(i, n):
    return pl.ds(pl.multiple_of(i * n, 128), n)


def fold8(v):
    return jnp.sum(v.reshape(v.shape[0] // 8, 8, v.shape[1]), axis=0)


def stats(v):
    centre = jnp.mean(v, axis=-1, keepdims=True)
    centred = v - centre
    spread = jnp.mean(centred * centred, axis=-1, keepdims=True)
    return centred, lax.rsqrt(spread + EPSILON)


def layers_kernel(hid, lengths, gains_in, shifts_in, qkv_in, out_in, up_in, b_up_in, down_in, b_down_in, gout, *refs):
    (hid_out, dhid, dgain, dshift, dup, dbup, ddown, dbdown,
     sp_qkv, sp_x, sp_mid, sp_act, sp_gp, sp_nf, sp_probs) = refs[:15]
    refs = refs[15:]
    W = [refs[0:4], refs[4:8]]
    vec, rows_v, bup_v, sums, sbup = refs[8:13]
    X, MID, TMP, ACT, ACTP, GP, DPP, NF, NFP, G, GPN = refs[13:24]
    idc, idq = refs[24:26]
    PROBS = W[1][UP]
    landing_sets = [refs[26:29], refs[29:32]]
    passing_sets = [refs[32:36], refs[36:40]]
    small_land, small_pass = refs[40:43], refs[43:47]
    small_from_c, small_to = refs[47:49]
    loc, swp, credit = refs[49:52]
    gsems = refs[52:60]
    ssems = refs[60:66]
    p = Place()
    p.barrier()
    c = p.c

    def local(src, dst, i):
        return pltpu.make_async_copy(src, dst, loc.at[i])

    def swap(src, dst, i):
        return pltpu.make_async_remote_copy(src_ref=src, dst_ref=dst, send_sem=swp.at[0, i], recv_sem=swp.at[1, i],
                                            device_id=p.C, device_id_type=MESH)

    def half_of(n, cc):
        return pl.ds(pl.multiple_of(cc * (n // 2), 128), n // 2)

    def stage_short():
        block = small_from_c.at[0]
        block[...] = jnp.zeros((16, 128), F32)
        b_up, b_down = b_up_in[...].astype(F32), b_down_in[...].astype(F32)
        for l in range(LAYERS):
            block[l * 8:l * 8 + 2, 0:24] = gains_in[l].astype(F32)
            block[l * 8 + 2:l * 8 + 4, 0:24] = shifts_in[l].astype(F32)
            block[l * 8 + 4:l * 8 + 5, 0:24] = b_down[l:l + 1]
            block[l * 8 + 5:l * 8 + 6, 0:96] = b_up[l:l + 1]
        vec[c, pl.ds(pl.multiple_of(p.f * 16, 16), 16)] = block[...].astype(BF)

    load_x = local(hid, G, 1)
    load_x.start()
    down_own = []
    for l in range(LAYERS):
        rows = pl.ds(pl.multiple_of(p.f * 192 + c * 96, 16), 96)
        cp = local(down_in.at[l, :, half_of(D, c)], W[l][DOWN].at[rows, half_of(D, c)], 2 + l)
        cp.start()
        down_own.append(cp)
    stage_short()
    for cc in range(2):
        @pl.when(c == cc)
        def _():
            for l in range(LAYERS):
                off = 0
                for w, n in zip((qkv_in, out_in, up_in), WIDTHS):
                    ACT[32 * l:32 * l + 24, off:off + n // 2] = w[l, :, (1 - cc) * (n // 2):(2 - cc) * (n // 2)]
                    off += n // 2
    p.met()
    down_swap = []
    for l in range(LAYERS):
        rows = pl.ds(pl.multiple_of(p.f * 192 + c * 96, 16), 96)
        cp = swap(down_in.at[l, :, half_of(D, 1 - c)], W[l][DOWN].at[rows, half_of(D, 1 - c)], l)
        down_swap.append(cp)
    pin_swap = []
    for l in range(LAYERS):
        cp = swap(ACT.at[pl.ds(l * 32, 32)], ACTP.at[pl.ds(l * 32, 32)], 2 + l)
        cp.start()
        pin_swap.append(cp)
    for cp in down_swap:
        cp.start()

    chunks = [Gather(p, vec, 16, 0, gsems, by_core=True)]
    for l in range(LAYERS):
        for j in range(4):
            chunks.append(Gather(p, W[l][j], 192 if j == DOWN else 48, 1 + l * 4 + j, gsems))

    def assemble(l):
        pin_swap[l].wait()
        off = 0
        for j, n in enumerate(WIDTHS):
            half = n // 2
            rows = pl.ds(pl.multiple_of(p.f * 48, 16), 48)
            for cc in range(2):
                @pl.when(c == cc)
                def _():
                    mine = (qkv_in, out_in, up_in)[j][l, :, cc * half:(cc + 1) * half]
                    other = ACTP[l * 32:l * 32 + 24, off:off + half]
                    pair = [mine, other] if cc == 0 else [other, mine]
                    W[l][j][rows, cc * half:(cc + 1) * half] = jnp.concatenate(pair, axis=0)
            off += half

    def ready(k):
        if k in (1, 2):
            assemble(k - 1)
        if k in (4, 8):
            down_own[k // 8].wait()
            down_swap[k // 8].wait()

    starts, total = [], jnp.int32(0)
    for j in range(16):
        starts.append(total)
        total = total + lengths[0, j]

    def numbers(places):
        ids = jnp.zeros(places.shape, jnp.int32)
        for s in starts:
            ids = ids + (places >= s).astype(jnp.int32)
        return ids

    def caption_numbers():
        def body(i):
            idc[rows_at(i)] = numbers(iota((ROW, 128), 0) + i * ROW)
        loop(SEQ // ROW, body)
        for i in range(4):
            idq[i] = numbers(iota((8, 128), 1) + 128 * i)

    def unpack_vectors():
        whole = vec[...].reshape(512, 128)

        def spread(per):
            return (iota((128, D), 1) % per == iota((128, D), 0)).astype(BF)

        for l in range(LAYERS):
            for j in range(6):
                per = 96 if j == 5 else 24
                dev = iota((32, 512), 0)
                pick = iota((32, 512), 1) == (dev % 2) * 256 + (dev // 2) * 16 + (l * 8 + j)
                wide = dot(dot(pick.astype(BF), whole).astype(BF), spread(per))
                for q in range(per // 24):
                    own = iota((32, D), 0) == (iota((32, D), 1) + q * D) // per
                    line = jnp.sum(jnp.where(own, wide, 0.0), axis=0, keepdims=True)
                    if j == 5:
                        bup_v[l, 0:1, q * D:(q + 1) * D] = line
                    else:
                        rows_v[l, j:j + 1] = line

    def ln_forward(src, l, j, dst):
        def body(i):
            centred, inverse = stats(src[rows_at(i)])
            dst[rows_at(i)] = (centred * inverse * rows_v[l, j:j + 1] + rows_v[l, 2 + j:3 + j]).astype(BF)
        loop(SEQ // ROW, body)

    def first_input():
        load_x.wait()

        def body(i):
            X[rows_at(i)] = G[rows_at(i)].astype(F32)
        loop(SEQ // ROW, body)
        local(gout, G, 4).start()

    def qkv_tile(l, t):
        cols = slice(768 * t, 768 * (t + 1))
        for h in range(3):
            cc = slice(768 * t + 256 * h, 768 * t + 256 * (h + 1))
            GP[:, cc] = dot(NF[...], W[l][QKV][:, cc]).astype(BF)

    left = None

    def lanes(v, keep_left):
        lane = iota(v.shape, 1)
        return jnp.where((lane < 64) if keep_left else (lane >= 64), v, jnp.zeros_like(v))

    def stacked(v):
        return jnp.concatenate([lanes(v, True), lanes(v, False)], axis=0)

    def unstacked(v):
        top, bottom = v[:128], v[128:]
        return jnp.where(iota(top.shape, 1) < 64, top, bottom)

    def heads_pair(j):
        return [(stacked(GP[128 * i:128 * i + 128, col_at(j, 128)] * jnp.asarray(SCALE, BF)),
                 GP[WINDOWS[i]:WINDOWS[i] + 256, col_at(j + 6, 128)],
                 GP[WINDOWS[i]:WINDOWS[i] + 256, col_at(j + 12, 128)]) for i in range(4)]

    def kept(ref, j, i):
        return ref.at[rows_at(j // 3, 256), pl.ds(pl.multiple_of((j % 3) * 1024 + 256 * i, 256), 256)]

    def attend(j):
        mixed, probs_of = [], []
        for i, (q, k, v) in enumerate(heads_pair(j)):
            w = WINDOWS[i]
            scores = dot_transposed(k, q)
            same = idc[w:w + 256] == idq[i, 0:1]
            same = jnp.concatenate([same, same], axis=1)
            scores = jnp.where(same, scores, -1e30)
            weights = jnp.exp(scores - jnp.max(scores, axis=0, keepdims=True))
            probs = (weights * (1.0 / jnp.sum(weights, axis=0, keepdims=True))).astype(BF)
            probs_of.append(probs)
            mixed.append(unstacked(transposed_dot(probs, v)).astype(BF))
        for i in range(4):
            DPP[128 * i:128 * i + 128, col_at(j, 128)] = mixed[i]
            kept(ACTP, j, i)[...] = probs_of[i]

    def out_tile(l, t):
        cols = slice(256 * t, 256 * (t + 1))
        MID[:, cols] = X[:, cols] + dot(DPP[:, 0:D], W[l][OUT][:, cols])

    def up_tiles(l, first, count):
        def body(t):
            cols = col_at(t + first, 256)
            for h in range(2):
                rr = slice(256 * h, 256 * (h + 1))
                pre = dot(NF[rr], W[l][UP][:, cols]) + bup_v[l, 0:1, cols]
                act, slope = gelu_both(pre)
                ACT[rr, cols] = act.astype(BF)
                GP[rr, cols] = slope.astype(BF)
        loop(count, body)

    def down_tile(l, t):
        cols = slice(256 * t, 256 * (t + 1))
        X[:, cols] = MID[:, cols] + dot(ACT[...], W[l][DOWN][:, cols]) + rows_v[l, 4:5, cols]

    def start(src, dst, i):
        return lambda: local(src, dst, i).start()

    def forward_pieces(l):
        todo = []
        if l == 0:
            todo += [("cap", caption_numbers), ("unpack", unpack_vectors), ("first", first_input)]
            todo += [("ln", lambda: ln_forward(X, 0, 0, NF))]
        else:
            def begin():
                local(NF, sp_nf, 10).wait()
                local(GP, sp_gp, 9).wait()
                ln_forward(X, 1, 0, NF)
                local(X, sp_x, 11).start()
            todo += [("ln", begin)]
        for t in range(3):
            todo.append(("qkv", lambda t=t: qkv_tile(l, t)))
        todo.append(("spill", start(GP.at[:, 0:3 * D], sp_qkv.at[l], 5 + l)))
        def attention(t):
            if l == 1 and t == 0:
                local(ACTP, sp_probs.at[0], 26).wait()
            loop(2, lambda j: attend(2 * t + j))
            if t == 2:
                local(ACTP, sp_probs.at[l], 26 + l).start()
        for t in range(3):
            todo.append(("att", lambda t=t: attention(t)))

        def middle(t):
            if l == 1 and t == 0:
                local(MID, sp_mid, 7).wait()
                local(ACTP, sp_probs.at[1], 27).wait()
            out_tile(l, t)
        for t in range(3):
            todo.append(("out", lambda t=t: middle(t)))
        todo.append(("ln", lambda: ln_forward(MID, l, 1, NF)))

        def widen(zi):
            if zi == PLANES[0]:
                local(GP.at[:, 0:3 * D], sp_qkv.at[l], 5 + l).wait()
                if l == 1:
                    local(ACT, sp_act, 8).wait()
                    local(gout, G, 4).wait()
                    g_swap(1).start()
                    nf_swap(1).start()
            up_tiles(l, 3 * zi, 3)
            if l == 1:
                act_swap(1, zi).start()
        for zi in PLANES:
            todo.append(("up", lambda zi=zi: widen(zi)))
        if l == 0:
            for src, dst, i in ((MID, sp_mid, 7), (ACT, sp_act, 8), (GP, sp_gp, 9), (NF, sp_nf, 10)):
                todo.append(("spill", start(src, dst, i)))
        else:
            todo += down_blocks(1)

        def narrow(t):
            if l == 1 and t == 0:
                local(X, sp_x, 11).wait()
            down_tile(l, t)
        for t in range(3):
            todo.append(("down", lambda t=t: narrow(t)))
        if l == 1:
            todo.append(("spill", start(X, hid_out, 12)))
        return todo

    def act_swap(l, zi):
        cols = slice(D * zi, D * (zi + 1))
        return swap((sp_act, ACT)[l].at[:, cols], ACTP.at[:, cols], 8 + 4 * l + zi)

    def g_swap(l):
        return swap(G.at[:, half_of(D, 1 - c)], GPN, 4 + l)

    def nf_swap(l):
        return swap(NF, NFP, 6 + l)

    def pre_swap(l):
        return swap(GP.at[:, half_of(FF, 1 - c)], DPP, 16 + l)

    scatters = []
    for k in range(4):
        scatters.append(Scatter(p, k, *passing_sets[k % 2], *landing_sets[k % 2], ssems, credit.at[k % 2], k >= 2))
    small = Scatter(p, 4, *small_pass, *small_land, ssems, None, False)

    def down_block(l, k, zi):
        for yi in range(2):
            cols = slice(768 * zi + 384 * yi, 768 * zi + 384 * (yi + 1))
            acc = transposed_dot(ACT[:, cols], G[:, half_of(D, c)]) + transposed_dot(ACTP[:, cols], GPN[...])
            scatters[k].grad[zi, yi] = acc.astype(BF).reshape(2, 192, 384)

    def up_block(l, k, zi):
        rows = slice(192 * zi, 192 * (zi + 1))
        for t in range(3):
            cols = pl.ds(pl.multiple_of(c * (FF // 2) + 512 * t, 128), 512)
            acc = transposed_dot(NF[:, rows], GP[:, cols]) + transposed_dot(NFP[:, rows], DPP[:, 512 * t:512 * (t + 1)])
            scatters[k].grad[zi, :, :, :, 512 * t:512 * (t + 1)] = acc.astype(BF).reshape(2, 2, 48, 512)

    def out_rows(k):
        return (ddown, 96, D) if k % 2 == 0 else (dup, 24, FF)

    def deliver(k):
        s, l = scatters[k], 1 - k // 2
        s.last()
        out, n, wide = out_rows(k)
        for cc in range(2):
            @pl.when(c == cc)
            def _():
                cols = pl.ds(wide // 2 * cc, wide // 2)
                swap(s.total.at[pl.ds(n * (1 - cc), n)], out.at[l, :, cols], 18 + k).start()
                local(s.total.at[pl.ds(n * cc, n)], out.at[l, :, cols], 20 + k).start()

    def delivered(k):
        s, l = scatters[k], 1 - k // 2
        out, n, wide = out_rows(k)
        cols = pl.ds(0, wide // 2)
        cp = swap(s.total.at[pl.ds(0, n)], out.at[l, :, cols], 18 + k)
        cp.wait_send()
        cp.wait_recv()
        local(s.total.at[pl.ds(0, n)], out.at[l, :, cols], 20 + k).wait()

    def d_down_bias(l):
        acc = jnp.zeros((8, D), F32)
        for i in range(SEQ // ROW):
            acc = acc + fold8(G[i * ROW:(i + 1) * ROW].astype(F32))
        sums[l, 4] = acc

    def d_pre_tiles(l, first, count):
        def body(t):
            cols = col_at(t + first, 256)
            rows = pl.ds(pl.multiple_of((t + first) * 256, 256), 256)
            acc = jnp.zeros((8, 256), F32)
            d_act = dot_transposed(G[...], W[l][DOWN][rows])
            for h in range(2):
                rr = slice(256 * h, 256 * (h + 1))
                d = (d_act[rr] * GP[rr, cols].astype(F32)).astype(BF)
                GP[rr, cols] = d
                acc = acc + fold8(d.astype(F32))
            sbup[l, :, cols] = acc
        loop(count, body)

    def d_normed_f_tile(l, t):
        TMP[:, 256 * t:256 * (t + 1)] = dot_transposed(GP[...], W[l][UP][256 * t:256 * (t + 1)])

    def ln_backward(src, grad, add, l, j, dst, low, convert=None):
        sums[l, j] = jnp.zeros((8, D), F32)
        sums[l, 2 + j] = jnp.zeros((8, D), F32)

        def body(i):
            rr = rows_at(i)
            centred, inverse = stats(src[rr].astype(F32))
            unit = centred * inverse
            d = grad[rr]
            sums[l, j] += fold8(d * unit)
            sums[l, 2 + j] += fold8(d)
            scaled = d * rows_v[l, j:j + 1]
            mean_d = jnp.mean(scaled, axis=-1, keepdims=True)
            mean_u = jnp.mean(scaled * unit, axis=-1, keepdims=True)
            result = add[rr].astype(F32) + inverse * (scaled - mean_d - unit * mean_u)
            dst[rr] = result
            if low is not None:
                low[rr, 0:D] = result.astype(BF)
        loop(SEQ // ROW, body, LN_UNROLL)

    def d_mixed_tile(l, t):
        ACT[:, 3 * D + 256 * t:3 * D + 256 * (t + 1)] = dot_transposed(ACT[:, 0:D], W[l][OUT][256 * t:256 * (t + 1)]).astype(BF)

    def attend_back(j):
        d_q, d_k, d_v = [], [], []
        d_out = [stacked(ACT[128 * i:128 * i + 128, col_at(j + 18, 128)]) for i in range(4)]
        probs_of = [kept(PROBS, j, i)[...] for i in range(4)]
        for i, (q, k, v) in enumerate(heads_pair(j)):
            probs = probs_of[i].astype(F32)
            d_v.append(dot(probs_of[i], d_out[i]))
            d_probs = dot_transposed(v, d_out[i])
            centre = jnp.sum(d_probs * probs, axis=0, keepdims=True)
            d_scores = (probs * (d_probs - centre)).astype(BF)
            d_k.append(dot(d_scores, q))
            d_q.append((unstacked(transposed_dot(d_scores, k)) * SCALE).astype(BF))

        def joined(parts):
            rows = []
            for b in range(8):
                held = [parts[i][64 * b - WINDOWS[i]:64 * b - WINDOWS[i] + 64] for i in range(4)
                        if 0 <= 64 * b - WINDOWS[i] < 256]
                rows.append(sum(held[1:], held[0]))
            return jnp.concatenate(rows, axis=0).astype(BF)

        for i in range(4):
            ACT[128 * i:128 * i + 128, col_at(j, 128)] = d_q[i]
        ACT[:, col_at(j + 6, 128)] = joined(d_k)
        ACT[:, col_at(j + 12, 128)] = joined(d_v)

    def d_normed_a_tile(l, t):
        TMP[:, 256 * t:256 * (t + 1)] = dot_transposed(ACT[:, 0:3 * D], W[l][QKV][256 * t:256 * (t + 1)])

    def pack_small(late):
        dev = iota((32, D), 0)
        number = (dev % 16) * 2 + dev // 16
        for per, group in ((24, (0, 1, 2, 3, 4)), (96, (5,))):
            chosen = [(l, j) for l in range(LAYERS) for j in group if (l == 0 and j in (0, 2)) == late]
            if not chosen:
                continue
            spread = (iota((D, 128), 0) % per == iota((D, 128), 1)).astype(F32)
            owns = [number == (iota((32, D), 1) + q * D) // per for q in range(per // 24)]
            lines = []
            for l, j in chosen:
                picked = jnp.zeros((32, D), F32)
                for q, own in enumerate(owns):
                    full = sbup[l, :, q * D:(q + 1) * D] if j == 5 else sums[l, j]
                    picked = picked + jnp.where(own, jnp.sum(full, axis=0, keepdims=True), 0.0)
                lines.append(picked)
            part = jnp.dot(jnp.concatenate(lines, axis=0), spread, precision=lax.Precision.HIGHEST, preferred_element_type=F32)
            for i, (l, j) in enumerate(chosen):
                small_to[:, :, l * 8 + j, :] = part[32 * i:32 * i + 32].reshape(2, 16, 128)

    def gradient_block(k, zi, fn):
        l = 1 - k // 2
        first = zi == PLANES[0]
        if k % 2 == 0:
            act_swap(l, zi).wait_recv()
        if first:
            for cp in ([g_swap(l)], [nf_swap(l), pre_swap(l)])[k % 2]:
                cp.wait_recv()
            if k >= 2:
                scatters[k - 2].sent()
                delivered(k - 2)
        fn(l, k, zi)
        scatters[k].bsend(zi, first)

    def down_blocks(l):
        k = 2 * (1 - l)
        return [("dbias", lambda: d_down_bias(l))] + [("ddown", lambda zi=zi: gradient_block(k, zi, down_block)) for zi in PLANES]

    def up_blocks(l):
        k = 2 * (1 - l) + 1
        return [("dup", lambda zi=zi: gradient_block(k, zi, up_block)) for zi in PLANES]

    def backward_pieces(l):
        todo = []
        if l == 0:
            def begin():
                g_swap(0).start()
                for src, dst, i in ((sp_act, ACT, 19), (sp_gp, GP, 18), (sp_nf, NF, 17), (sp_mid, MID, 24)):
                    local(src, dst, i).wait()
            todo += [("sendg", begin)] + down_blocks(0)
        todo += [("dpre", lambda t=t: d_pre_tiles(l, (1 - c) * 6 + 2 * t, 2)) for t in range(3)]

        def send_pre():
            if l == 0:
                nf_swap(0).start()
            pre_swap(l).start()
        todo.append(("sendpre", send_pre))
        todo += [("dpre", lambda t=t: d_pre_tiles(l, c * 6 + 2 * t, 2)) for t in range(3)]
        todo += up_blocks(l)
        todo += [("dnf", lambda t=t: d_normed_f_tile(l, t)) for t in range(3)]
        if l == 1:
            def send_act():
                for zi in PLANES:
                    act_swap(0, zi).start()
            todo.append(("sendact", send_act))

        def at_middle():
            for cp in [g_swap(l), nf_swap(l), pre_swap(l)] + [act_swap(l, zi) for zi in PLANES]:
                cp.wait_send()
            local(sp_qkv.at[l], GP.at[:, 0:3 * D], 13 + l).start()
            if l == 1:
                chunks[7].finish()
                local(sp_probs.at[1], PROBS.at[0:SEQ], 28).start()
                local(X, hid_out, 12).wait()
                local(sp_x, X, 15).start()
                local(sp_nf, NF, 17).start()
            else:
                local(hid, NF, 16).start()
            ln_backward(MID, TMP, G if l == 1 else X, l, 1, MID, ACT)
        todo.append(("lnb", at_middle))
        todo += [("dmix", lambda t=t: d_mixed_tile(l, t)) for t in range(3)]

        def attention_back(t):
            if t == 0:
                local(sp_qkv.at[l], GP.at[:, 0:3 * D], 13 + l).wait()
                local(sp_probs.at[l], PROBS.at[0:SEQ], 28 + (1 - l)).wait()
            loop(2, lambda i: attend_back(2 * t + i))
            if l == 1 and t == 2:
                local(sp_gp, GP, 18).start()
                local(sp_probs.at[0], PROBS.at[0:SEQ], 29).start()
        todo += [("attb", lambda t=t: attention_back(t)) for t in range(3)]
        todo += [("dna", lambda t=t: d_normed_a_tile(l, t)) for t in range(3)]
        if l == 0:
            todo.append(("prepack", lambda: pack_small(False)))

        def at_input():
            if l == 1:
                local(sp_act, ACT, 19).start()
                local(sp_x, X, 15).wait()
                ln_backward(X, TMP, MID, l, 0, X, G)
                local(sp_mid, MID, 24).start()
            else:
                local(hid, NF, 16).wait()
                ln_backward(NF, TMP, MID, l, 0, X, None)
                local(X, dhid, 25).start()
        todo.append(("lnb", at_input))
        return todo

    small_swap = swap(small_to.at[1 - c], small_from_c, 22)

    def pack():
        pack_small(True)
        small_swap.start()

    def send_small():
        small_swap.wait()
        small.grad[...] = (small_to[c] + small_from_c[...]).reshape(ZS, YS, XS, 16, 128)
        for zi in PLANES:
            small.bsend(zi, False)

    def finish_small():
        small.last()
        for l in range(LAYERS):
            dgain[l] = small.total[l * 8:l * 8 + 2, 0:24]
            dshift[l] = small.total[l * 8 + 2:l * 8 + 4, 0:24]
            dbdown[l:l + 1] = small.total[l * 8 + 4:l * 8 + 5, 0:24]
            dbup[l:l + 1] = small.total[l * 8 + 5:l * 8 + 6, 0:96]

    pieces = forward_pieces(0) + forward_pieces(1) + backward_pieces(1) + backward_pieces(0)
    pieces += [("pack", pack), ("small", send_small)]
    sums_of = scatters + [small]
    begun = set()

    def first_wait(k, zi):
        sums_of[k].bwait(zi, k not in begun)
        begun.add(k)

    def start_chunk(k, _):
        ready(k)
        chunks[k].own()

    steps = (
        start_chunk,
        lambda k, d: chunks[k].zvisit(d),
        lambda k, d: chunks[k].xvisit(d),
        lambda k, d: chunks[k].avisit(d),
        lambda k, d: chunks[k].bvisit(d),
        lambda k, d: chunks[k].cvisit(d),
        first_wait,
        lambda k, zi: sums_of[k].await_(zi),
        None,
        lambda k, _: finish_small() if k == 4 else deliver(k),
        lambda i, j: pieces[10 * i + j][1](),
    )
    for code in ORDER:
        steps[code // 1000](code // 10 % 100, code % 10)
    for k in range(len(chunks)):
        if k != 7:
            chunks[k].finish()
    small.sent()
    for k in (2, 3):
        scatters[k].sent()
        delivered(k)
    local(X, dhid, 25).wait()


ORDER = (
    0, 10, 20, 30, 2000, 40, 50, 60, 2010, 1001, 2001, 3000, 3050, 1011, 2011, 1021,
    3060, 3010, 3001, 70, 4000, 1031, 4050, 5000, 1041, 2020, 1002, 2002, 2021, 5050, 3011, 4060,
    4010, 4001, 3020, 2030, 3002, 1012, 5060, 1022, 3021, 5010, 5001, 4011, 2012, 4020, 1071, 3030,
    5011, 5020, 4002, 2022, 2031, 4021, 1032, 5002, 3012, 5021, 4030, 3022, 5030, 3031, 4012, 2032,
    4022, 1051, 5012, 2040, 5022, 4031, 5051, 3032, 1042, 1003, 2003, 5031, 2041, 3040, 1061, 5061,
    3003, 1013, 2013, 1023, 2023, 4032, 5032, 1072, 2042, 4003, 3013, 5003, 10000, 10001, 3023, 1033,
    2033, 3041, 10002, 10003, 4040, 4013, 4023, 3033, 5013, 10004, 80, 5023, 2070, 10005, 3042, 5040,
    1052, 10006, 10007, 10008, 4033, 1043, 2043, 5052, 2071, 4041, 10009, 5033, 1062, 2072, 3070, 10010,
    3043, 4042, 5041, 5062, 1073, 2073, 10011, 10012, 10013, 10014, 5042, 1081, 2080, 3071, 10015, 10016,
    3072, 10017, 10018, 4043, 4070, 2081, 10019, 10020, 10021, 10022, 3073, 1053, 5043, 10023, 10024, 5053,
    5070, 3080, 10025, 1063, 10026, 10027, 5063, 4071, 1082, 2082, 10028, 10029, 10030, 10031, 5071, 10032,
    4073, 1083, 2083, 3081, 10033, 5073, 4080, 10034, 4072, 3082, 10035, 10036, 3083, 10037, 5080, 5072,
    10038, 10039, 4081, 4082, 10040, 4083, 10041, 10042, 10043, 10044, 5081, 5082, 10045, 5083, 10046, 6003,
    10047, 10048, 10049, 6000, 10050, 10051, 10052, 10053, 6002, 10054, 10055, 10056, 10057, 6001, 7003, 10058,
    10059, 7000, 10060, 7002, 10061, 7001, 10062, 10063, 10064, 6013, 10065, 10066, 6010, 10067, 10068, 10069,
    10070, 6012, 10071, 7013, 6011, 9000, 7010, 10072, 7012, 7011, 10073, 10074, 10075, 10076, 10077, 10078,
    10079, 10080, 10081, 10082, 10083, 10084, 9010, 6023, 10085, 10086, 10087, 6020, 10088, 10089, 6022, 10090,
    10091, 6021, 10092, 7023, 10093, 10094, 7020, 10095, 7022, 10096, 10097, 6033, 10098, 10099, 10100, 10101,
    7021, 6030, 10102, 6032, 10103, 7033, 6031, 10104, 9020, 7030, 10105, 7032, 10106, 7031, 10107, 10108,
    10109, 10110, 6040, 6041, 6042, 6043, 7040, 7041, 7042, 7043, 9030, 9040,
)
PLANES_FIRST = (5, 6,)
WINDOWS = (0, 64, 192, 256)
LN_UNROLL = 1


def layers_on_slice(hidden_in, caption_lengths, norm_gain, norm_bias, qkv_weight, out_weight, up_weight, up_bias, down_weight, down_bias, grad_out):
    shape = jax.ShapeDtypeStruct
    vm, hbm, sm = [pl.BlockSpec(memory_space=s) for s in (pltpu.VMEM, pl.ANY, pltpu.SMEM)]
    outs = [
        (shape((SEQ, D), F32), hbm), (shape((SEQ, D), F32), hbm),
        (shape((2, 2, 24), F32), vm), (shape((2, 2, 24), F32), vm),
        (shape((2, 24, FF), F32), hbm), (shape((2, 96), F32), vm),
        (shape((2, 96, D), F32), hbm), (shape((2, 24), F32), vm),
        (shape((2, SEQ, 3 * D), BF), hbm), (shape((SEQ, D), F32), hbm), (shape((SEQ, D), F32), hbm),
        (shape((SEQ, FF), BF), hbm), (shape((SEQ, FF), BF), hbm), (shape((SEQ, D), BF), hbm), (shape((2, SEQ, FF), BF), hbm),
    ]
    v = pltpu.VMEM
    scratch = []
    for l in range(LAYERS):
        scratch += [v((D, 3 * D), BF), v((D, D), BF), v((D, FF), BF), v((FF, D), BF)]
    scratch += [v((2, 256, 128), BF), v((2, 8, D), F32), v((2, 1, FF), F32), v((2, 5, 8, D), F32), v((2, 8, FF), F32)]
    scratch += [v((SEQ, D), F32)] * 3
    scratch += [v((SEQ, FF), BF)] * 3
    scratch += [v((SEQ, FF // 2), BF), v((SEQ, D), BF), v((SEQ, D), BF), v((SEQ, D), BF), v((SEQ, D // 2), BF)]
    scratch += [v((SEQ, 128), jnp.int32), v((4, 8, 128), jnp.int32)]
    scratch += landing(DOWN_SHARD, BF) + landing(UP_SHARD, BF)
    scratch += passing(DOWN_SHARD, BF) + passing(UP_SHARD, BF)
    scratch += landing(SMALL_SHARD, F32) + passing(SMALL_SHARD, F32)
    scratch += [v((16, 16, 128), F32), v((2, 16, 16, 128), F32)]
    scratch += [pltpu.SemaphoreType.DMA((30,)), pltpu.SemaphoreType.DMA((2, 23)), pltpu.SemaphoreType.REGULAR((2, 5))]
    scratch += gather_sems(9) + scatter_sems(5)
    got = pl.pallas_call(
        layers_kernel,
        out_shape=[o[0] for o in outs],
        in_specs=[hbm, sm, vm, vm, vm, vm, vm, vm, hbm, vm, hbm],
        out_specs=[o[1] for o in outs],
        scratch_shapes=scratch,
        compiler_params=pltpu.CompilerParams(collective_id=0, has_side_effects=True, vmem_limit_bytes=VMEM_LIMIT),
    )(hidden_in, caption_lengths, norm_gain, norm_bias, qkv_weight, out_weight, up_weight, up_bias, down_weight,
      down_bias, grad_out)
    return tuple(got[:8])


VMEM_LIMIT = 64 * 2**20


def solution(mesh):
    in_specs = (
        P(("fsdp", "rep"), None),
        P(("fsdp", "rep"), None),
        P(None, None, ("fsdp", "rep")),
        P(None, None, ("fsdp", "rep")),
        P(None, ("fsdp", "rep"), None),
        P(None, ("fsdp", "rep"), None),
        P(None, ("fsdp", "rep"), None),
        P(None, ("fsdp", "rep")),
        P(None, ("fsdp", "rep"), None),
        P(None, ("fsdp", "rep")),
        P(("fsdp", "rep"), None),
    )
    out_specs = (
        P(("fsdp", "rep"), None),
        P(("fsdp", "rep"), None),
        P(None, None, ("fsdp", "rep")),
        P(None, None, ("fsdp", "rep")),
        P(None, ("fsdp", "rep"), None),
        P(None, ("fsdp", "rep")),
        P(None, ("fsdp", "rep"), None),
        P(None, ("fsdp", "rep")),
    )
    near = dict(mesh.shape) == {"fsdp": 16, "rep": 2}
    return jax.shard_map(
        layers_on_slice if near else per_device, mesh=mesh, in_specs=in_specs, out_specs=out_specs, check_vma=False
    )
```
